32 devices in a mesh: fsdp: 4 (over z), ctx: 2 (over core), tp: 4 (over y, x).
Axes of the slice: x: 2, y: 2, z: 4, core: 2. Of those that a mesh axis runs over, the one named last changes fastest.
Arguments:
- layer_input: bfloat16 [4, 2048, 1024], P('fsdp', 'ctx', 'tp'), may hold values from -6 to 6
- segment_ids: int32 [4, 2048], P('fsdp', 'ctx'), may hold values from 0 to 21, as said below
- cotangent: bfloat16 [4, 2048, 1024], P('fsdp', 'ctx', 'tp'), may hold values from -6 to 6
- norm_gain: float32 [1024], P('tp'), may hold values from 0.1 to 1.9
- ema_damping: float32 [16, 1024], P(None, 'tp'), may hold values from 0.000125 to 0.06666667
- ema_eta: float32 [16, 1024], P(None, 'tp'), may hold values from -8 to 8
- query_gain: float32 [128], replicated, may hold values from -8 to 8
- key_gain: float32 [128], replicated, may hold values from -8 to 8
- ffn_gain: float32 [1024], P('tp'), may hold values from 0.1 to 1.9
- shared_weight: bfloat16 [1024, 128], P(('fsdp', 'ctx')), may hold values from -0.1875 to 0.1875
- value_weight: bfloat16 [1024, 2048], P(('fsdp', 'ctx'), 'tp'), may hold values from -0.1875 to 0.1875
- gate_weight: bfloat16 [1024, 2048], P(('fsdp', 'ctx'), 'tp'), may hold values from -0.1875 to 0.1875
- hidden_weight: bfloat16 [1024, 1024], P('tp', ('fsdp', 'ctx')), may hold values from -0.1875 to 0.1875
- attended_weight: bfloat16 [2048, 1024], P('tp', ('fsdp', 'ctx')), may hold values from -0.5 to 0.5
- update_weight: bfloat16 [1024, 1024], P('tp', ('fsdp', 'ctx')), may hold values from -0.1875 to 0.1875
- ffn_up_weight: bfloat16 [1024, 4096], P(('fsdp', 'ctx'), 'tp'), may hold values from -0.1875 to 0.1875
- ffn_down_weight: bfloat16 [4096, 1024], P('tp', ('fsdp', 'ctx')), may hold values from -0.09375 to 0.09375
Outputs:
- layer_output: bfloat16 [4, 2048, 1024], P('fsdp', 'ctx', 'tp')
- grad_input: float32 [4, 2048, 1024], P('fsdp', 'ctx', 'tp')
- grad_norm_gain: float32 [1024], P('tp')
- grad_ema_damping: float32 [16, 1024], P(None, 'tp')
- grad_ema_eta: float32 [16, 1024], P(None, 'tp')
- grad_query_gain: float32 [128], replicated
- grad_key_gain: float32 [128], replicated
- grad_ffn_gain: float32 [1024], P('tp')
- grad_shared_weight: float32 [1024, 128], P(('fsdp', 'ctx'))
- grad_value_weight: float32 [1024, 2048], P(('fsdp', 'ctx'), 'tp')
- grad_gate_weight: float32 [1024, 2048], P(('fsdp', 'ctx'), 'tp')
- grad_hidden_weight: float32 [1024, 1024], P('tp', ('fsdp', 'ctx'))
- grad_attended_weight: float32 [2048, 1024], P('tp', ('fsdp', 'ctx'))
- grad_update_weight: float32 [1024, 1024], P('tp', ('fsdp', 'ctx'))
- grad_ffn_up_weight: float32 [1024, 4096], P(('fsdp', 'ctx'), 'tp')
- grad_ffn_down_weight: float32 [4096, 1024], P('tp', ('fsdp', 'ctx'))
The draws below stay inside these ranges and needn't reach their ends.
Inputs may be any that keep to these rules, and one draw needn't show every extreme that they name: `segment_ids`: within each sequence the ids start at 0 at its first token, never fall and rise by at most one from a token to the next. Every document has 60 to 800 tokens, except that the last one of a sequence may be cut short; the first document of every sequence has exactly min(800, 2048) tokens, and in the 0th sequence every later document has exactly 60 tokens (cut short at its end).
All inputs are finite; a program needn't handle non-finite values.
Results may differ from the reference program's by a relative error of at most 0.015.
The reference program's roundings to bfloat16 on the way count: a program that leaves them out, or rounds other values in their place, can miss the bound.
Values may be sent and summed in bfloat16 or wider, within the bound.
A program may use at most 320 MiB of HBM per device.

```python
import math
from functools import partial
import jax
import jax.numpy as jnp
from jax import lax

D = 1024
Z = 128
V = 2048
NDIM = 16
FF = 4096
LENGTH = 2048
DOC_MIN = 60
DOC_MOST = 800
SEQS = 4


def draw_segment_ids(key, part):
    doc_count = LENGTH // DOC_MIN + 2
    doc_lengths = jax.random.randint(key, (SEQS, doc_count), DOC_MIN, DOC_MOST + 1)
    doc_lengths = doc_lengths.at[0, :].set(DOC_MIN)
    doc_lengths = doc_lengths.at[:, 0].set(DOC_MOST)
    doc_ends = jnp.cumsum(doc_lengths, axis=1)
    positions = jnp.arange(LENGTH, dtype=jnp.int32)
    passed = (positions[None, :, None] >= doc_ends[:, None, :]).astype(jnp.int32)
    return jnp.sum(passed, axis=2).astype(jnp.int32)


def levels(stream_key, extent, cuts, smallest, largest):
    def one(position, parts):
        steps = jax.random.uniform(jax.random.fold_in(jax.random.fold_in(stream_key, 6), position), (parts,), jnp.float32, smallest / len(cuts), largest / len(cuts))
        return jnp.repeat(jnp.exp(steps), extent[position] // parts).reshape((-1,) + (1,) * (len(extent) - position - 1))

    factor_of = one(*cuts[0])
    for cut in cuts[1:]:
        factor_of = factor_of * one(*cut)
    return factor_of


def normal_values(own_key, extent, spread, bound, shards=(), kind=jnp.bfloat16):
    array = spread * jax.random.normal(own_key, extent, jnp.float32)
    if shards:
        array = array * levels(own_key, extent, shards, -0.22, 0.18)
    return jnp.clip(array, -bound, bound).astype(kind)


def setup_inputs(seed: int = 0) -> dict:
    splits = jax.random.split(jax.random.key(seed), 18)
    layer_input = normal_values(splits[0], (SEQS, LENGTH, D), 1.0, 6.0, ((0, 4), (1, 2), (2, 4)))
    segment_ids = draw_segment_ids(jax.random.fold_in(splits[17], 71), 0)
    cotangent = normal_values(splits[2], (SEQS, LENGTH, D), 1.0, 6.0, ((0, 4), (1, 2), (2, 4)))
    norm_gain = jnp.clip(1.0 + 0.18 * jax.random.normal(splits[3], (D,), jnp.float32), 0.1, 1.9)
    ema_damping = jnp.clip(jnp.exp(math.log(0.06666667) - 6.2791466 * jax.random.uniform(splits[4], (NDIM, D), jnp.float32) ** levels(splits[4], (NDIM, D), ((1, 4),), -0.2, 0.2)), 0.000125, 0.06666667)
    ema_eta = normal_values(splits[5], (NDIM, D), 2.0, 8.0, ((1, 4),), jnp.float32)
    query_gain = normal_values(splits[6], (Z,), 3.0, 8.0, (), jnp.float32)
    key_gain = normal_values(splits[7], (Z,), 3.0, 8.0, (), jnp.float32)
    ffn_gain = jnp.clip(1.0 + 0.18 * jax.random.normal(splits[8], (D,), jnp.float32), 0.1, 1.9)
    shared_weight = normal_values(splits[9], (D, Z), D ** -0.5, 0.1875, ((0, 8),))
    value_weight = normal_values(splits[10], (D, V), D ** -0.5, 0.1875, ((0, 8), (1, 4)))
    gate_weight = normal_values(splits[11], (D, V), D ** -0.5, 0.1875, ((0, 8), (1, 4)))
    hidden_weight = normal_values(splits[12], (D, D), D ** -0.5, 0.1875, ((0, 4), (1, 8)))
    attended_weight = normal_values(splits[13], (V, D), (V // 16) ** -0.5, 0.5, ((0, 4), (1, 8)))
    update_weight = normal_values(splits[14], (D, D), D ** -0.5, 0.1875, ((0, 4), (1, 8)))
    ffn_up_weight = normal_values(splits[15], (D, FF), D ** -0.5, 0.1875, ((0, 8), (1, 4)))
    ffn_down_weight = normal_values(splits[16], (FF, D), FF ** -0.5, 0.09375, ((0, 4), (1, 8)))
    return {"layer_input": layer_input, "segment_ids": segment_ids, "cotangent": cotangent, "norm_gain": norm_gain, "ema_damping": ema_damping, "ema_eta": ema_eta, "query_gain": query_gain, "key_gain": key_gain, "ffn_gain": ffn_gain, "shared_weight": shared_weight, "value_weight": value_weight, "gate_weight": gate_weight, "hidden_weight": hidden_weight, "attended_weight": attended_weight, "update_weight": update_weight, "ffn_up_weight": ffn_up_weight, "ffn_down_weight": ffn_down_weight}


@jax.custom_vjp
def low(v):
    return lax.optimization_barrier(v.astype(jnp.bfloat16)).astype(jnp.float32)

@jax.custom_vjp
def low_back(v):
    return v

def low_keep(v):
    return (low(v), None)

def low_pass(kept, grad):
    return (grad,)

def back_keep(v):
    return (v, None)

def back_low(kept, grad):
    return (low(grad),)
low.defvjp(low_keep, low_pass)
low_back.defvjp(back_keep, back_low)
EPSILON = 1e-06

def matmul(left_side, right_side):
    return jnp.dot(left_side, right_side, precision=lax.Precision.HIGHEST, preferred_element_type=jnp.float32)

def rms_norm(values_in, gain_vector):
    return values_in * lax.rsqrt(lax.optimization_barrier(jnp.mean(values_in * values_in, axis=-1, keepdims=True)) + EPSILON) * gain_vector

def linear_pair(first_pair, second_pair):
    return (second_pair[0] * first_pair[0], second_pair[1] + second_pair[0] * first_pair[1])

def one_sequence(tokens, segment, params):
    norm_gain, ema_damping, ema_eta, query_gain, key_gain, ffn_gain, shared_weight, value_weight, gate_weight, hidden_weight, attended_weight, update_weight, ffn_up_weight, ffn_down_weight = params
    length = tokens.shape[0]
    normed = rms_norm(tokens, norm_gain)
    same_doc = (segment[1:] == segment[:-1]).astype(jnp.float32)
    keep_flags = jnp.concatenate([jnp.zeros((1,), jnp.float32), same_doc])
    decays = keep_flags[:, None, None] * (1.0 - ema_damping)[None]
    inputs = ema_damping[None] * normed[:, None, :]
    cumulative, states = lax.associative_scan(linear_pair, (decays, inputs), axis=0)
    ema_out = lax.optimization_barrier(jnp.sum(ema_eta[None] * states, axis=1))
    ema_mixed = low(jax.nn.silu(ema_out + normed))
    normed_low = low(normed)
    shared = jax.nn.silu(low_back(matmul(ema_mixed, shared_weight)))
    queries = low(shared * query_gain)
    key_rows = low(shared * key_gain)
    values = low(jax.nn.silu(low_back(matmul(normed_low, value_weight))))
    gate_rows = jax.nn.silu(low_back(matmul(ema_mixed, gate_weight)))
    scores = matmul(queries, key_rows.T) / math.sqrt(Z)
    positions = jnp.arange(length)
    allowed = (positions[:, None] >= positions[None, :]) & (segment[:, None] == segment[None, :])
    scores = jnp.where(allowed, scores, -1e+30)
    probs_low = low(jax.nn.softmax(scores, axis=-1))
    attended = low_back(matmul(probs_low, values))
    gated_rows = low(gate_rows * attended)
    hidden_pre = low_back(matmul(ema_mixed, hidden_weight) + matmul(gated_rows, attended_weight))
    update_pre = low_back(matmul(ema_mixed, update_weight))
    update = jax.nn.sigmoid(update_pre)
    block_out = update * jax.nn.silu(hidden_pre) + (1.0 - update) * tokens
    ffn_in = low(rms_norm(block_out, ffn_gain))
    ffn_hidden = low(jax.nn.silu(low_back(matmul(ffn_in, ffn_up_weight))))
    return block_out + low_back(matmul(ffn_hidden, ffn_down_weight))

def sequence_pair(params, pair_in):
    return one_sequence(pair_in[0], pair_in[1], params)

def reference(layer_input, segment_ids, cotangent, norm_gain, ema_damping, ema_eta, query_gain, key_gain, ffn_gain, shared_weight, value_weight, gate_weight, hidden_weight, attended_weight, update_weight, ffn_up_weight, ffn_down_weight):
    floats = jax.tree.map(lambda array_in: array_in.astype(jnp.float32), (norm_gain, ema_damping, ema_eta, query_gain, key_gain, ffn_gain, shared_weight, value_weight, gate_weight, hidden_weight, attended_weight, update_weight, ffn_up_weight, ffn_down_weight))

    def run_all(tokens_all, params):
        return lax.map(jax.checkpoint(partial(sequence_pair, params)), (tokens_all, segment_ids))
    output, backward = jax.vjp(run_all, layer_input.astype(jnp.float32), floats)
    input_grad, param_grads = backward(cotangent.astype(jnp.float32))
    return (output.astype(jnp.bfloat16), input_grad, param_grads[0], param_grads[1], param_grads[2], param_grads[3], param_grads[4], param_grads[5], param_grads[6], param_grads[7], param_grads[8], param_grads[9], param_grads[10], param_grads[11], param_grads[12], param_grads[13])
```

```python
import functools
import math

import jax
import jax.numpy as jnp
from jax import lax
from jax.experimental import pallas as pl
from jax.experimental.pallas import tpu as pltpu
from jax.sharding import PartitionSpec as P

D = 1024
Z = 128
EPSILON = 1e-06
MESH = pl.DeviceIdType.MESH
F32 = jnp.float32
BF16 = jnp.bfloat16
VMEM = pl.BlockSpec(memory_space=pltpu.VMEM)
HIGH = lax.Precision.HIGHEST


def spot(f=None, c=None, t=None):
    return (
        lax.axis_index("fsdp") if f is None else f,
        lax.axis_index("ctx") if c is None else c,
        lax.axis_index("tp") if t is None else t,
    )


def greet(devices):
    barrier = pltpu.get_barrier_semaphore()
    for device in devices:
        pl.semaphore_signal(barrier, inc=1, device_id=device, device_id_type=MESH)
    pl.semaphore_wait(barrier, len(devices))


def tp_peers():
    t = lax.axis_index("tp")
    return t, t + 1 - 2 * (t % 2), (t + 2) % 4, 3 - t


def remote(src, dst, send, recv, device):
    return pltpu.make_async_remote_copy(
        src_ref=src, dst_ref=dst, send_sem=send, recv_sem=recv, device_id=device, device_id_type=MESH
    )


class Gather:
    def __init__(self, count, source, place, send, recv, base=0):
        self.count, self.half = count, count // 2
        self.source, self.place, self.send, self.recv, self.base = source, place, send, recv, base
        self.t, self.x, self.y, _ = tp_peers()

    def copy(self, src, owner, i, way, to):
        n = self.base + way * self.count + i
        return remote(src, self.place(owner, i), self.send.at[n], self.recv.at[n], spot(t=to))

    def first(self, i, way):
        return self.copy(self.source(i), self.t, i, way, self.x if way == 0 else self.y)

    def start(self):
        for k in range(self.half):
            self.first(k, 0).start()
            self.first(k + self.half, 1).start()
        for k in range(self.half):
            self.first(k + self.half, 0).start()
            self.first(k, 1).start()

    def onward(self, i):
        if i < self.half:
            return self.copy(self.place(self.x, i), self.x, i, 2, self.y)
        return self.copy(self.place(self.y, i), self.y, i, 2, self.x)

    def forward(self):
        for k in range(self.half):
            self.first(k, 0).wait_recv()
            self.onward(k).start()
            self.first(k + self.half, 1).wait_recv()
            self.onward(k + self.half).start()

    def finish(self):
        for k in range(self.half):
            self.first(k + self.half, 0).wait_recv()
            self.first(k, 1).wait_recv()
        for i in range(self.count):
            self.onward(i).wait()
            self.first(i, 0).wait_send()
            self.first(i, 1).wait_send()


def gather_kernel(arrays, chunks, *refs):
    sources, places = refs[:arrays], refs[arrays : 2 * arrays]
    send, recv = refs[2 * arrays :]
    t, x, y, d = tp_peers()
    greet([spot(t=x), spot(t=y)])
    runs = []
    for k, (src, dst) in enumerate(zip(sources, places)):
        rows, width = src.shape
        size = rows // chunks
        runs.append(
            Gather(
                chunks,
                lambda i, src=src, size=size: src.at[pl.ds(i * size, size)],
                lambda o, i, dst=dst, size=size, width=width: dst.at[
                    pl.ds(i * size, size), pl.ds(pl.multiple_of(o * width, width), width)
                ],
                send,
                recv,
                3 * chunks * k,
            )
        )
    for run in runs:
        run.start()
    for src, dst in zip(sources, places):
        width = src.shape[1]
        for o in range(4):

            @pl.when(t == o)
            def _():
                dst[:, o * width : (o + 1) * width] = src[...]

    for run in runs:
        run.forward()
    for run in runs:
        run.finish()


def tp_gather(ident, *arrays):
    chunks = 8
    n = 3 * chunks * len(arrays)
    return pl.pallas_call(
        functools.partial(gather_kernel, len(arrays), chunks),
        out_shape=[jax.ShapeDtypeStruct((a.shape[0], 4 * a.shape[1]), a.dtype) for a in arrays],
        in_specs=[VMEM] * len(arrays),
        out_specs=[VMEM] * len(arrays),
        scratch_shapes=[pltpu.SemaphoreType.DMA((n,)), pltpu.SemaphoreType.DMA((n,))],
        compiler_params=pltpu.CompilerParams(
            collective_id=ident, has_side_effects=True, vmem_limit_bytes=48 * 2**20
        ),
        name="tp_gather",
    )(*arrays)


class Scatter:
    def __init__(self, count, part, first_diag, first_own, second, send, recv, base=0):
        self.count, self.part = count, part
        self.diag, self.own, self.second = first_diag, first_own, second
        self.send, self.recv, self.base = send, recv, base
        self.t, self.x, self.y, self.d = tp_peers()

    def ways(self, i):
        return (self.x, self.y) if i % 2 == 0 else (self.y, self.x)

    def copy(self, i, kind):
        near, far = self.ways(i)
        n = self.base + kind * self.count + i
        if kind == 0:
            src, dst, to = self.part(self.d, i), self.diag(i), near
        elif kind == 1:
            src, dst, to = self.part(near, i), self.own(i), near
        else:
            src, dst, to = self.part(far, i), self.second(i), far
        return remote(src, dst, self.send.at[n], self.recv.at[n], spot(t=to))

    def start(self):
        for i in range(self.count):
            self.copy(i, 0).start()
        for i in range(self.count):
            self.copy(i, 1).start()

    def forward(self):
        for i in range(self.count):
            self.copy(i, 0).wait_recv()
            mine = self.part(self.ways(i)[1], i)
            mine[...] = (mine[...].astype(F32) + self.diag(i)[...].astype(F32)).astype(BF16)
            self.copy(i, 2).start()

    def collect(self, i):
        self.copy(i, 1).wait_recv()
        self.copy(i, 2).wait_recv()
        return self.own(i)[...].astype(F32) + self.second(i)[...].astype(F32)

    def finish(self):
        for i in range(self.count):
            for kind in range(3):
                self.copy(i, kind).wait_send()


def scatter_kernel(arrays, chunks, *refs):
    sources, outs = refs[:arrays], refs[arrays : 2 * arrays]
    part = refs[2 * arrays : 3 * arrays]
    diag, own, second, send, recv = refs[3 * arrays :]
    t, x, y, d = tp_peers()
    for k in range(arrays):
        width = outs[k].shape[1]
        for o in range(4):
            part[k][o] = sources[k][:, o * width : (o + 1) * width]
    greet([spot(t=x), spot(t=y)])
    runs = []
    for k in range(arrays):
        size = outs[k].shape[0] // chunks
        runs.append(
            Scatter(
                chunks,
                lambda o, i, k=k, size=size: part[k].at[o, pl.ds(i * size, size)],
                lambda i, k=k: diag.at[k * chunks + i],
                lambda i, k=k: own.at[k * chunks + i],
                lambda i, k=k: second.at[k * chunks + i],
                send,
                recv,
                3 * chunks * k,
            )
        )
    for run in runs:
        run.start()
    for run in runs:
        run.forward()
    for k, run in enumerate(runs):
        size = outs[k].shape[0] // chunks
        for i in range(chunks):
            outs[k][i * size : (i + 1) * size] = run.collect(i) + run.part(t, i)[...].astype(F32)
    for run in runs:
        run.finish()


def tp_scatter(ident, *arrays):
    chunks = 8
    k = len(arrays)
    n = 3 * chunks * k
    rows, width = arrays[0].shape[0], arrays[0].shape[1] // 4
    block = pltpu.VMEM((k * chunks, rows // chunks, width), BF16)
    return pl.pallas_call(
        functools.partial(scatter_kernel, k, chunks),
        out_shape=[jax.ShapeDtypeStruct((rows, width), F32) for a in arrays],
        in_specs=[VMEM] * k,
        out_specs=[VMEM] * k,
        scratch_shapes=[pltpu.VMEM((4, rows, width), BF16)] * k
        + [block, block, block, pltpu.SemaphoreType.DMA((n,)), pltpu.SemaphoreType.DMA((n,))],
        compiler_params=pltpu.CompilerParams(
            collective_id=ident, has_side_effects=True, vmem_limit_bytes=48 * 2**20
        ),
        name="tp_scatter",
    )(*arrays)


def swap_kernel(arrays, *refs):
    sources, outs = refs[:arrays], refs[arrays : 2 * arrays]
    send, recv = refs[2 * arrays :]
    other = spot(c=1 - lax.axis_index("ctx"))
    greet([other])
    copies = [
        remote(src, dst, send.at[k], recv.at[k], other)
        for k, (src, dst) in enumerate(zip(sources, outs))
    ]
    for copy in copies:
        copy.start()
    for copy in copies:
        copy.wait()


def core_swap(ident, *arrays):
    k = len(arrays)
    return pl.pallas_call(
        functools.partial(swap_kernel, k),
        out_shape=[jax.ShapeDtypeStruct(a.shape, a.dtype) for a in arrays],
        in_specs=[VMEM] * k,
        out_specs=[VMEM] * k,
        scratch_shapes=[pltpu.SemaphoreType.DMA((k,)), pltpu.SemaphoreType.DMA((k,))],
        compiler_params=pltpu.CompilerParams(
            collective_id=ident, has_side_effects=True, vmem_limit_bytes=48 * 2**20
        ),
        name="core_swap",
    )(*arrays)


def shard_at(ref, kind, index, size):
    if kind == "row":
        return ref.at[pl.ds(pl.multiple_of(index * size, size), size)]
    return ref.at[:, pl.ds(pl.multiple_of(index * size, size), size)]


def turned(kind, size):
    return kind == "col" and size % 128 != 0


def weights_kernel(kinds, sizes, count, *refs):
    k = len(kinds)
    sources, outs = refs[:k], refs[k : 2 * k]
    here, send_up, send_down, send_core, recv, recv_core = refs[2 * k :]
    z, c = lax.axis_index("fsdp"), lax.axis_index("ctx")
    other = spot(c=1 - c)
    up, down = spot(f=(z + 1) % count), spot(f=(z + count - 1) % count)
    greet([other, up, down])

    def slot(w, owner, core):
        return shard_at(outs[w], kinds[w], owner * 2 + core, sizes[w])

    def to_core(w, owner, src):
        return remote(src, slot(w, owner, c), send_core.at[w, owner], recv_core.at[w, owner], other)

    def to_up(w, owner, src):
        return remote(src, slot(w, owner, c), send_up.at[w, owner], recv.at[w, owner], up)

    def to_down(w, owner, src):
        return remote(src, slot(w, owner, c), send_down.at[w, owner], recv.at[w, owner], down)

    def keep(w):
        return pltpu.make_async_copy(sources[w], slot(w, z, c), here.at[w])

    for w in range(k):

        @pl.when(z + 1 < count)
        def _():
            to_up(w, z, sources[w]).start()

        @pl.when(z > 0)
        def _():
            to_down(w, z, sources[w]).start()

        to_core(w, z, sources[w]).start()
        keep(w).start()

    @pl.loop(1, count)
    def _(step):
        for w in range(k):
            low, high = z - step, z + step

            @pl.when(low >= 0)
            def _():
                got = slot(w, low, c)
                to_up(w, low, got).wait_recv()

                @pl.when(z + 1 < count)
                def _():
                    to_up(w, low, got).start()

                to_core(w, low, got).start()

            @pl.when(high < count)
            def _():
                got = slot(w, high, c)
                to_down(w, high, got).wait_recv()

                @pl.when(z > 0)
                def _():
                    to_down(w, high, got).start()

                to_core(w, high, got).start()

    @pl.loop(0, count)
    def _(owner):
        for w in range(k):
            got = slot(w, owner, c)
            to_core(w, owner, got).wait()

            @pl.when((owner <= z) & (z + 1 < count))
            def _():
                to_up(w, owner, got).wait_send()

            @pl.when((owner >= z) & (z > 0))
            def _():
                to_down(w, owner, got).wait_send()

    for w in range(k):
        keep(w).wait()


def weights_gather(ident, count, kinds, shards):
    turns = [turned(k, s.shape[1]) for k, s in zip(kinds, shards)]
    shards = [s.T if turn else s for turn, s in zip(turns, shards)]
    kinds = ["row" if turn else k for turn, k in zip(turns, kinds)]
    sizes = [s.shape[0] if k == "row" else s.shape[1] for k, s in zip(kinds, shards)]
    outs = []
    for kind, size, s in zip(kinds, sizes, shards):
        shape = (2 * count * size, s.shape[1]) if kind == "row" else (s.shape[0], 2 * count * size)
        outs.append(jax.ShapeDtypeStruct(shape, s.dtype))
    k = len(shards)
    dma = pltpu.SemaphoreType.DMA
    got = pl.pallas_call(
        functools.partial(weights_kernel, kinds, sizes, count),
        out_shape=outs,
        in_specs=[VMEM] * k,
        out_specs=[VMEM] * k,
        scratch_shapes=[dma((k,))] + [dma((k, count))] * 5,
        compiler_params=pltpu.CompilerParams(
            collective_id=ident, has_side_effects=True, vmem_limit_bytes=48 * 2**20
        ),
        name="weights_gather",
    )(*shards)
    return [g.T if turn else g for turn, g in zip(turns, got)]


def grads_kernel(kinds, sizes, count, *refs):
    k = len(kinds)
    sources, outs = refs[:k], refs[k : 2 * k]
    pair, line = refs[2 * k : 3 * k], refs[3 * k : 4 * k]
    send_core, recv_core, send, recv = refs[4 * k :]
    z, c = lax.axis_index("fsdp"), lax.axis_index("ctx")
    other = spot(c=1 - c)
    up, down = spot(f=(z + 1) % count), spot(f=(z + count - 1) % count)
    greet([other, up, down])

    def block(w, owner, core):
        return shard_at(sources[w], kinds[w], owner * 2 + core, sizes[w])

    def to_core(w, owner):
        return remote(
            block(w, owner, 1 - c), pair[w].at[owner], send_core.at[w, owner], recv_core.at[w, owner], other
        )

    def to_up(w, owner):
        return remote(pair[w].at[owner], line[w].at[owner], send.at[w, owner], recv.at[w, owner], up)

    def to_down(w, owner):
        at = jnp.where(owner == z - 1, count, owner)
        return remote(pair[w].at[owner], line[w].at[at], send.at[w, owner], recv.at[w, at], down)

    def arrived(w, at):
        remote(pair[w].at[0], line[w].at[at], send.at[w, 0], recv.at[w, at], up).wait_recv()

    def plus(w, owner):
        return pair[w][owner].astype(F32) + block(w, owner, c)[...].astype(F32)

    @pl.loop(0, count)
    def _(i):
        for w in range(k):
            to_core(w, count - 1 - i).start()

    @pl.loop(0, count)
    def _(i):
        for w in range(k):
            for owner, going_up in ((count - 1 - i, True), (i, False)):

                @pl.when(owner > z if going_up else owner < z)
                def _():
                    to_core(w, owner).wait_recv()
                    total = plus(w, owner)
                    pair[w][owner] = total.astype(BF16)

                    @pl.when(z > 0 if going_up else z + 1 < count)
                    def _():
                        arrived(w, owner)
                        pair[w][owner] = (total + line[w][owner].astype(F32)).astype(BF16)

                    (to_up if going_up else to_down)(w, owner).start()

    for w in range(k):
        to_core(w, z).wait_recv()
        outs[w][...] = plus(w, z)

        @pl.when(z > 0)
        def _():
            arrived(w, z)
            outs[w][...] += line[w][z].astype(F32)

        @pl.when(z + 1 < count)
        def _():
            arrived(w, count)
            outs[w][...] += line[w][count].astype(F32)

    @pl.loop(0, count)
    def _(owner):
        for w in range(k):
            to_core(w, owner).wait_send()

            @pl.when(owner > z)
            def _():
                to_up(w, owner).wait_send()

            @pl.when(owner < z)
            def _():
                to_down(w, owner).wait_send()


def grads_scatter(ident, count, kinds, grads):
    grads = [g.astype(BF16) for g in grads]
    turns = [turned(k, g.shape[1] // (2 * count)) for k, g in zip(kinds, grads)]
    grads = [g.T if turn else g for turn, g in zip(turns, grads)]
    kinds = ["row" if turn else k for turn, k in zip(turns, kinds)]
    sizes = [g.shape[0 if k == "row" else 1] // (2 * count) for k, g in zip(kinds, grads)]
    blocks = [
        (s, g.shape[1]) if k == "row" else (g.shape[0], s) for k, s, g in zip(kinds, sizes, grads)
    ]
    k = len(grads)
    dma = pltpu.SemaphoreType.DMA
    got = pl.pallas_call(
        functools.partial(grads_kernel, kinds, sizes, count),
        out_shape=[jax.ShapeDtypeStruct(b, F32) for b in blocks],
        in_specs=[VMEM] * k,
        out_specs=[VMEM] * k,
        scratch_shapes=[pltpu.VMEM((count,) + b, BF16) for b in blocks]
        + [pltpu.VMEM((count + 1,) + b, BF16) for b in blocks]
        + [dma((k, count)), dma((k, count)), dma((k, count)), dma((k, count + 1))],
        compiler_params=pltpu.CompilerParams(
            collective_id=ident, has_side_effects=True, vmem_limit_bytes=48 * 2**20
        ),
        name="grads_scatter",
    )(*grads)
    return [g.T if turn else g for turn, g in zip(turns, got)]


def row_exchange(rows, send, recv):
    t, x, y, d = tp_peers()
    return [
        remote(rows.at[t], rows.at[t], send.at[k], recv.at[k], spot(t=p))
        for k, p in enumerate((x, y, d))
    ]


def row_sums(values):
    return lax.dot_general(
        jnp.ones((8, values.shape[1]), F32),
        values,
        (((1,), (1,)), ((), ())),
        precision=HIGH,
        preferred_element_type=F32,
    )


def tree_sum(terms):
    while len(terms) > 1:
        terms = [a + b for a, b in zip(terms[::2], terms[1::2])]
    return terms[0]


def wide(row):
    return jnp.broadcast_to(row, (8, 128))


def power(base, exponent):
    result, square = None, base
    while exponent:
        if exponent & 1:
            result = square if result is None else result * square
        exponent >>= 1
        if exponent:
            square = square * square
    return result


def front_kernel(
    tok, keep, gain, damp, eta,
    normed4, mixed4, mix_pre, xn, inv_out,
    low_n, low_m, rows, ends, starts, end_out, end_in,
    send, recv, row_send, row_recv, core_send, core_recv,
):
    t, x, y, d = tp_peers()
    c = lax.axis_index("ctx")
    other = spot(c=1 - c)
    groups, count = xn.shape[0], xn.shape[1]
    step, nj = count // 8, damp.shape[0]
    end_in[...] = jnp.zeros_like(end_in)
    value = tok[...].astype(F32)
    rows[t] = row_sums(value * value)
    greet([spot(t=x), spot(t=y), spot(t=d), other])
    sums = row_exchange(rows, row_send, row_recv)
    for copy in sums:
        copy.start()
    for copy in sums:
        copy.wait()
    inv = lax.rsqrt((rows[0] + rows[1] + rows[2] + rows[3]) / D + EPSILON)
    inv_out[...] = inv
    normed = tok[...].astype(F32) * inv.T[:, 0:1] * gain[...]
    low_n[...] = normed.astype(BF16)
    for g in range(groups):
        xn[g] = normed[:, g * 128 : (g + 1) * 128]
    width = groups * 128
    chunks = 8
    size = count // chunks
    first = Gather(
        chunks,
        lambda i: low_n.at[pl.ds(i * size, size)],
        lambda o, i: normed4.at[pl.ds(i * size, size), pl.ds(pl.multiple_of(o * width, width), width)],
        send, recv, 0,
    )
    halves = [
        Gather(
            4,
            lambda i, g=g: low_m.at[pl.ds(i * 2 * size, 2 * size), pl.ds(g * 128, 128)],
            lambda o, i, g=g: mixed4.at[
                pl.ds(i * 2 * size, 2 * size), pl.ds(pl.multiple_of(o * width + g * 128, 128), 128)
            ],
            send, recv, 24 + 12 * g,
        )
        for g in range(groups)
    ]
    first.start()

    for g in range(groups):
        ln = pl.ds(g * 128, 128)
        decay = [wide(1.0 - damp[pl.ds(j, 1), ln]) for j in range(nj)]

        def scan(s, carry):
            states, chain = carry
            at = pl.ds(s, 8, stride=step)
            v, k = xn[g, at, :], keep[at, :]
            return tuple(v + (k * r) * a for r, a in zip(decay, states)), chain * k

        zero = jnp.zeros((8, 128), F32)
        states, chain = lax.fori_loop(0, step, scan, ((zero,) * nj, zero + 1.0), unroll=4)
        for j in range(nj):
            ends[0, j, :, ln] = states[j]
            ends[1, j, :, ln] = power(decay[j], step) * chain

    last = jnp.zeros((nj, width), F32)
    for q in range(8):
        last = ends[0, :, q, :] + ends[1, :, q, :] * last
    end_out[...] = last
    across = remote(end_out, end_in, core_send.at[0], core_recv.at[0], other)
    across.start()
    across.wait()
    last = jnp.where(c == 0, 0.0, end_in[...])
    for q in range(8):
        starts[:, q, :] = last
        last = ends[0, :, q, :] + ends[1, :, q, :] * last

    for g in range(groups):
        ln = pl.ds(g * 128, 128)
        decay = [wide(1.0 - damp[pl.ds(j, 1), ln]) for j in range(nj)]
        weight = [wide(damp[pl.ds(j, 1), ln] * eta[pl.ds(j, 1), ln]) for j in range(nj)]

        def scan(s, states):
            at = pl.ds(s, 8, stride=step)
            v, k = xn[g, at, :], keep[at, :]
            states = tuple(v + (k * r) * a for r, a in zip(decay, states))
            mix_pre[g, at, :] = v + tree_sum([w * a for w, a in zip(weight, states)])
            return states

        lax.fori_loop(0, step, scan, tuple(starts[j, :, ln] for j in range(nj)), unroll=4)
        pre = mix_pre[g]
        low_m[:, ln] = (pre * jax.nn.sigmoid(pre)).astype(BF16)
        halves[g].start()
    for o in range(4):

        @pl.when(t == o)
        def _():
            normed4[:, o * width : (o + 1) * width] = low_n[...]
            mixed4[:, o * width : (o + 1) * width] = low_m[...]

    first.forward()
    for run in halves:
        run.forward()
    for run in [first] + halves:
        run.finish()


def front(ident, tok, keep, gain, damp, eta):
    count, width = tok.shape
    groups, nj = width // 128, damp.shape[0]
    dma = pltpu.SemaphoreType.DMA
    lanes = jax.ShapeDtypeStruct((groups, count, 128), F32)
    full = jax.ShapeDtypeStruct((count, 4 * width), BF16)
    n = 24 + 12 * groups
    return pl.pallas_call(
        front_kernel,
        out_shape=[full, full, lanes, lanes, jax.ShapeDtypeStruct((8, count), F32)],
        in_specs=[VMEM] * 5,
        out_specs=[VMEM] * 5,
        scratch_shapes=[
            pltpu.VMEM((count, width), BF16),
            pltpu.VMEM((count, width), BF16),
            pltpu.VMEM((4, 8, count), F32),
            pltpu.VMEM((2, nj, 8, width), F32),
            pltpu.VMEM((nj, 8, width), F32),
            pltpu.VMEM((nj, width), F32),
            pltpu.VMEM((nj, width), F32),
            dma((n,)), dma((n,)), dma((3,)), dma((3,)), dma((1,)), dma((1,)),
        ],
        compiler_params=pltpu.CompilerParams(
            collective_id=ident, has_side_effects=True, vmem_limit_bytes=48 * 2**20
        ),
        name="front",
    )(tok, keep, gain[None], damp, eta)


def tail_kernel(
    mix_sum, value_sum, mix_pre, xn, tok, inv_in, keep_next, gain, damp, eta, tok_part,
    grad_in, gain_grad, eta_grad, damp_grad,
    grad_mix, back, rows, ends, starts, end_out, end_in,
    row_send, row_recv, core_send, core_recv,
):
    t, x, y, d = tp_peers()
    c = lax.axis_index("ctx")
    other = spot(c=1 - c)
    groups, count = xn.shape[0], xn.shape[1]
    step, nj, width = count // 8, damp.shape[0], damp.shape[1]
    part = 8
    zero = jnp.zeros((8, 128), F32)
    end_in[...] = jnp.zeros_like(end_in)
    for g in range(groups):
        pre = mix_pre[g]
        sig = jax.nn.sigmoid(pre)
        grad_mix[g] = mix_sum[:, g * 128 : (g + 1) * 128] * (sig * (1.0 + pre * (1.0 - sig)))
    greet([spot(t=x), spot(t=y), spot(t=d), other])

    for g in range(groups):
        ln = pl.ds(g * 128, 128)
        for j0 in range(0, nj, part):
            decay = [wide(1.0 - damp[pl.ds(j, 1), ln]) for j in range(j0, j0 + part)]

            def scan(i, carry):
                a, w, chain = carry
                at = pl.ds(step - 1 - i, 8, stride=step)
                v, k = grad_mix[g, at, :], keep_next[at, :]
                held = [k * r for r in decay]
                w = tuple(k * p + r * q for p, r, q in zip(a, held, w))
                a = tuple(v + r * p for r, p in zip(held, a))
                return a, w, chain * k

            a, w, chain = lax.fori_loop(
                0, step, scan, ((zero,) * part, (zero,) * part, zero + 1.0), unroll=4
            )
            for n in range(part):
                less = power(decay[n], step - 1)
                ends[0, j0 + n, :, ln] = a[n]
                ends[1, j0 + n, :, ln] = w[n]
                ends[2, j0 + n, :, ln] = less * decay[n] * chain
                ends[3, j0 + n, :, ln] = float(step) * less * chain

    def merge(q, a, w):
        return (
            ends[0, :, q, :] + ends[2, :, q, :] * a,
            ends[1, :, q, :] + ends[2, :, q, :] * w + ends[3, :, q, :] * a,
        )

    a = w = jnp.zeros((nj, width), F32)
    for q in range(7, -1, -1):
        a, w = merge(q, a, w)
    end_out[0] = a
    end_out[1] = w
    across = remote(end_out, end_in, core_send.at[0], core_recv.at[0], other)
    across.start()
    across.wait()
    a, w = jnp.where(c == 0, end_in[0], 0.0), jnp.where(c == 0, end_in[1], 0.0)
    for q in range(7, -1, -1):
        starts[0, :, q, :] = a
        starts[1, :, q, :] = w
        a, w = merge(q, a, w)

    for g in range(groups):
        ln = pl.ds(g * 128, 128)
        for j0 in range(0, nj, part):
            span = range(j0, j0 + part)
            decay = [wide(1.0 - damp[pl.ds(j, 1), ln]) for j in span]
            weight = [wide(damp[pl.ds(j, 1), ln] * eta[pl.ds(j, 1), ln]) for j in span]

            def scan(i, carry):
                a, w, sum_a, sum_w = carry
                at = pl.ds(step - 1 - i, 8, stride=step)
                v, k, u = grad_mix[g, at, :], keep_next[at, :], xn[g, at, :]
                held = [k * r for r in decay]
                w = tuple(k * p + r * q for p, r, q in zip(a, held, w))
                a = tuple(v + r * p for r, p in zip(held, a))
                sum_a = tuple(s + u * p for s, p in zip(sum_a, a))
                sum_w = tuple(s + u * p for s, p in zip(sum_w, w))
                base = v if j0 == 0 else back[g, at, :]
                back[g, at, :] = base + tree_sum([r * p for r, p in zip(weight, a)])
                return a, w, sum_a, sum_w

            first = (tuple(starts[0, j, :, ln] for j in span), tuple(starts[1, j, :, ln] for j in span))
            _, _, sum_a, sum_w = lax.fori_loop(
                0, step, scan, first + ((zero,) * part, (zero,) * part), unroll=4
            )
            for n, j in enumerate(span):
                at = pl.ds(j, 1)
                all_a = jnp.sum(sum_a[n], axis=0, keepdims=True)
                all_w = jnp.sum(sum_w[n], axis=0, keepdims=True)
                rate = damp[at, ln]
                eta_grad[at, ln] = rate * all_a
                damp_grad[at, ln] = eta[at, ln] * (all_a - rate * all_w)

    inv = inv_in[...].T[:, 0:1]
    value = tok[...].astype(F32)
    back_all = jnp.concatenate([back[g] for g in range(groups)], axis=1)
    grad_normed = value_sum[...] + back_all
    gain_grad[...] = jnp.sum(grad_normed * value * inv, axis=0, keepdims=True)
    scaled = grad_normed * gain[...]
    rows[t] = row_sums(scaled * value)
    sums = row_exchange(rows, row_send, row_recv)
    for copy in sums:
        copy.start()
    grad_in[...] = tok_part[...] + inv * scaled
    for copy in sums:
        copy.wait()
    factor = inv_in[...]
    factor = factor * factor * factor * (rows[0] + rows[1] + rows[2] + rows[3]) / D
    grad_in[...] -= value * factor.T[:, 0:1]


def tail(ident, mix_sum, value_sum, mix_pre, xn, tok, inv_in, keep_next, gain, damp, eta, tok_part):
    count, width = tok.shape
    groups, nj = width // 128, damp.shape[0]
    dma = pltpu.SemaphoreType.DMA
    small = jax.ShapeDtypeStruct((nj, width), F32)
    return pl.pallas_call(
        tail_kernel,
        out_shape=[
            jax.ShapeDtypeStruct((count, width), F32),
            jax.ShapeDtypeStruct((1, width), F32),
            small,
            small,
        ],
        in_specs=[VMEM] * 11,
        out_specs=[VMEM] * 4,
        scratch_shapes=[
            pltpu.VMEM((groups, count, 128), F32),
            pltpu.VMEM((groups, count, 128), F32),
            pltpu.VMEM((4, 8, count), F32),
            pltpu.VMEM((4, nj, 8, width), F32),
            pltpu.VMEM((2, nj, 8, width), F32),
            pltpu.VMEM((2, nj, width), F32),
            pltpu.VMEM((2, nj, width), F32),
            dma((3,)), dma((3,)), dma((1,)), dma((1,)),
        ],
        compiler_params=pltpu.CompilerParams(
            collective_id=ident, has_side_effects=True, vmem_limit_bytes=48 * 2**20
        ),
        name="tail",
    )(mix_sum, value_sum, mix_pre, xn, tok, inv_in, keep_next, gain[None], damp, eta, tok_part)


def multiply(left_side, right_side):
    return jnp.dot(left_side, right_side, preferred_element_type=F32)


def multiply_left(left_side, right_side):
    return lax.dot_general(
        left_side, right_side, (((0,), (0,)), ((), ())), preferred_element_type=F32
    )


def multiply_right(left_side, right_side):
    return lax.dot_general(
        left_side, right_side, (((1,), (1,)), ((), ())), preferred_element_type=F32
    )


def silu_grad(pre_act):
    sigmoid_pre = jax.nn.sigmoid(pre_act)
    return sigmoid_pre * (1.0 + pre_act * (1.0 - sigmoid_pre))


KINDS = ("row", "row", "row", "col", "col", "col", "row", "col")


def on_device(
    line_count,
    layer_input, segment_ids, cotangent, norm_gain, ema_damping, ema_eta, query_gain, key_gain,
    ffn_gain, *weights,
):
    tok = layer_input[0]
    tokens = tok.astype(F32)
    segment = segment_ids[0]
    row_count, local_dim = tok.shape
    core = lax.axis_index("ctx")
    offset = core * row_count
    all_ids = lax.all_gather(segment, "ctx", axis=0, tiled=True)
    key_count = all_ids.shape[0]
    same = jnp.concatenate(
        [jnp.zeros((1,), F32), (all_ids[1:] == all_ids[:-1]).astype(F32), jnp.zeros((1,), F32)]
    )
    keep = lax.dynamic_slice_in_dim(same, offset, row_count, 0)
    keep_next = lax.dynamic_slice_in_dim(same, offset + 1, row_count, 0)
    keep_wide = jnp.broadcast_to(keep[:, None], (row_count, 128))
    next_wide = jnp.broadcast_to(keep_next[:, None], (row_count, 128))

    (
        full_shared, full_value, full_gate, full_hidden, full_attended, full_update, full_up, full_down,
    ) = weights_gather(1, line_count, KINDS, weights)
    normed_full, mixed_full, mix_pre, xn, inv_in = front(2, tok, keep_wide, norm_gain, ema_damping, ema_eta)
    mixed_low = lax.dynamic_slice_in_dim(mixed_full, lax.axis_index("tp") * local_dim, local_dim, 1)

    shared_pre = multiply(mixed_full, full_shared)
    shared = jax.nn.silu(shared_pre)
    queries = (shared * query_gain[None]).astype(BF16)
    key_rows = (shared * key_gain[None]).astype(BF16)
    value_pre = multiply(normed_full, full_value)
    values = jax.nn.silu(value_pre).astype(BF16)
    gate_pre = multiply(mixed_full, full_gate)
    gate_rows = jax.nn.silu(gate_pre)
    other_keys, other_values = core_swap(3, key_rows, values)

    def both(own, other):
        return jnp.where(core == 0, jnp.concatenate([own, other]), jnp.concatenate([other, own]))

    all_keys, all_values = both(key_rows, other_keys), both(values, other_values)
    block_size = math.gcd(row_count, 512)
    block_count = row_count // block_size
    key_position = jnp.arange(key_count)

    def block_scores(block_index):
        first_row = block_index * block_size
        query_block = lax.dynamic_slice_in_dim(queries, first_row, block_size, 0)
        ids_block = lax.dynamic_slice_in_dim(segment, first_row, block_size, 0)
        query_position = offset + first_row + jnp.arange(block_size)
        raw_scores = multiply_right(query_block, all_keys) / math.sqrt(Z)
        allowed = (query_position[:, None] >= key_position[None, :]) & (
            ids_block[:, None] == all_ids[None, :]
        )
        return (jnp.where(allowed, raw_scores, -1e30), query_block)

    def attend_block(block_index):
        scores, query_block = block_scores(block_index)
        row_peak = jnp.max(scores, axis=1, keepdims=True)
        exponent = jnp.exp(scores - row_peak)
        row_total = jnp.sum(exponent, axis=1, keepdims=True)
        probabilities = (exponent / row_total).astype(BF16)
        return (multiply(probabilities, all_values), (row_peak + jnp.log(row_total))[:, 0])

    attended_blocks, log_blocks = lax.map(attend_block, jnp.arange(block_count))
    attended = attended_blocks.reshape(row_count, -1)
    log_totals = log_blocks.reshape(row_count)
    gated_rows = (gate_rows * attended).astype(BF16)
    hidden_part = multiply(mixed_low, full_hidden) + multiply(gated_rows, full_attended)
    update_part = multiply(mixed_low, full_update)
    hidden_pre, update_pre = tp_scatter(4, hidden_part.astype(BF16), update_part.astype(BF16))
    update = jax.nn.sigmoid(update_pre)
    hidden_act = jax.nn.silu(hidden_pre)
    block_out = update * hidden_act + (1.0 - update) * tokens
    squares = lax.psum(jnp.sum(block_out * block_out, axis=1), "tp")
    inverse_mid = lax.rsqrt(squares / D + EPSILON)
    ffn_normed = block_out * inverse_mid[:, None] * ffn_gain[None]
    ffn_full, grad_full = tp_gather(5, ffn_normed.astype(BF16), cotangent[0])
    up_pre = multiply(ffn_full, full_up)
    up_rows = jax.nn.silu(up_pre).astype(BF16)
    ffn_part = multiply(up_rows, full_down)
    grad_down = multiply_left(up_rows, grad_full)
    grad_up_pre = (multiply_right(grad_full, full_down) * silu_grad(up_pre)).astype(BF16)
    grad_up = multiply_left(ffn_full, grad_up_pre)
    grad_ffn_part = multiply_right(grad_up_pre, full_up)
    ffn_out, grad_ffn_normed = tp_scatter(6, ffn_part.astype(BF16), grad_ffn_part.astype(BF16))
    result = (block_out + ffn_out).astype(BF16)
    grad_out = cotangent[0].astype(F32)
    scaled = grad_ffn_normed * ffn_gain[None]
    inner_sums = lax.psum(jnp.sum(scaled * block_out, axis=1), "tp")
    grad_mid = (
        inverse_mid[:, None] * scaled
        - block_out * (inverse_mid * inverse_mid * inverse_mid * inner_sums / D)[:, None]
    )
    grad_ffn_gain = jnp.sum(grad_ffn_normed * block_out * inverse_mid[:, None], axis=0)
    grad_block = grad_out + grad_mid
    grad_update_pre = (grad_block * (hidden_act - tokens) * update * (1.0 - update)).astype(BF16)
    grad_hidden_pre = (grad_block * update * silu_grad(hidden_pre)).astype(BF16)
    grad_tokens = grad_block * (1.0 - update)
    grad_hidden_full, grad_update_full = tp_gather(7, grad_hidden_pre, grad_update_pre)
    grad_hidden_weight = multiply_left(mixed_low, grad_hidden_full)
    grad_update_weight = multiply_left(mixed_low, grad_update_full)
    grad_attended_weight = multiply_left(gated_rows, grad_hidden_full)
    grad_gated = multiply_right(grad_hidden_full, full_attended)
    grad_mixed_local = multiply_right(grad_hidden_full, full_hidden) + multiply_right(
        grad_update_full, full_update
    )
    grad_attended = (grad_gated * gate_rows).astype(BF16)
    grad_gate_pre = (grad_gated * attended * silu_grad(gate_pre)).astype(BF16)

    def backward_block(running, block_index):
        key_sums, value_sums = running
        scores, query_block = block_scores(block_index)
        first_row = block_index * block_size
        exact = jnp.exp(
            scores - lax.dynamic_slice_in_dim(log_totals, first_row, block_size, 0)[:, None]
        )
        grad_block_out = lax.dynamic_slice_in_dim(grad_attended, first_row, block_size, 0)
        value_sums = value_sums + multiply_left(exact.astype(BF16), grad_block_out)
        grad_probs = multiply_right(grad_block_out, all_values)
        row_inner = jnp.sum(exact * grad_probs, axis=1, keepdims=True)
        grad_scores = exact * (grad_probs - row_inner) / math.sqrt(Z)
        scores_high = grad_scores.astype(BF16)
        scores_rest = (grad_scores - scores_high.astype(F32)).astype(BF16)
        grad_query_block = multiply(scores_high, all_keys) + multiply(scores_rest, all_keys)
        key_sums = (
            key_sums
            + multiply_left(scores_high, query_block)
            + multiply_left(scores_rest, query_block)
        )
        return ((key_sums, value_sums), grad_query_block)

    (key_sums, value_sums), query_blocks = lax.scan(
        backward_block,
        (
            jnp.zeros((key_count, key_rows.shape[1]), F32),
            jnp.zeros((key_count, values.shape[1]), F32),
        ),
        jnp.arange(block_count),
    )
    grad_queries = query_blocks.reshape(row_count, -1)

    def half(sums, which):
        return lax.dynamic_slice_in_dim(sums, which * row_count, row_count, 0)

    far_keys, far_values = core_swap(8, half(key_sums, 1 - core), half(value_sums, 1 - core))
    key_grads = half(key_sums, core) + far_keys
    value_grads = half(value_sums, core) + far_values
    grad_queries, key_grads = lax.psum((grad_queries, key_grads), "tp")
    grad_value_pre = (value_grads * silu_grad(value_pre)).astype(BF16)
    grad_shared = grad_queries * query_gain[None] + key_grads * key_gain[None]
    grad_query_gain = jnp.sum(shared * grad_queries, axis=0)
    grad_key_gain = jnp.sum(shared * key_grads, axis=0)
    grad_shared_pre = (grad_shared * silu_grad(shared_pre)).astype(BF16)
    grad_shared_weight = multiply_left(mixed_full, grad_shared_pre)
    grad_value_weight = multiply_left(normed_full, grad_value_pre)
    grad_gate_weight = multiply_left(mixed_full, grad_gate_pre)
    own_shared = lax.dynamic_slice_in_dim(
        full_shared, lax.axis_index("tp") * local_dim, local_dim, 0
    )
    grad_mixed_local = grad_mixed_local + multiply_right(grad_shared_pre, own_shared)
    back_value, back_gate = tp_scatter(
        9,
        multiply_right(grad_value_pre, full_value).astype(BF16),
        multiply_right(grad_gate_pre, full_gate).astype(BF16),
    )
    grad_in, grad_norm_gain, grad_eta, grad_damping = tail(
        10, grad_mixed_local + back_gate, back_value, mix_pre, xn, tok, inv_in, next_wide,
        norm_gain, ema_damping, ema_eta, grad_tokens,
    )
    small_sums = lax.psum(
        (grad_norm_gain[0], grad_damping, grad_eta, grad_query_gain, grad_key_gain, grad_ffn_gain),
        ("fsdp", "ctx"),
    )
    weight_sums = grads_scatter(
        11, line_count, KINDS,
        (
            grad_shared_weight, grad_value_weight, grad_gate_weight, grad_hidden_weight,
            grad_attended_weight, grad_update_weight, grad_up, grad_down,
        ),
    )
    return (result[None], grad_in[None], *small_sums, *weight_sums)


def solution(mesh):
    token = P("fsdp", "ctx", "tp")
    row, col = P(("fsdp", "ctx"), "tp"), P("tp", ("fsdp", "ctx"))
    shared = P(("fsdp", "ctx"), None)
    weights = (shared, row, row, col, col, col, row, col)
    small = P(None, "tp")
    return jax.shard_map(
        functools.partial(on_device, mesh.shape["fsdp"]),
        mesh=mesh,
        in_specs=(token, P("fsdp", "ctx"), token, P("tp"), small, small, P(), P(), P("tp")) + weights,
        out_specs=(token, token, P("tp"), small, small, P(), P(), P("tp")) + weights,
        check_vma=False,
    )
```

```python
import functools
import inspect
import math
import types

import jax
import jax.numpy as jnp
from jax import lax
from jax.experimental import pallas as pl
from jax.experimental.pallas import tpu as pltpu
from jax.sharding import PartitionSpec as P

D = 1024
Z = 128
EPSILON = 1e-06
MESH = pl.DeviceIdType.MESH
F32 = jnp.float32
BF16 = jnp.bfloat16
VMEM = pl.BlockSpec(memory_space=pltpu.VMEM)
ANY = pl.BlockSpec(memory_space=pl.ANY)
HIGH = lax.Precision.HIGHEST


def named(signature):
    return list(inspect.signature(signature).parameters)


def spot(f=None, c=None, t=None):
    return (
        lax.axis_index("fsdp") if f is None else f,
        lax.axis_index("ctx") if c is None else c,
        lax.axis_index("tp") if t is None else t,
    )


def greet(devices):
    barrier = pltpu.get_barrier_semaphore()
    for device in devices:
        pl.semaphore_signal(barrier, inc=1, device_id=device, device_id_type=MESH)
    pl.semaphore_wait(barrier, len(devices))


def tp_peers():
    t = lax.axis_index("tp")
    return t, t + 1 - 2 * (t % 2), (t + 2) % 4, 3 - t


def remote(src, dst, send, recv, device):
    return pltpu.make_async_remote_copy(
        src_ref=src, dst_ref=dst, send_sem=send, recv_sem=recv, device_id=device, device_id_type=MESH
    )


class Gather:
    def __init__(self, count, source, place, send, recv, base=0):
        self.count, self.half = count, count // 2
        self.source, self.place, self.send, self.recv, self.base = source, place, send, recv, base
        self.t, self.x, self.y, _ = tp_peers()

    def copy(self, src, owner, i, way, to):
        n = self.base + way * self.count + i
        return remote(src, self.place(owner, i), self.send.at[n], self.recv.at[n], spot(t=to))

    def first(self, i, way):
        return self.copy(self.source(i), self.t, i, way, self.x if way == 0 else self.y)

    def start(self):
        for k in range(self.half):
            self.first(k, 0).start()
            self.first(k + self.half, 1).start()
        for k in range(self.half):
            self.first(k + self.half, 0).start()
            self.first(k, 1).start()

    def onward(self, i):
        if i < self.half:
            return self.copy(self.place(self.x, i), self.x, i, 2, self.y)
        return self.copy(self.place(self.y, i), self.y, i, 2, self.x)

    def forward(self):
        for k in range(self.half):
            self.first(k, 0).wait_recv()
            self.onward(k).start()
            self.first(k + self.half, 1).wait_recv()
            self.onward(k + self.half).start()

    def finish(self):
        for k in range(self.half):
            self.first(k + self.half, 0).wait_recv()
            self.first(k, 1).wait_recv()
        for i in range(self.count):
            self.onward(i).wait()
            self.first(i, 0).wait_send()
            self.first(i, 1).wait_send()


class Scatter:
    def __init__(self, count, part, first_diag, first_own, second, send, recv, base=0):
        self.count, self.part = count, part
        self.diag, self.own, self.second = first_diag, first_own, second
        self.send, self.recv, self.base = send, recv, base
        self.t, self.x, self.y, self.d = tp_peers()

    def ways(self, i):
        return (self.x, self.y) if i % 2 == 0 else (self.y, self.x)

    def copy(self, i, kind):
        near, far = self.ways(i)
        n = self.base + kind * self.count + i
        if kind == 0:
            src, dst, to = self.part(self.d, i), self.diag(i), near
        elif kind == 1:
            src, dst, to = self.part(near, i), self.own(i), near
        else:
            src, dst, to = self.part(far, i), self.second(i), far
        return remote(src, dst, self.send.at[n], self.recv.at[n], spot(t=to))

    def start(self):
        for i in range(self.count):
            self.copy(i, 0).start()
        for i in range(self.count):
            self.copy(i, 1).start()

    def forward(self):
        for i in range(self.count):
            self.copy(i, 0).wait_recv()
            mine = self.part(self.ways(i)[1], i)
            mine[...] = (mine[...].astype(F32) + self.diag(i)[...].astype(F32)).astype(BF16)
            self.copy(i, 2).start()

    def collect(self, i):
        self.copy(i, 1).wait_recv()
        self.copy(i, 2).wait_recv()
        return self.own(i)[...].astype(F32) + self.second(i)[...].astype(F32)

    def finish(self):
        for i in range(self.count):
            for kind in range(3):
                self.copy(i, kind).wait_send()


def shard_at(ref, kind, index, size):
    if kind == "row":
        return ref.at[pl.ds(pl.multiple_of(index * size, size), size)]
    return ref.at[:, pl.ds(pl.multiple_of(index * size, size), size)]


def turned(kind, size):
    return kind == "col" and size % 128 != 0


def row_exchange(rows, send, recv):
    t, x, y, d = tp_peers()
    return [
        remote(rows.at[t], rows.at[t], send.at[k], recv.at[k], spot(t=p))
        for k, p in enumerate((x, y, d))
    ]


class Named:
    def __init__(self, names, refs):
        for name, ref in zip(names, refs, strict=True):
            setattr(self, name, ref)


class Transfer:
    def __init__(self, copy):
        self.copy, self.waited = copy, False

    def start(self):
        self.copy.start()

    def wait(self):
        if not self.waited:
            self.waited = True
            self.copy.wait()


def need(*transfers):
    for transfer in transfers:
        transfer.wait()


def dot(left, right):
    return jnp.dot(left, right, preferred_element_type=F32)


def dot_t(left, right):
    return lax.dot_general(left, right, (((1,), (1,)), ((), ())), preferred_element_type=F32)


def t_dot(left, right):
    return lax.dot_general(left, right, (((0,), (0,)), ((), ())), preferred_element_type=F32)


def sigmoid(v):
    return 1.0 / (1.0 + jnp.exp(-v))


def d_silu(v, s):
    return s * (1.0 + v * (1.0 - s))


def as_rows(column):
    return jnp.broadcast_to(column, (column.shape[0], 128)).T[0:8]


def as_column(rows):
    return rows.T[:, 0:1]


def at_block(i, size):
    return pl.ds(i * size if isinstance(i, int) else pl.multiple_of(i * size, size), size)


def wide(row):
    return jnp.broadcast_to(row, (8, 128))


def tree_sum(terms):
    while len(terms) > 1:
        terms = [a + b for a, b in zip(terms[::2], terms[1::2])]
    return terms[0]


def power(base, exponent):
    result, square = None, base
    while exponent:
        if exponent & 1:
            result = square if result is None else result * square
        exponent >>= 1
        if exponent:
            square = square * square
    return result


def row_sums(values):
    return lax.dot_general(
        jnp.ones((8, values.shape[1]), F32), values, (((1,), (1,)), ((), ())),
        precision=HIGH, preferred_element_type=F32,
    )


class Line:
    def __init__(self, kinds, sizes, count, sources, places, sems):
        self.kinds, self.sizes, self.count = kinds, sizes, count
        self.sources, self.places = sources, places
        self.here, self.send_up, self.send_down, self.send_core, self.recv, self.recv_core = sems
        self.z, self.c = lax.axis_index("fsdp"), lax.axis_index("ctx")
        self.other = spot(c=1 - self.c)
        self.up = spot(f=(self.z + 1) % count)
        self.down = spot(f=(self.z + count - 1) % count)
        self.next = {}

    def slot(self, w, owner, core):
        return shard_at(self.places[w], self.kinds[w], owner * 2 + core, self.sizes[w])

    def to_core(self, w, owner, src):
        return remote(
            src, self.slot(w, owner, self.c), self.send_core.at[w, owner], self.recv_core.at[w, owner], self.other
        )

    def to_up(self, w, owner, src):
        return remote(src, self.slot(w, owner, self.c), self.send_up.at[w, owner], self.recv.at[w, owner], self.up)

    def to_down(self, w, owner, src):
        return remote(src, self.slot(w, owner, self.c), self.send_down.at[w, owner], self.recv.at[w, owner], self.down)

    def keep(self, w):
        return pltpu.make_async_copy(self.sources[w], self.slot(w, self.z, self.c), self.here.at[w])

    def own(self, group):
        for w in group:

            @pl.when(self.z + 1 < self.count)
            def _():
                self.to_up(w, self.z, self.sources[w]).start()

            @pl.when(self.z > 0)
            def _():
                self.to_down(w, self.z, self.sources[w]).start()

            self.to_core(w, self.z, self.sources[w]).start()
            self.keep(w).start()
            self.next[w] = 1

    def hand_on(self, w, step):
        low, high = self.z - step, self.z + step

        @pl.when(low >= 0)
        def _():
            got = self.slot(w, low, self.c)
            self.to_up(w, low, got).wait_recv()

            @pl.when(self.z + 1 < self.count)
            def _():
                self.to_up(w, low, got).start()

            self.to_core(w, low, got).start()

        @pl.when(high < self.count)
        def _():
            got = self.slot(w, high, self.c)
            self.to_down(w, high, got).wait_recv()

            @pl.when(self.z > 0)
            def _():
                self.to_down(w, high, got).start()

            self.to_core(w, high, got).start()

    def pump(self, group):
        for w in group:
            if self.next[w] < self.count:
                self.hand_on(w, self.next[w])
                self.next[w] += 1

    def done(self, group):
        for w in group:
            if self.next[w] < self.count:

                @pl.loop(self.next[w], self.count)
                def _(step):
                    self.hand_on(w, step)

            @pl.loop(0, self.count)
            def _(owner):
                got = self.slot(w, owner, self.c)
                self.to_core(w, owner, got).wait()

                @pl.when((owner <= self.z) & (self.z + 1 < self.count))
                def _():
                    self.to_up(w, owner, got).wait_send()

                @pl.when((owner >= self.z) & (self.z > 0))
                def _():
                    self.to_down(w, owner, got).wait_send()

            self.keep(w).wait()


WEIGHTS = named(lambda shared, value, gate, hidden, attended, update, up, down: None)
KINDS = ("row", "row", "row", "col", "col", "col", "row", "col")
A_IN = named(lambda tok, keep, gain, damp, eta, q_gain, k_gain, ids_row, cot: None) + ["s_" + w for w in WEIGHTS]
A_OUT = named(
    lambda rows_update, normed4, mixed4, mix_pre, xn, inv_rows, s_pre, v_pre, g_pre, keys, vals,
    queries, log_sum, attended, gated, hid_pre, upd_pre, cot4: None
) + ["w_" + w for w in WEIGHTS if w != "update"]
A_HBM = named(
    lambda rows_update, normed4, mixed4, mix_pre, xn, v_pre, g_pre, keys, vals, attended, gated,
    hid_pre, upd_pre, cot4: None
) + [
    "w_" + w for w in WEIGHTS if w != "update"
]
A_SCRATCH = named(
    lambda low_n, low_m, rows, ends, starts, end_out, end_in, part_h, got_h, w_update, send, recv,
    s_rows, r_rows, s_core, r_core, s_upd, r_upd, s_kv, r_kv, s_out, z_here, z_up, z_down, z_core,
    z_recv, z_recv_core: None
)


def front_kernel(kinds, sizes, turns, line_count, *refs):
    aside = [w for w, turn in zip(WEIGHTS, turns) if turn and w != "down"]
    names = A_IN + A_OUT + A_SCRATCH + ["v_" + n for n in A_HBM] + ["t_" + w for w in aside]
    m = Named(names, refs)
    outs = {}
    for k, n in enumerate(A_HBM):
        outs[n] = pltpu.make_async_copy(getattr(m, "v_" + n), getattr(m, n), m.s_out.at[k])
        setattr(m, n, getattr(m, "v_" + n))
    out = types.SimpleNamespace(**outs)
    t, x, y, d = tp_peers()
    c = lax.axis_index("ctx")
    other = spot(c=1 - c)
    groups, count = m.xn.shape[0], m.xn.shape[1]
    step, nj, width = count // 8, m.damp.shape[0], m.damp.shape[1]
    B = 256
    half, nb, span = B // 2, count // B, count + B
    scale = 1.0 / math.sqrt(Z)

    def lanes(o):
        return pl.ds(pl.multiple_of(o * width, width), width)

    line = Line(
        kinds, sizes, line_count, [getattr(m, "s_" + w) for w in WEIGHTS],
        [getattr(m, ("t_" if w in aside else "w_") + w) for w in WEIGHTS],
        (m.z_here, m.z_up, m.z_down, m.z_core, m.z_recv, m.z_recv_core),
    )
    first_w, second_w, third_w, fourth_w = (0, 1, 2), (3, 4, 5), (6,), (7,)

    m.end_in[...] = jnp.zeros_like(m.end_in)
    value = m.tok[...].astype(F32)
    m.rows[t] = row_sums(value * value)
    greet([spot(t=x), spot(t=y), spot(t=d), other, line.up, line.down])
    sums = [
        remote(m.rows.at[t], m.rows.at[t], m.s_rows.at[k], m.r_rows.at[k], spot(t=p))
        for k, p in enumerate((x, y, d))
    ]
    for copy in sums:
        copy.start()
    line.own(first_w)
    line.own(second_w)
    for copy in sums:
        copy.wait()
    inv = lax.rsqrt((m.rows[0] + m.rows[1] + m.rows[2] + m.rows[3]) / D + EPSILON)
    m.inv_rows[...] = inv
    normed = m.tok[...].astype(F32) * inv.T[:, 0:1] * m.gain[...]
    m.low_n[...] = normed.astype(BF16)
    for g in range(groups):
        m.xn[g] = normed[:, g * 128 : (g + 1) * 128]
    out.xn.start()
    chunks = 8
    size = count // chunks

    def whole_run(low, place, base):
        return Gather(
            chunks,
            lambda i: low.at[pl.ds(i * size, size)],
            lambda o, i: place.at[pl.ds(i * size, size), lanes(o)],
            m.send, m.recv, base,
        )

    norm_run = whole_run(m.low_n, m.normed4, 0)
    cot_run = whole_run(m.cot, m.cot4, 24)
    mix_runs = [
        Gather(
            4,
            lambda i, g=g: m.low_m.at[pl.ds(i * 2 * size, 2 * size), pl.ds(g * 128, 128)],
            lambda o, i, g=g: m.mixed4.at[
                pl.ds(i * 2 * size, 2 * size), pl.ds(pl.multiple_of(o * width + g * 128, 128), 128)
            ],
            m.send, m.recv, 48 + 12 * g,
        )
        for g in range(groups)
    ]
    norm_run.start()

    for g in range(groups):
        ln = pl.ds(g * 128, 128)
        decay = [wide(1.0 - m.damp[pl.ds(j, 1), ln]) for j in range(nj)]

        def scan(s, carry):
            states, chain = carry
            at = pl.ds(s, 8, stride=step)
            v, k = m.xn[g, at, :], m.keep[at, :]
            return tuple(v + (k * r) * a for r, a in zip(decay, states)), chain * k

        zero = jnp.zeros((8, 128), F32)
        states, chain = lax.fori_loop(0, step, scan, ((zero,) * nj, zero + 1.0), unroll=4)
        for j in range(nj):
            m.ends[0, j, :, ln] = states[j]
            m.ends[1, j, :, ln] = power(decay[j], step) * chain

    last = jnp.zeros((nj, width), F32)
    for q in range(8):
        last = m.ends[0, :, q, :] + m.ends[1, :, q, :] * last
    m.end_out[...] = last
    across = remote(m.end_out, m.end_in, m.s_core.at[0], m.r_core.at[0], other)
    across.start()
    line.pump(first_w)
    line.own(third_w)
    across.wait()
    last = jnp.where(c == 0, 0.0, m.end_in[...])
    for q in range(8):
        m.starts[:, q, :] = last
        last = m.ends[0, :, q, :] + m.ends[1, :, q, :] * last

    for g in range(groups):
        ln = pl.ds(g * 128, 128)
        decay = [wide(1.0 - m.damp[pl.ds(j, 1), ln]) for j in range(nj)]
        weight = [wide(m.damp[pl.ds(j, 1), ln] * m.eta[pl.ds(j, 1), ln]) for j in range(nj)]

        def scan(s, states):
            at = pl.ds(s, 8, stride=step)
            v, k = m.xn[g, at, :], m.keep[at, :]
            states = tuple(v + (k * r) * a for r, a in zip(decay, states))
            m.mix_pre[g, at, :] = v + tree_sum([w * a for w, a in zip(weight, states)])
            return states

        lax.fori_loop(0, step, scan, tuple(m.starts[j, :, ln] for j in range(nj)), unroll=4)
        pre = m.mix_pre[g]
        m.low_m[:, ln] = (pre * sigmoid(pre)).astype(BF16)
        mix_runs[g].start()
    out.mix_pre.start()
    line.pump(first_w)
    line.pump(second_w)
    line.own(fourth_w)
    for o in range(4):

        @pl.when(t == o)
        def _():
            m.normed4[:, o * width : (o + 1) * width] = m.low_n[...]
            m.mixed4[:, o * width : (o + 1) * width] = m.low_m[...]
            m.cot4[:, o * width : (o + 1) * width] = m.cot[...]

    norm_run.forward()
    for run in mix_runs:
        run.forward()
    cot_run.start()
    line.pump(first_w)
    line.pump(second_w)
    line.pump(third_w)
    for run in [norm_run] + mix_runs:
        run.finish()
    out.normed4.start()
    out.mixed4.start()
    line.done(first_w)
    for copy in (out.w_shared, out.w_value, out.w_gate):
        copy.start()

    def rows(i):
        return at_block(i, B)

    def mine(i):
        return pl.ds(pl.multiple_of(count + i * B, B), B)

    def window(i):
        return pl.ds(pl.multiple_of(i * B, B), span)

    def kv_run(i):
        return [
            remote(m.keys.at[mine(i)], m.keys.at[rows(i)], m.s_kv.at[2 * i], m.r_kv.at[2 * i], other),
            remote(m.vals.at[mine(i)], m.vals.at[rows(i)], m.s_kv.at[2 * i + 1], m.r_kv.at[2 * i + 1], other),
        ]

    @pl.loop(0, nb)
    def _(i):
        value = dot(m.normed4[rows(i), :], m.w_value[...])
        m.v_pre[rows(i), :] = value.astype(BF16)
        m.vals[mine(i), :] = (value * sigmoid(value)).astype(BF16)
        pre = dot(m.mixed4[rows(i), :], m.w_shared[...])
        m.s_pre[rows(i), :] = pre
        shared = pre * sigmoid(pre)
        m.queries[rows(i), :] = (shared * m.q_gain[...]).astype(BF16)
        m.keys[mine(i), :] = (shared * m.k_gain[...]).astype(BF16)
        for copy in kv_run(i):
            copy.start()
        m.g_pre[rows(i), :] = dot(m.mixed4[rows(i), :], m.w_gate[...])

    out.v_pre.start()
    out.g_pre.start()
    cot_run.forward()
    line.pump(second_w)
    line.pump(third_w)
    line.pump(fourth_w)
    for i in range(nb):
        for copy in kv_run(i):
            copy.wait()
    out.keys.start()
    out.vals.start()
    line.done(second_w)
    for w in aside:
        getattr(m, "w_" + w)[...] = getattr(m, "t_" + w)[...].astype(F32).T.astype(BF16)
    for copy in (out.w_hidden, out.w_attended):
        copy.start()
    upd = [
        remote(m.w_update.at[:, lanes(p)], m.rows_update.at[pl.ds(pl.multiple_of(t * width, width), width)],
               m.s_upd.at[n], m.r_upd.at[n], spot(t=p))
        for n, p in enumerate((x, y, d))
    ]
    for copy in upd:
        copy.start()
    for o in range(4):

        @pl.when(t == o)
        def _():
            m.rows_update[o * width : (o + 1) * width, :] = m.w_update[:, o * width : (o + 1) * width]

    def run_h(i):
        return Scatter(
            2,
            lambda o, n: m.part_h.at[o, pl.ds(pl.multiple_of(i * B + n * half, half), half)],
            lambda n: m.got_h.at[0, i * 2 + n],
            lambda n: m.got_h.at[1, i * 2 + n],
            lambda n: m.got_h.at[2, i * 2 + n],
            m.send, m.recv, 48 + 12 * groups + i * 6,
        )

    def attend(i):
        raw = dot_t(m.queries[rows(i), :], m.keys[window(i), :]) * scale
        same = as_column(m.ids_row[:, mine(i)]) == m.ids_row[0:1, window(i)]
        place = lax.broadcasted_iota(jnp.int32, raw.shape, 1) - lax.broadcasted_iota(jnp.int32, raw.shape, 0)
        s = jnp.where(same & (place <= count), raw, -1e30)
        peak = jnp.max(s, axis=1, keepdims=True)
        e = jnp.exp(s - peak)
        total = jnp.sum(e, axis=1, keepdims=True)
        m.log_sum[rows(i), :] = jnp.broadcast_to(peak + jnp.log(total), (B, 128))
        attended = dot((e * (1.0 / total)).astype(BF16), m.vals[window(i), :])
        m.attended[rows(i), :] = attended.astype(BF16)
        gate = m.g_pre[rows(i), :]
        gated = (gate * sigmoid(gate) * attended).astype(BF16)
        m.gated[rows(i), :] = gated
        part = dot(m.mixed4[rows(i), lanes(t)], m.w_hidden[...]) + dot(gated, m.w_attended[...])
        part = part.astype(BF16)
        for o in range(4):
            m.part_h[o, rows(i), :] = part[:, o * width : (o + 1) * width]
        run_h(i).start()

    def collect(i):
        run = run_h(i)
        for n in range(2):
            m.hid_pre[pl.ds(i * B + n * half, half), :] = run.collect(n) + run.part(t, n)[...].astype(F32)
        run.finish()

    @pl.loop(0, nb)
    def _(i):
        attend(i)

        @pl.when(i > 0)
        def _():
            run_h(i - 1).forward()

    line.pump(third_w)
    line.pump(fourth_w)
    out.attended.start()
    out.gated.start()
    for copy in upd:
        copy.wait()
    run_h(nb - 1).forward()

    @pl.loop(0, nb)
    def _(i):
        m.upd_pre[rows(i), :] = dot(m.mixed4[rows(i), :], m.rows_update[...])

    out.upd_pre.start()
    out.rows_update.start()
    for i in range(nb):
        collect(i)
    out.hid_pre.start()
    cot_run.finish()
    out.cot4.start()
    line.done(third_w)
    out.w_up.start()
    line.done(fourth_w)
    out.w_down.start()
    for copy in outs.values():
        copy.wait()


def front(ident, line_count, tok, keep, gain, damp, eta, q_gain, k_gain, ids_row, cot, shards):
    count, width = tok.shape
    groups, nj = width // 128, damp.shape[0]
    nb = count // 256
    turns = [turned(k, s.shape[1]) for k, s in zip(KINDS, shards)]
    shards = [s.T if turn else s for turn, s in zip(turns, shards)]
    kinds = ["row" if turn else k for turn, k in zip(turns, KINDS)]
    sizes = [s.shape[0] if k == "row" else s.shape[1] for k, s in zip(kinds, shards)]
    full = 4 * width
    values = shards[1].shape[1]
    s = jax.ShapeDtypeStruct
    outs = dict(
        rows_update=s((full, width), BF16),
        normed4=s((count, full), BF16),
        mixed4=s((count, full), BF16),
        mix_pre=s((groups, count, 128), F32),
        xn=s((groups, count, 128), F32),
        inv_rows=s((8, count), F32),
        s_pre=s((count, Z), F32),
        v_pre=s((count, values), BF16),
        g_pre=s((count, values), F32),
        keys=s((2 * count, Z), BF16),
        vals=s((2 * count, values), BF16),
        queries=s((count, Z), BF16),
        log_sum=s((count, 128), F32),
        attended=s((count, values), BF16),
        gated=s((count, values), BF16),
        hid_pre=s((count, width), F32),
        upd_pre=s((count, width), F32),
        cot4=s((count, full), BF16),
    )
    aside = []
    for name, kind, size, shard in zip(WEIGHTS, kinds, sizes, shards):
        shape = (2 * line_count * size, shard.shape[1]) if kind == "row" else (shard.shape[0], 2 * line_count * size)
        if kind == "row" and turns[WEIGHTS.index(name)] and name != "down":
            aside.append(pltpu.VMEM(shape, shard.dtype))
            shape = shape[::-1]
        outs["w_" + name] = s(shape, shard.dtype)
    v, dma, k = pltpu.VMEM, pltpu.SemaphoreType.DMA, len(WEIGHTS)
    n = 48 + 12 * groups + 6 * nb
    scratch = dict(
        low_n=v((count, width), BF16),
        low_m=v((count, width), BF16),
        rows=v((4, 8, count), F32),
        ends=v((2, nj, 8, width), F32),
        starts=v((nj, 8, width), F32),
        end_out=v((nj, width), F32),
        end_in=v((nj, width), F32),
        part_h=v((4, count, width), BF16),
        got_h=v((3, 2 * nb, 128, width), BF16),
        w_update=v(outs["w_update"].shape, BF16),
        send=dma((n,)), recv=dma((n,)), s_rows=dma((3,)), r_rows=dma((3,)), s_core=dma((1,)), r_core=dma((1,)),
        s_upd=dma((3,)), r_upd=dma((3,)), s_kv=dma((2 * nb,)), r_kv=dma((2 * nb,)), s_out=dma((len(A_HBM),)),
        z_here=dma((k,)), z_up=dma((k, line_count)), z_down=dma((k, line_count)), z_core=dma((k, line_count)),
        z_recv=dma((k, line_count)), z_recv_core=dma((k, line_count)),
    )
    got = pl.pallas_call(
        functools.partial(front_kernel, kinds, sizes, turns, line_count),
        out_shape=[outs[n] for n in A_OUT],
        in_specs=[VMEM] * len(A_IN),
        out_specs=[ANY if n in A_HBM else VMEM for n in A_OUT],
        scratch_shapes=[scratch[n] for n in A_SCRATCH] + [v(outs[n].shape, outs[n].dtype) for n in A_HBM] + aside,
        compiler_params=pltpu.CompilerParams(collective_id=ident, has_side_effects=True, vmem_limit_bytes=60 * 2**20),
        name="front",
    )(tok, keep, gain[None], damp, eta, q_gain[None], k_gain[None], ids_row, cot, *shards)
    a = Named(A_OUT, got)
    if turns[WEIGHTS.index("down")]:
        a.w_down = a.w_down.T
    return a


class LineSum:
    def __init__(self, kinds, sizes, count, sources, pair, line, outs, sems):
        self.kinds, self.sizes, self.count = kinds, sizes, count
        self.sources, self.pair, self.line, self.outs = sources, pair, line, outs
        self.send_core, self.recv_core, self.send, self.recv = sems
        self.z, self.c = lax.axis_index("fsdp"), lax.axis_index("ctx")
        self.other = spot(c=1 - self.c)

    def block(self, w, owner, core):
        return shard_at(self.sources[w], self.kinds[w], owner * 2 + core, self.sizes[w])

    def across(self, w, owner):
        return remote(
            self.block(w, owner, 1 - self.c), self.pair[w].at[owner],
            self.send_core.at[w, owner], self.recv_core.at[w, owner], self.other,
        )

    def along(self, w, k):
        owner = (self.z + k) % self.count
        return remote(
            self.pair[w].at[owner], self.line[w].at[self.z], self.send.at[w, k], self.recv.at[w, self.z],
            spot(f=owner),
        )

    def start(self, w):
        @pl.loop(1, self.count + 1)
        def _(k):
            self.across(w, (self.z + k) % self.count).start()

    def plus(self, w, owner):
        return self.pair[w][owner].astype(F32) + self.block(w, owner, self.c)[...].astype(F32)

    def send_on(self, w):
        @pl.loop(1, self.count)
        def _(k):
            owner = (self.z + k) % self.count
            self.across(w, owner).wait_recv()
            self.pair[w][owner] = self.plus(w, owner).astype(BF16)
            self.along(w, k).start()

    def end(self, w):
        self.across(w, self.z).wait_recv()
        self.outs[w][...] = self.plus(w, self.z)

        @pl.loop(1, self.count)
        def _(k):
            source = (self.z + k) % self.count
            got = self.line[w].at[source]
            remote(got, got, self.send.at[w, k], self.recv.at[w, source], self.other).wait_recv()
            self.outs[w][...] += got[...].astype(F32)
            self.along(w, k).wait_send()

        @pl.loop(0, self.count)
        def _(owner):
            self.across(w, owner).wait_send()


def line_plan(shapes, kinds, count):
    turns = [turned(k, s[1] // (2 * count)) for k, s in zip(kinds, shapes)]
    shapes = [s[::-1] if turn else s for turn, s in zip(turns, shapes)]
    kinds = ["row" if turn else k for turn, k in zip(turns, kinds)]
    sizes = [s[0 if k == "row" else 1] // (2 * count) for k, s in zip(kinds, shapes)]
    blocks = [(n, s[1]) if k == "row" else (s[0], n) for k, n, s in zip(kinds, sizes, shapes)]
    return turns, kinds, sizes, shapes, blocks


def line_peers(count):
    z = lax.axis_index("fsdp")
    return [spot(f=(z + k) % count) for k in range(1, count)]


MID_LOAD = named(
    lambda hid_pre, upd_pre, w_down, cot4, w_up, w_attended, g_pre, attended, w_gate, w_upd,
    w_hidden, queries, keys, vals, log_sum, v_pre: None
)
MID_IN = MID_LOAD + named(lambda tok, cot, f_gain, ids_row: None)
MID_STORE = named(
    lambda block, part_f, part_t, tok_grad, mix_grad, value_grad, hid4, upd_grad, gate_grad: None
)
MID_OUT = MID_STORE + named(lambda f_gain_grad, q_grad, k_grad, d_up, d_down: None)
MID_SCRATCH = named(
    lambda up_rows, up_grads, ffn4, att_grad, k_all, v_all, part_g, got_g, low, rows_a, rows_b,
    k_send, v_send, k_got, v_got, p_up, p_down, l_up, l_down, send, recv, s_rows, r_rows, s_gr,
    r_gr, s_in, s_out, c_send, c_recv, l_send, l_recv: None
)


def mid_kernel(kinds, sizes, turns, line_count, *refs):
    m = Named(
        MID_IN + MID_OUT + MID_SCRATCH + ["i_" + n for n in MID_LOAD] + ["o_" + n for n in MID_STORE], refs
    )
    loads, stores = {}, {}
    for k, n in enumerate(MID_LOAD):
        loads[n] = Transfer(pltpu.make_async_copy(getattr(m, n), getattr(m, "i_" + n), m.s_in.at[k]))
        setattr(m, n, getattr(m, "i_" + n))
        loads[n].start()
    for k, n in enumerate(MID_STORE):
        stores[n] = pltpu.make_async_copy(getattr(m, "o_" + n), getattr(m, n), m.s_out.at[k])
        setattr(m, n, getattr(m, "o_" + n))
    load, store = types.SimpleNamespace(**loads), types.SimpleNamespace(**stores)
    t, x, y, d = tp_peers()
    other = spot(c=1 - lax.axis_index("ctx"))
    count, width = m.tok.shape
    B = 256
    half, nb, span = B // 2, count // B, count + B
    scale = 1.0 / math.sqrt(Z)

    def rows(i):
        return at_block(i, B)

    def mine(i):
        return pl.ds(count + i * B, B)

    def window(i):
        return pl.ds(i * B, span)

    def lanes(o):
        return pl.ds(pl.multiple_of(o * width, width), width)

    greet([spot(t=x), spot(t=y), spot(t=d), other] + line_peers(line_count))
    m.f_gain_grad[...] = jnp.zeros_like(m.f_gain_grad)

    def gather_run(kind, i, low, place):
        return Gather(
            2,
            lambda n: low.at[pl.ds(i * B + n * half, half)],
            lambda o, n: place.at[pl.ds(i * B + n * half, half), lanes(o)],
            m.send, m.recv, (kind * nb + i) * 6,
        )

    def scatter_run(kind, i, part, got):
        return Scatter(
            2,
            lambda o, n: part.at[o, pl.ds(i * B + n * half, half)],
            lambda n: got.at[0, i * 2 + n],
            lambda n: got.at[1, i * 2 + n],
            lambda n: got.at[2, i * 2 + n],
            m.send, m.recv, (kind * nb + i) * 6,
        )

    run_p = [gather_run(0, i, m.low, m.ffn4) for i in range(nb)]
    run_gh = [gather_run(1, i, m.low, m.hid4) for i in range(nb)]
    run_g = [scatter_run(2, i, m.part_g, m.got_g) for i in range(nb)]
    line = LineSum(
        kinds, sizes, line_count, [m.w_up, m.w_down], [m.p_up, m.p_down], [m.l_up, m.l_down], [m.d_up, m.d_down],
        (m.c_send, m.c_recv, m.l_send, m.l_recv),
    )

    def row_run(kind, i, buf):
        return [
            remote(
                buf.at[t, :, rows(i)], buf.at[t, :, rows(i)],
                m.s_rows.at[(kind * nb + i) * 3 + n], m.r_rows.at[(kind * nb + i) * 3 + n], spot(t=p),
            )
            for n, p in enumerate((x, y, d))
        ]

    def row_total(buf, i):
        return buf[0, :, rows(i)] + buf[1, :, rows(i)] + buf[2, :, rows(i)] + buf[3, :, rows(i)]

    def split(part, i, value):
        low = value.astype(BF16)
        for o in range(4):
            part[o, rows(i), :] = low[:, o * width : (o + 1) * width]

    def place_own(full_ref, i):
        for o in range(4):

            @pl.when(t == o)
            def _():
                full_ref[rows(i), o * width : (o + 1) * width] = m.low[rows(i), :]

    def joined(run):
        pieces = [run.collect(n) + run.part(t, n)[...].astype(F32) for n in range(2)]
        return jnp.concatenate(pieces, axis=0)

    def inverse_mid(i):
        return lax.rsqrt(row_total(m.rows_a, i) / D + EPSILON)

    def block_stage(i):
        need(load.hid_pre, load.upd_pre)
        hidden_pre, update = m.hid_pre[rows(i), :], sigmoid(m.upd_pre[rows(i), :])
        block = update * (hidden_pre * sigmoid(hidden_pre)) + (1.0 - update) * m.tok[rows(i), :].astype(F32)
        m.block[rows(i), :] = block
        m.low[rows(i), :] = (block * m.f_gain[...]).astype(BF16)
        run_p[i].start()
        m.rows_a[t, :, rows(i)] = as_rows(jnp.sum(block * block, axis=1, keepdims=True))
        for copy in row_run(0, i, m.rows_a):
            copy.start()
        place_own(m.ffn4, i)

    def ffn_stage(i):
        need(load.w_down, load.cot4)
        back = dot_t(m.cot4[rows(i), :], m.w_down[...])
        run_p[i].finish()
        for copy in row_run(0, i, m.rows_a):
            copy.wait()
        need(load.w_up)
        inv = as_column(inverse_mid(i))
        raw = dot(m.ffn4[rows(i), :], m.w_up[...])
        up_pre = raw * inv
        sig = sigmoid(up_pre)
        grad_up = (back * d_silu(up_pre, sig)).astype(BF16)
        split(m.part_g, i, dot_t(grad_up, m.w_up[...]))
        run_g[i].start()
        wide_grad = grad_up.astype(F32)
        m.up_grads[rows(i), :] = (wide_grad * inv).astype(BF16)
        m.rows_b[t, :, rows(i)] = as_rows(jnp.sum(wide_grad * raw, axis=1, keepdims=True))
        for copy in row_run(1, i, m.rows_b):
            copy.start()
        up_rows = (up_pre * sig).astype(BF16)
        m.up_rows[rows(i), :] = up_rows
        split(m.part_f, i, dot(up_rows, m.w_down[...]))

    def grad_stage(i):
        grad_ffn = joined(run_g[i])
        for copy in row_run(1, i, m.rows_b):
            copy.wait()
        block = m.block[rows(i), :]
        inv_rows = inverse_mid(i)
        factor = inv_rows * inv_rows * inv_rows * row_total(m.rows_b, i) / D
        inv = as_column(inv_rows)
        grad_block = (
            m.cot[rows(i), :].astype(F32) + inv * (grad_ffn * m.f_gain[...]) - block * as_column(factor)
        )
        m.f_gain_grad[...] += jnp.sum(grad_ffn * block * inv, axis=0, keepdims=True)
        hidden_pre, update = m.hid_pre[rows(i), :], sigmoid(m.upd_pre[rows(i), :])
        sig = sigmoid(hidden_pre)
        m.low[rows(i), :] = (grad_block * update * d_silu(hidden_pre, sig)).astype(BF16)
        run_gh[i].start()
        keep = grad_block * (1.0 - update)
        m.tok_grad[rows(i), :] = keep
        tokens = m.tok[rows(i), :].astype(F32)
        m.upd_grad[rows(i), :] = (keep * (hidden_pre * sig - tokens) * update).astype(BF16)
        place_own(m.hid4, i)
        run_g[i].finish()

    def gate_stage(i):
        need(load.w_attended, load.g_pre, load.attended, load.w_gate, load.w_upd, load.w_hidden)
        run_gh[i].finish()
        grad_hidden = m.hid4[rows(i), :]
        grad_gated = dot_t(grad_hidden, m.w_attended[...])
        gate = m.g_pre[rows(i), :]
        sig = sigmoid(gate)
        grad_gate = (grad_gated * m.attended[rows(i), :].astype(F32) * d_silu(gate, sig)).astype(BF16)
        m.gate_grad[rows(i), :] = grad_gate
        split(m.part_t, i, dot_t(grad_gate, m.w_gate[...]) + dot_t(m.upd_grad[rows(i), :], m.w_upd[...]))
        m.att_grad[rows(i), :] = (grad_gated * (gate * sig)).astype(BF16)
        m.mix_grad[rows(i), :] = dot_t(grad_hidden, m.w_hidden[...])

    def grads_run(i):
        return [
            remote(m.k_send.at[rows(i)], m.k_got.at[rows(i)], m.s_gr.at[2 * i], m.r_gr.at[2 * i], other),
            remote(m.v_send.at[rows(i)], m.v_got.at[rows(i)], m.s_gr.at[2 * i + 1], m.r_gr.at[2 * i + 1], other),
        ]

    def attend_back(i):
        need(load.queries, load.keys, load.vals, load.log_sum)
        raw = dot_t(m.queries[rows(i), :], m.keys[window(i), :]) * scale
        same = as_column(m.ids_row[:, mine(i)]) == m.ids_row[0:1, window(i)]
        place = lax.broadcasted_iota(jnp.int32, raw.shape, 1) - lax.broadcasted_iota(jnp.int32, raw.shape, 0)
        exact = jnp.exp(jnp.where(same & (place <= count), raw, -1e30) - m.log_sum[rows(i), 0:1])
        grad_rows = m.att_grad[rows(i), :]
        value_part = t_dot(exact.astype(BF16), grad_rows)
        grad_probs = dot_t(grad_rows, m.vals[window(i), :])
        inner = jnp.sum(exact * grad_probs, axis=1, keepdims=True)
        grad_scores = exact * (grad_probs - inner) * scale
        high = grad_scores.astype(BF16)
        rest = (grad_scores - high.astype(F32)).astype(BF16)
        keys, queries = m.keys[window(i), :], m.queries[rows(i), :]
        m.q_grad[rows(i), :] = dot(high, keys) + dot(rest, keys)
        key_part = t_dot(high, queries) + t_dot(rest, queries)
        if i == 0:
            m.v_all[window(0), :] = value_part
            m.k_all[window(0), :] = key_part
        else:
            old, new = pl.ds(i * B, span - B), pl.ds(span + (i - 1) * B, B)
            m.v_all[old, :] += value_part[: span - B]
            m.v_all[new, :] = value_part[span - B :]
            m.k_all[old, :] += key_part[: span - B]
            m.k_all[new, :] = key_part[span - B :]
        m.k_send[rows(i), :] = m.k_all[rows(i), :].astype(BF16)
        m.v_send[rows(i), :] = m.v_all[rows(i), :].astype(BF16)
        for copy in grads_run(i):
            copy.start()

    def product(w, left, right):
        if turns[w]:
            left, right = right, left
        dst = line.sources[w]
        for k in range(right.shape[1] // B):
            at = slice(k * B, (k + 1) * B)
            dst[:, at] = t_dot(left[...], right[:, at]).astype(BF16)
        line.start(w)

    def key_end(i):
        need(load.v_pre)
        for copy in grads_run(i):
            copy.wait()
        m.k_grad[rows(i), :] = m.k_all[mine(i), :] + m.k_got[rows(i), :].astype(F32)
        value = m.v_pre[rows(i), :].astype(F32)
        grad = m.v_all[mine(i), :] + m.v_got[rows(i), :].astype(F32)
        m.value_grad[rows(i), :] = (grad * d_silu(value, sigmoid(value))).astype(BF16)

    block_stage(0)
    block_stage(1)
    block_stage(2)
    block_stage(3)
    run_p[0].forward()
    run_p[1].forward()
    ffn_stage(0)
    run_p[2].forward()
    run_p[3].forward()
    ffn_stage(1)
    run_g[0].forward()
    ffn_stage(2)
    run_g[1].forward()
    grad_stage(0)
    ffn_stage(3)
    run_g[2].forward()
    grad_stage(1)
    run_gh[0].forward()
    store.block.start()
    store.part_f.start()
    product(1, m.up_rows, m.cot4)
    run_g[3].forward()
    grad_stage(2)
    run_gh[1].forward()
    gate_stage(0)
    product(0, m.ffn4, m.up_grads)
    line.send_on(1)
    grad_stage(3)
    run_gh[2].forward()
    gate_stage(1)
    attend_back(0)
    line.send_on(0)
    run_gh[3].forward()
    gate_stage(2)
    attend_back(1)
    gate_stage(3)
    store.hid4.start()
    store.upd_grad.start()
    store.gate_grad.start()
    store.tok_grad.start()
    store.part_t.start()
    store.mix_grad.start()
    attend_back(2)
    attend_back(3)
    key_end(0)
    key_end(1)
    key_end(2)
    key_end(3)
    store.value_grad.start()
    line.end(1)
    line.end(0)
    for copy in stores.values():
        copy.wait()


def middle(ident, line_count, ins):
    tok, f_gain = ins["tok"], ins["f_gain"]
    count, width = tok.shape
    full = 4 * width
    values, hidden = ins["w_gate"].shape[1], ins["w_up"].shape[1]
    nb = count // 256
    turns, kinds, sizes, _, blocks = line_plan([(full, hidden), (hidden, full)], KINDS[-2:], line_count)
    dma, s, v = pltpu.SemaphoreType.DMA, jax.ShapeDtypeStruct, pltpu.VMEM
    outs = dict(
        block=s((count, width), F32),
        part_f=s((4, count, width), BF16),
        part_t=s((4, count, width), BF16),
        tok_grad=s((count, width), F32),
        mix_grad=s((count, width), F32),
        value_grad=s((count, values), BF16),
        hid4=s((count, full), BF16),
        upd_grad=s((count, width), BF16),
        gate_grad=s((count, values), BF16),
        f_gain_grad=s((1, width), F32),
        q_grad=s((count, Z), F32),
        k_grad=s((count, Z), F32),
        d_up=s(blocks[0], F32),
        d_down=s(blocks[1], F32),
    )
    scratch = dict(
        up_rows=v((count, hidden), BF16),
        up_grads=v((count, hidden), BF16),
        ffn4=v((count, full), BF16),
        att_grad=v((count, values), BF16),
        k_all=v((2 * count, Z), F32),
        v_all=v((2 * count, values), F32),
        part_g=v((4, count, width), BF16),
        got_g=v((3, 2 * nb, 128, width), BF16),
        low=v((count, width), BF16),
        rows_a=v((4, 8, count), F32),
        rows_b=v((4, 8, count), F32),
        k_send=v((count, Z), BF16),
        v_send=v((count, values), BF16),
        k_got=v((count, Z), BF16),
        v_got=v((count, values), BF16),
        p_up=v((line_count,) + blocks[0], BF16),
        p_down=v((line_count,) + blocks[1], BF16),
        l_up=v((line_count,) + blocks[0], BF16),
        l_down=v((line_count,) + blocks[1], BF16),
        c_send=dma((2, line_count)), c_recv=dma((2, line_count)),
        l_send=dma((2, line_count)), l_recv=dma((2, line_count)),
        send=dma((18 * nb,)), recv=dma((18 * nb,)),
        s_rows=dma((6 * nb,)), r_rows=dma((6 * nb,)),
        s_gr=dma((2 * nb,)), r_gr=dma((2 * nb,)),
        s_in=dma((len(MID_LOAD),)), s_out=dma((len(MID_STORE),)),
    )
    got_all = pl.pallas_call(
        functools.partial(mid_kernel, kinds, sizes, turns, line_count),
        out_shape=[outs[n] for n in MID_OUT],
        in_specs=[ANY if n in MID_LOAD else VMEM for n in MID_IN],
        out_specs=[ANY if n in MID_STORE else VMEM for n in MID_OUT],
        scratch_shapes=[scratch[n] for n in MID_SCRATCH]
        + [v(ins[n].shape, ins[n].dtype) for n in MID_LOAD]
        + [v(outs[n].shape, outs[n].dtype) for n in MID_STORE],
        compiler_params=pltpu.CompilerParams(collective_id=ident, has_side_effects=True, vmem_limit_bytes=62 * 2**20),
        name="middle",
    )(*[ins[n] for n in MID_IN])
    got_all = Named(MID_OUT, got_all)
    if turns[1]:
        got_all.d_down = got_all.d_down.T
    return got_all


REAR_LOAD = named(
    lambda part_t, value_grad, w_value, gated, hid4, mixed4, upd_grad, gate_grad, normed4, part_f,
    mix_grad, mix_pre, xn, tok_grad, block: None
)
REAR_IN = REAR_LOAD + named(
    lambda q_grad, k_grad, s_pre, w_shared, tok, inv_rows, keep_next, gain, damp, eta, q_gain,
    k_gain, f_gain_grad: None
)
REAR_WEIGHTS = WEIGHTS[:-2]
REAR_OUT = named(lambda grad_in, small, out: None) + ["d_" + w for w in REAR_WEIGHTS]
REAR_SCRATCH = named(
    lambda part_v, got_v, got_t, got_f, part_s, got_s, low_s, full_s, grad_mix, back, rows, ends,
    starts, end_out, end_in, small_core, small_all, own_q, all_q, upd_cols, send, recv, s_rows,
    r_rows, s_core, r_core, s_upd, r_upd, s_small, r_small, s_q, r_q, s_in, c_send, c_recv, l_send,
    l_recv: None
)


def rear_kernel(kinds, sizes, turns, line_count, *refs):
    groups_of = [p + w for p in ("p_", "g_", "l_") for w in REAR_WEIGHTS]
    m = Named(REAR_IN + REAR_OUT + REAR_SCRATCH + groups_of + ["i_" + n for n in REAR_LOAD], refs)
    loads = {}
    for k, n in enumerate(REAR_LOAD):
        loads[n] = Transfer(pltpu.make_async_copy(getattr(m, n), getattr(m, "i_" + n), m.s_in.at[k]))
        setattr(m, n, getattr(m, "i_" + n))
        loads[n].start()
    load = types.SimpleNamespace(**loads)
    t, x, y, d = tp_peers()
    z, c = lax.axis_index("fsdp"), lax.axis_index("ctx")
    other = spot(c=1 - c)
    groups, count = m.xn.shape[0], m.xn.shape[1]
    step, nj, width = count // 8, m.damp.shape[0], m.damp.shape[1]
    B = 256
    half, nb = B // 2, count // B
    part = 8
    zero = jnp.zeros((8, 128), F32)

    def lanes(o):
        return pl.ds(pl.multiple_of(o * width, width), width)

    line = LineSum(
        kinds, sizes, line_count,
        [getattr(m, "g_" + w) for w in REAR_WEIGHTS], [getattr(m, "p_" + w) for w in REAR_WEIGHTS],
        [getattr(m, "l_" + w) for w in REAR_WEIGHTS], [getattr(m, "d_" + w) for w in REAR_WEIGHTS],
        (m.c_send, m.c_recv, m.l_send, m.l_recv),
    )
    m.end_in[...] = jnp.zeros_like(m.end_in)
    greet([spot(t=x), spot(t=y), spot(t=d), other] + line_peers(line_count))

    run_s = Scatter(
        2,
        lambda o, n: m.part_s.at[pl.ds(pl.multiple_of(o * B + n * half, half), half)],
        lambda n: m.got_s.at[0, n], lambda n: m.got_s.at[1, n], lambda n: m.got_s.at[2, n],
        m.send, m.recv, 0,
    )
    run_full = Gather(
        2,
        lambda n: m.low_s.at[pl.ds(n * half, half)],
        lambda o, n: m.full_s.at[pl.ds(pl.multiple_of(o * B + n * half, half), half)],
        m.send, m.recv, 6,
    )

    def scatter_runs(kind, parts, got):
        return [
            Scatter(
                2,
                lambda o, n, i=i: parts.at[o, pl.ds(i * B + n * half, half)],
                lambda n, i=i: got.at[0, i * 2 + n],
                lambda n, i=i: got.at[1, i * 2 + n],
                lambda n, i=i: got.at[2, i * 2 + n],
                m.send, m.recv, 12 + 6 * (kind * nb + i),
            )
            for i in range(nb)
        ]

    run_t, run_v, run_f = (
        scatter_runs(k, parts, got)
        for k, (parts, got) in enumerate(((m.part_t, m.got_t), (m.part_v, m.got_v), (m.part_f, m.got_f)))
    )

    m.part_s[...] = (m.q_grad[...] * m.q_gain[...] + m.k_grad[...] * m.k_gain[...]).astype(BF16)
    run_s.start()
    shared = m.s_pre[...] * sigmoid(m.s_pre[...])
    m.own_q[...] = jnp.zeros_like(m.own_q)
    m.own_q[0:1, 0:Z] = jnp.sum(shared * m.q_grad[...], axis=0, keepdims=True)
    m.own_q[0:1, Z:] = jnp.sum(shared * m.k_grad[...], axis=0, keepdims=True)
    m.all_q[t] = m.own_q[...]
    gains = [
        remote(m.own_q, m.all_q.at[t], m.s_q.at[k], m.r_q.at[k], spot(t=p)) for k, p in enumerate((x, y, d))
    ]
    for copy in gains:
        copy.start()
    need(load.part_t)
    for run in run_t:
        run.start()
    def product(w, left, right):
        dst = getattr(m, "g_" + w)
        if turns[REAR_WEIGHTS.index(w)]:
            left, right = right, left
        size = min(256, right.shape[1])
        for k in range(right.shape[1] // size):
            at = slice(k * size, (k + 1) * size)
            dst[:, at] = t_dot(left, right[:, at]).astype(BF16)

    at_w = {w: k for k, w in enumerate(REAR_WEIGHTS)}

    need(load.value_grad, load.w_value)

    def value_part(i):
        rows = slice(i * B, (i + 1) * B)
        low = dot_t(m.value_grad[rows, :], m.w_value[...]).astype(BF16)
        for o in range(4):
            m.part_v[o, rows, :] = low[:, o * width : (o + 1) * width]

    need(load.gated, load.hid4)
    product("attended", m.gated[...], m.hid4[...])
    line.start(at_w["attended"])
    run_s.forward()
    value_part(0)
    value_part(1)
    run_t[0].forward()
    run_t[1].forward()
    value_part(2)
    value_part(3)
    line.send_on(at_w["attended"])
    quarter = pl.ds(pl.multiple_of(t * B, B), B)
    for n in range(2):
        total = run_s.collect(n) + run_s.part(t, n)[...].astype(F32)
        pre = m.s_pre[pl.ds(pl.multiple_of(t * B + n * half, half), half), :]
        m.low_s[n * half : (n + 1) * half, :] = (total * d_silu(pre, sigmoid(pre))).astype(BF16)
    run_full.start()
    m.full_s[quarter, :] = m.low_s[...]
    run_t[2].forward()
    run_t[3].forward()
    for run in run_v:
        run.start()
    need(load.mixed4, load.upd_grad)
    turn_update = turns[at_w["update"]]
    if turn_update:
        m.upd_cols[...] = t_dot(m.upd_grad[...], m.mixed4[...]).astype(BF16)
    else:
        m.upd_cols[...] = t_dot(m.mixed4[...], m.upd_grad[...]).astype(BF16)

    def ends_of(p):
        if turn_update:
            return m.upd_cols.at[:, lanes(p)], m.g_update.at[lanes(t)]
        return m.upd_cols.at[lanes(p)], m.g_update.at[:, lanes(t)]

    turn_copies = [
        remote(*ends_of(p), m.s_upd.at[k], m.r_upd.at[k], spot(t=p)) for k, p in enumerate((x, y, d))
    ] + [pltpu.make_async_copy(*ends_of(t), m.s_upd.at[3])]
    for copy in turn_copies:
        copy.start()
    product("hidden", m.mixed4[:, lanes(t)], m.hid4[...])
    line.start(at_w["hidden"])
    run_full.forward()
    need(load.gate_grad, load.normed4)
    product("gate", m.mixed4[...], m.gate_grad[...])
    line.start(at_w["gate"])
    line.send_on(at_w["hidden"])
    for copy in turn_copies:
        copy.wait()
    line.start(at_w["update"])
    run_v[0].forward()
    run_v[1].forward()
    product("value", m.normed4[...], m.value_grad[...])
    line.start(at_w["value"])
    line.send_on(at_w["gate"])
    line.send_on(at_w["update"])
    run_s.finish()
    run_full.finish()
    product("shared", m.mixed4[...], m.full_s[...])
    line.start(at_w["shared"])
    line.send_on(at_w["value"])
    run_v[2].forward()
    run_v[3].forward()
    need(load.mix_grad, load.mix_pre, load.xn, load.tok_grad)
    own_shared = m.w_shared[lanes(t), :]
    for i in range(nb):
        for n in range(2):
            at = pl.ds(i * B + n * half, half)
            mix = m.mix_grad[at, :] + run_t[i].collect(n) + run_t[i].part(t, n)[...].astype(F32)
            mix = mix + dot_t(m.full_s[at, :], own_shared)
            for g in range(groups):
                pre = m.mix_pre[g, at, :]
                m.grad_mix[g, at, :] = mix[:, g * 128 : (g + 1) * 128] * d_silu(pre, sigmoid(pre))
        run_t[i].finish()
    need(load.part_f, load.block)
    for run in run_f:
        run.start()
    line.send_on(at_w["shared"])

    for g in range(groups):
        ln = pl.ds(g * 128, 128)
        for j0 in range(0, nj, part):
            decay = [wide(1.0 - m.damp[pl.ds(j, 1), ln]) for j in range(j0, j0 + part)]

            def scan(i, carry):
                a, w, chain = carry
                at = pl.ds(step - 1 - i, 8, stride=step)
                v, k = m.grad_mix[g, at, :], m.keep_next[at, :]
                held = [k * r for r in decay]
                w = tuple(k * p + r * q for p, r, q in zip(a, held, w))
                a = tuple(v + r * p for r, p in zip(held, a))
                return a, w, chain * k

            a, w, chain = lax.fori_loop(0, step, scan, ((zero,) * part, (zero,) * part, zero + 1.0), unroll=4)
            for n in range(part):
                less = power(decay[n], step - 1)
                m.ends[0, j0 + n, :, ln] = a[n]
                m.ends[1, j0 + n, :, ln] = w[n]
                m.ends[2, j0 + n, :, ln] = less * decay[n] * chain
                m.ends[3, j0 + n, :, ln] = float(step) * less * chain

    def merge(q, a, w):
        return (
            m.ends[0, :, q, :] + m.ends[2, :, q, :] * a,
            m.ends[1, :, q, :] + m.ends[2, :, q, :] * w + m.ends[3, :, q, :] * a,
        )

    a = w = jnp.zeros((nj, width), F32)
    for q in range(7, -1, -1):
        a, w = merge(q, a, w)
    m.end_out[0] = a
    m.end_out[1] = w
    across = remote(m.end_out, m.end_in, m.s_core.at[0], m.r_core.at[0], other)
    across.start()
    for run in run_f:
        run.forward()
    across.wait()
    a, w = jnp.where(c == 0, m.end_in[0], 0.0), jnp.where(c == 0, m.end_in[1], 0.0)
    for q in range(7, -1, -1):
        m.starts[0, :, q, :] = a
        m.starts[1, :, q, :] = w
        a, w = merge(q, a, w)

    for g in range(groups):
        ln = pl.ds(g * 128, 128)
        for j0 in range(0, nj, part):
            span = range(j0, j0 + part)
            decay = [wide(1.0 - m.damp[pl.ds(j, 1), ln]) for j in span]
            weight = [wide(m.damp[pl.ds(j, 1), ln] * m.eta[pl.ds(j, 1), ln]) for j in span]

            def scan(i, carry):
                a, w, sum_a, sum_w = carry
                at = pl.ds(step - 1 - i, 8, stride=step)
                v, k, u = m.grad_mix[g, at, :], m.keep_next[at, :], m.xn[g, at, :]
                held = [k * r for r in decay]
                w = tuple(k * p + r * q for p, r, q in zip(a, held, w))
                a = tuple(v + r * p for r, p in zip(held, a))
                sum_a = tuple(s + u * p for s, p in zip(sum_a, a))
                sum_w = tuple(s + u * p for s, p in zip(sum_w, w))
                base = v if j0 == 0 else m.back[g, at, :]
                m.back[g, at, :] = base + tree_sum([r * p for r, p in zip(weight, a)])
                return a, w, sum_a, sum_w

            first = (tuple(m.starts[0, j, :, ln] for j in span), tuple(m.starts[1, j, :, ln] for j in span))
            _, _, sum_a, sum_w = lax.fori_loop(
                0, step, scan, first + ((zero,) * part, (zero,) * part), unroll=4
            )
            for n, j in enumerate(span):
                at = pl.ds(j, 1)
                all_a = jnp.sum(sum_a[n], axis=0, keepdims=True)
                all_w = jnp.sum(sum_w[n], axis=0, keepdims=True)
                rate = m.damp[at, ln]
                m.small[at, ln] = m.eta[at, ln] * (all_a - rate * all_w)
                m.small[pl.ds(nj + j, 1), ln] = rate * all_a

    inv = m.inv_rows[...].T[:, 0:1]
    value = m.tok[...].astype(F32)
    for i in range(nb):
        for n in range(2):
            at = pl.ds(i * B + n * half, half)
            got = run_v[i].collect(n) + run_v[i].part(t, n)[...].astype(F32)
            m.grad_in[at, :] = got + jnp.concatenate([m.back[g, at, :] for g in range(groups)], axis=1)
        run_v[i].finish()
    grad_normed = m.grad_in[...]
    m.small[2 * nj :, :] = jnp.zeros((m.small.shape[0] - 2 * nj, width), F32)
    m.small[2 * nj : 2 * nj + 1, :] = jnp.sum(grad_normed * value * inv, axis=0, keepdims=True)
    m.small[2 * nj + 1 : 2 * nj + 2, :] = m.f_gain_grad[...]
    for copy in gains:
        copy.wait()
    m.small[2 * nj + 2 : 2 * nj + 3, :] = (
        m.all_q[0, 0:1] + m.all_q[1, 0:1] + m.all_q[2, 0:1] + m.all_q[3, 0:1]
    )
    scaled = grad_normed * m.gain[...]
    m.rows[t] = row_sums(scaled * value)
    sums = row_exchange(m.rows, m.s_rows, m.r_rows)
    pair = remote(m.small, m.small_core, m.s_small.at[0], m.r_small.at[0], other)
    for copy in sums + [pair]:
        copy.start()
    m.grad_in[...] = m.tok_grad[...] + inv * scaled
    pair.wait()
    m.small_all[z] = m.small[...] + m.small_core[...]
    wide_sums = [
        remote(
            m.small_all.at[z], m.small_all.at[z], m.s_small.at[k], m.r_small.at[k], spot(f=(z + k) % line_count)
        )
        for k in range(1, line_count)
    ]
    for copy in wide_sums:
        copy.start()
    for copy in sums:
        copy.wait()
    factor = m.inv_rows[...]
    factor = factor * factor * factor * (m.rows[0] + m.rows[1] + m.rows[2] + m.rows[3]) / D
    m.grad_in[...] -= value * factor.T[:, 0:1]
    for copy in wide_sums:
        copy.wait()
    total = m.small_all[0]
    for k in range(1, line_count):
        total = total + m.small_all[k]
    m.small[...] = total
    for i in range(nb):
        for n in range(2):
            at = pl.ds(i * B + n * half, half)
            got = run_f[i].collect(n) + run_f[i].part(t, n)[...].astype(F32)
            m.out[at, :] = (m.block[at, :] + got).astype(BF16)
        run_f[i].finish()
    for w in ("attended", "hidden", "update", "gate", "value", "shared"):
        line.end(at_w[w])


def rear(ident, line_count, ins):
    count, width = ins["tok"].shape
    groups, nj = width // 128, ins["damp"].shape[0]
    full = 4 * width
    nb = count // 256
    values = ins["value_grad"].shape[1]
    shapes = [(full, Z), (full, values), (full, values), (width, full), (values, full), (width, full)]
    turns, kinds, sizes, shapes, blocks = line_plan(shapes, KINDS[:-2], line_count)
    dma, s, v, k = pltpu.SemaphoreType.DMA, jax.ShapeDtypeStruct, pltpu.VMEM, len(REAR_WEIGHTS)
    tall = 2 * nj + 8
    n = 12 + 18 * nb
    lanes = v((groups, count, 128), F32)
    got = v((3, 2 * nb, 128, width), BF16)
    scratch = dict(
        part_v=v((4, count, width), BF16),
        got_v=got, got_t=got, got_f=got,
        part_s=v((count, Z), BF16),
        got_s=v((3, 2, 128, Z), BF16),
        low_s=v((256, Z), BF16),
        full_s=v((count, Z), BF16),
        grad_mix=lanes, back=lanes,
        rows=v((4, 8, count), F32),
        ends=v((4, nj, 8, width), F32),
        starts=v((2, nj, 8, width), F32),
        end_out=v((2, nj, width), F32),
        end_in=v((2, nj, width), F32),
        small_core=v((tall, width), F32),
        small_all=v((line_count, tall, width), F32),
        own_q=v((8, width), F32),
        all_q=v((4, 8, width), F32),
        upd_cols=v((width, full) if turns[REAR_WEIGHTS.index("update")] else (full, width), BF16),
        send=dma((n,)), recv=dma((n,)), s_rows=dma((3,)), r_rows=dma((3,)), s_core=dma((1,)), r_core=dma((1,)),
        s_upd=dma((4,)), r_upd=dma((3,)), s_small=dma((line_count,)), r_small=dma((line_count,)),
        s_q=dma((3,)), r_q=dma((3,)), s_in=dma((len(REAR_LOAD),)),
        c_send=dma((k, line_count)), c_recv=dma((k, line_count)),
        l_send=dma((k, line_count)), l_recv=dma((k, line_count)),
    )
    got = pl.pallas_call(
        functools.partial(rear_kernel, kinds, sizes, turns, line_count),
        out_shape=[s((count, width), F32), s((tall, width), F32), s((count, width), BF16)] + [s(b, F32) for b in blocks],
        in_specs=[ANY if name in REAR_LOAD else VMEM for name in REAR_IN],
        out_specs=[VMEM] * len(REAR_OUT),
        scratch_shapes=[scratch[name] for name in REAR_SCRATCH]
        + [v((line_count,) + b, BF16) for b in blocks]
        + [v(shape, BF16) for shape in shapes]
        + [v((line_count,) + b, BF16) for b in blocks]
        + [v(ins[name].shape, ins[name].dtype) for name in REAR_LOAD],
        compiler_params=pltpu.CompilerParams(collective_id=ident, has_side_effects=True, vmem_limit_bytes=62 * 2**20),
        name="rear",
    )(*[ins[name] for name in REAR_IN])
    grads = [g.T if turn else g for turn, g in zip(turns, got[3:])]
    return got[0], got[1], got[2], grads


def on_device(
    line_count,
    layer_input, segment_ids, cotangent, norm_gain, ema_damping, ema_eta, query_gain, key_gain,
    ffn_gain, *weights,
):
    tok, cot = layer_input[0], cotangent[0]
    segment = segment_ids[0]
    row_count = tok.shape[0]
    core = lax.axis_index("ctx")
    offset = core * row_count
    all_ids = lax.all_gather(segment, "ctx", axis=0, tiled=True)
    same = jnp.concatenate(
        [jnp.zeros((1,), F32), (all_ids[1:] == all_ids[:-1]).astype(F32), jnp.zeros((1,), F32)]
    )
    keep = lax.dynamic_slice_in_dim(same, offset, row_count, 0)
    keep_next = lax.dynamic_slice_in_dim(same, offset + 1, row_count, 0)
    keep_wide = jnp.broadcast_to(keep[:, None], (row_count, 128))
    next_wide = jnp.broadcast_to(keep_next[:, None], (row_count, 128))
    prev_ids = jnp.where(core > 0, all_ids[:row_count], -1)
    ids_row = jnp.broadcast_to(jnp.concatenate([prev_ids, segment]).astype(F32)[None], (8, 2 * row_count))
    a = front(
        1, line_count, tok, keep_wide, norm_gain, ema_damping, ema_eta, query_gain, key_gain, ids_row, cot, weights
    )
    ins = {n: getattr(a, n) for n in MID_LOAD if n != "w_upd"}
    ins.update(w_upd=a.rows_update, tok=tok, cot=cot, f_gain=ffn_gain[None], ids_row=ids_row)
    m = middle(2, line_count, ins)
    ins = {n: getattr(m if n in MID_OUT else a, n) for n in REAR_IN if n in MID_OUT or n in A_OUT}
    ins.update(
        tok=tok, keep_next=next_wide, gain=norm_gain[None], damp=ema_damping, eta=ema_eta,
        q_gain=query_gain[None], k_gain=key_gain[None],
    )
    grad_in, small, out, grads = rear(3, line_count, ins)
    n = ema_damping.shape[0]
    return (
        out[None], grad_in[None], small[2 * n], small[:n], small[n : 2 * n],
        small[2 * n + 2, :Z], small[2 * n + 2, Z:], small[2 * n + 1], *grads, m.d_up, m.d_down,
    )


def solution(mesh):
    token = P("fsdp", "ctx", "tp")
    row, col = P(("fsdp", "ctx"), "tp"), P("tp", ("fsdp", "ctx"))
    shared = P(("fsdp", "ctx"), None)
    weights = (shared, row, row, col, col, col, row, col)
    small = P(None, "tp")
    return jax.shard_map(
        functools.partial(on_device, mesh.shape["fsdp"]),
        mesh=mesh,
        in_specs=(token, P("fsdp", "ctx"), token, P("tp"), small, small, P(), P(), P("tp")) + weights,
        out_specs=(token, token, P("tp"), small, small, P(), P(), P("tp")) + weights,
        check_vma=False,
    )
```

```python
import functools
import inspect
import math
import types

import jax
import jax.numpy as jnp
from jax import lax
from jax.experimental import pallas as pl
from jax.experimental.pallas import tpu as pltpu
from jax.sharding import PartitionSpec as P

D = 1024
Z = 128
EPSILON = 1e-06
MESH = pl.DeviceIdType.MESH
F32 = jnp.float32
BF16 = jnp.bfloat16
VMEM = pl.BlockSpec(memory_space=pltpu.VMEM)
ANY = pl.BlockSpec(memory_space=pl.ANY)
HIGH = lax.Precision.HIGHEST


def named(signature):
    return list(inspect.signature(signature).parameters)


def spot(f=None, c=None, t=None):
    return (
        lax.axis_index("fsdp") if f is None else f,
        lax.axis_index("ctx") if c is None else c,
        lax.axis_index("tp") if t is None else t,
    )


def greet(devices):
    barrier = pltpu.get_barrier_semaphore()
    for device in devices:
        pl.semaphore_signal(barrier, inc=1, device_id=device, device_id_type=MESH)
    pl.semaphore_wait(barrier, len(devices))


def tp_peers():
    t = lax.axis_index("tp")
    return t, t + 1 - 2 * (t % 2), (t + 2) % 4, 3 - t


def remote(src, dst, send, recv, device):
    return pltpu.make_async_remote_copy(
        src_ref=src, dst_ref=dst, send_sem=send, recv_sem=recv, device_id=device, device_id_type=MESH
    )


class Gather:
    def __init__(self, count, source, place, send, recv, base=0):
        self.count, self.half = count, count // 2
        self.source, self.place, self.send, self.recv, self.base = source, place, send, recv, base
        self.t, self.x, self.y, _ = tp_peers()

    def copy(self, src, owner, i, way, to):
        n = self.base + way * self.count + i
        return remote(src, self.place(owner, i), self.send.at[n], self.recv.at[n], spot(t=to))

    def first(self, i, way):
        return self.copy(self.source(i), self.t, i, way, self.x if way == 0 else self.y)

    def start(self):
        for k in range(self.half):
            self.first(k, 0).start()
            self.first(k + self.half, 1).start()
        for k in range(self.half):
            self.first(k + self.half, 0).start()
            self.first(k, 1).start()

    def onward(self, i):
        if i < self.half:
            return self.copy(self.place(self.x, i), self.x, i, 2, self.y)
        return self.copy(self.place(self.y, i), self.y, i, 2, self.x)

    def forward(self):
        for k in range(self.half):
            self.first(k, 0).wait_recv()
            self.onward(k).start()
            self.first(k + self.half, 1).wait_recv()
            self.onward(k + self.half).start()

    def finish(self):
        for k in range(self.half):
            self.first(k + self.half, 0).wait_recv()
            self.first(k, 1).wait_recv()
        for i in range(self.count):
            self.onward(i).wait()
            self.first(i, 0).wait_send()
            self.first(i, 1).wait_send()


class Scatter:
    def __init__(self, count, part, first_diag, first_own, second, send, recv, base=0):
        self.count, self.part = count, part
        self.diag, self.own, self.second = first_diag, first_own, second
        self.send, self.recv, self.base = send, recv, base
        self.t, self.x, self.y, self.d = tp_peers()

    def ways(self, i):
        return (self.x, self.y) if i % 2 == 0 else (self.y, self.x)

    def copy(self, i, kind):
        near, far = self.ways(i)
        n = self.base + kind * self.count + i
        if kind == 0:
            src, dst, to = self.part(self.d, i), self.diag(i), near
        elif kind == 1:
            src, dst, to = self.part(near, i), self.own(i), near
        else:
            src, dst, to = self.part(far, i), self.second(i), far
        return remote(src, dst, self.send.at[n], self.recv.at[n], spot(t=to))

    def start(self):
        for i in range(self.count):
            self.copy(i, 0).start()
        for i in range(self.count):
            self.copy(i, 1).start()

    def forward(self):
        for i in range(self.count):
            self.copy(i, 0).wait_recv()
            mine = self.part(self.ways(i)[1], i)
            mine[...] = (mine[...].astype(F32) + self.diag(i)[...].astype(F32)).astype(BF16)
            self.copy(i, 2).start()

    def collect(self, i):
        self.copy(i, 1).wait_recv()
        self.copy(i, 2).wait_recv()
        return self.own(i)[...].astype(F32) + self.second(i)[...].astype(F32)

    def finish(self):
        for i in range(self.count):
            for kind in range(3):
                self.copy(i, kind).wait_send()


def shard_at(ref, kind, index, size):
    if kind == "row":
        return ref.at[pl.ds(pl.multiple_of(index * size, size), size)]
    return ref.at[:, pl.ds(pl.multiple_of(index * size, size), size)]


def turned(kind, size):
    return kind == "col" and size % 128 != 0


def row_exchange(rows, send, recv):
    t, x, y, d = tp_peers()
    return [
        remote(rows.at[t], rows.at[t], send.at[k], recv.at[k], spot(t=p))
        for k, p in enumerate((x, y, d))
    ]


class Named:
    def __init__(self, names, refs):
        for name, ref in zip(names, refs, strict=True):
            setattr(self, name, ref)


class Transfer:
    def __init__(self, copy):
        self.copy, self.waited = copy, False

    def start(self):
        self.copy.start()

    def wait(self):
        if not self.waited:
            self.waited = True
            self.copy.wait()


def need(*transfers):
    for transfer in transfers:
        transfer.wait()


def dot(left, right):
    return jnp.dot(left, right, preferred_element_type=F32)


def dot_t(left, right):
    return lax.dot_general(left, right, (((1,), (1,)), ((), ())), preferred_element_type=F32)


def t_dot(left, right):
    return lax.dot_general(left, right, (((0,), (0,)), ((), ())), preferred_element_type=F32)


def sigmoid(v):
    return 1.0 / (1.0 + jnp.exp(-v))


def d_silu(v, s):
    return s * (1.0 + v * (1.0 - s))


def as_rows(column):
    return jnp.broadcast_to(column, (column.shape[0], 128)).T[0:8]


def as_column(rows):
    return rows.T[:, 0:1]


def at_block(i, size):
    return pl.ds(i * size if isinstance(i, int) else pl.multiple_of(i * size, size), size)


def wide(row):
    return jnp.broadcast_to(row, (8, 128))


def tree_sum(terms):
    while len(terms) > 1:
        terms = [a + b for a, b in zip(terms[::2], terms[1::2])]
    return terms[0]


def power(base, exponent):
    result, square = None, base
    while exponent:
        if exponent & 1:
            result = square if result is None else result * square
        exponent >>= 1
        if exponent:
            square = square * square
    return result


def row_sums(values):
    return lax.dot_general(
        jnp.ones((8, values.shape[1]), F32), values, (((1,), (1,)), ((), ())),
        precision=HIGH, preferred_element_type=F32,
    )


class Line:
    def __init__(self, kinds, sizes, count, sources, places, sems):
        self.kinds, self.sizes, self.count = kinds, sizes, count
        self.sources, self.places = sources, places
        self.here, self.send_up, self.send_down, self.send_core, self.recv, self.recv_core = sems
        self.z, self.c = lax.axis_index("fsdp"), lax.axis_index("ctx")
        self.other = spot(c=1 - self.c)
        self.up = spot(f=(self.z + 1) % count)
        self.down = spot(f=(self.z + count - 1) % count)
        self.next = {}

    def slot(self, w, owner, core):
        return shard_at(self.places[w], self.kinds[w], owner * 2 + core, self.sizes[w])

    def to_core(self, w, owner, src):
        return remote(
            src, self.slot(w, owner, self.c), self.send_core.at[w, owner], self.recv_core.at[w, owner], self.other
        )

    def to_up(self, w, owner, src):
        return remote(src, self.slot(w, owner, self.c), self.send_up.at[w, owner], self.recv.at[w, owner], self.up)

    def to_down(self, w, owner, src):
        return remote(src, self.slot(w, owner, self.c), self.send_down.at[w, owner], self.recv.at[w, owner], self.down)

    def keep(self, w):
        return pltpu.make_async_copy(self.sources[w], self.slot(w, self.z, self.c), self.here.at[w])

    def own(self, group):
        for w in group:

            @pl.when(self.z + 1 < self.count)
            def _():
                self.to_up(w, self.z, self.sources[w]).start()

            @pl.when(self.z > 0)
            def _():
                self.to_down(w, self.z, self.sources[w]).start()

            self.to_core(w, self.z, self.sources[w]).start()
            self.keep(w).start()
            self.next[w] = 1

    def hand_on(self, w, step):
        low, high = self.z - step, self.z + step

        @pl.when(low >= 0)
        def _():
            got = self.slot(w, low, self.c)
            self.to_up(w, low, got).wait_recv()

            @pl.when(self.z + 1 < self.count)
            def _():
                self.to_up(w, low, got).start()

            self.to_core(w, low, got).start()

        @pl.when(high < self.count)
        def _():
            got = self.slot(w, high, self.c)
            self.to_down(w, high, got).wait_recv()

            @pl.when(self.z > 0)
            def _():
                self.to_down(w, high, got).start()

            self.to_core(w, high, got).start()

    def pump(self, group):
        for w in group:
            if self.next[w] < self.count:
                self.hand_on(w, self.next[w])
                self.next[w] += 1

    def done(self, group):
        for w in group:
            if self.next[w] < self.count:

                @pl.loop(self.next[w], self.count)
                def _(step):
                    self.hand_on(w, step)

            @pl.loop(0, self.count)
            def _(owner):
                got = self.slot(w, owner, self.c)
                self.to_core(w, owner, got).wait()

                @pl.when((owner <= self.z) & (self.z + 1 < self.count))
                def _():
                    self.to_up(w, owner, got).wait_send()

                @pl.when((owner >= self.z) & (self.z > 0))
                def _():
                    self.to_down(w, owner, got).wait_send()

            self.keep(w).wait()


class Fetch:
    def __init__(self, kind, size, count, source, place, sems):
        self.kind, self.size, self.count, self.source, self.place = kind, size, count, source, place
        self.send, self.recv, self.send_core, self.recv_core = sems
        self.z, self.c = lax.axis_index("fsdp"), lax.axis_index("ctx")
        self.other = spot(c=1 - self.c)

    def slot(self, owner, core):
        return shard_at(self.place, self.kind, owner * 2 + core, self.size)

    def along(self, k):
        to = spot(f=(self.z + k) % self.count)
        return remote(self.source, self.slot(self.z, self.c), self.send.at[k], self.recv.at[self.z], to)

    def across(self, owner):
        got = self.slot(owner, self.c)
        return remote(got, got, self.send_core.at[owner], self.recv_core.at[owner], self.other)

    def start(self):
        @pl.loop(1, self.count)
        def _(k):
            self.along(k).start()

        keep = pltpu.make_async_copy(self.source, self.slot(self.z, self.c), self.send.at[0])
        keep.start()
        keep.wait()
        self.across(self.z).start()

    def hand_on(self):
        @pl.loop(1, self.count)
        def _(k):
            owner = (self.z + k) % self.count
            got = self.slot(owner, self.c)
            remote(got, got, self.send.at[k], self.recv.at[owner], self.other).wait_recv()
            self.across(owner).start()

        @pl.loop(0, self.count)
        def _(owner):
            self.across(owner).wait()

        @pl.loop(1, self.count)
        def _(k):
            self.along(k).wait_send()


WEIGHTS = named(lambda shared, value, gate, hidden, attended, update, up, down: None)
KINDS = ("row", "row", "row", "col", "col", "col", "row", "col")
FRONT_WEIGHTS = WEIGHTS[:-1]
A_IN = named(lambda tok, keep, gain, damp, eta, q_gain, k_gain, ids_row, cot: None) + ["s_" + w for w in FRONT_WEIGHTS]
A_OUT = named(
    lambda rows_update, normed4, mixed4, mix_pre, xn, inv_rows, s_pre, v_pre, g_pre, keys, vals,
    queries, log_sum, attended, gated, hid_pre, upd_pre, cot4: None
) + ["w_" + w for w in FRONT_WEIGHTS if w != "update"]
A_HBM = named(
    lambda rows_update, normed4, mixed4, mix_pre, xn, v_pre, g_pre, keys, vals, attended, gated,
    hid_pre, upd_pre, cot4: None
) + [
    "w_" + w for w in FRONT_WEIGHTS if w != "update"
]
A_SCRATCH = named(
    lambda low_n, low_m, rows, ends, starts, end_out, end_in, part_h, got_h, w_update, send, recv,
    s_rows, r_rows, s_core, r_core, s_upd, r_upd, s_kv, r_kv, s_out, z_here, z_up, z_down, z_core,
    z_recv, z_recv_core: None
)


def front_kernel(kinds, sizes, turns, line_count, *refs):
    aside = [w for w, turn in zip(FRONT_WEIGHTS, turns) if turn]
    names = A_IN + A_OUT + A_SCRATCH + ["v_" + n for n in A_HBM] + ["t_" + w for w in aside]
    m = Named(names, refs)
    outs = {}
    for k, n in enumerate(A_HBM):
        outs[n] = pltpu.make_async_copy(getattr(m, "v_" + n), getattr(m, n), m.s_out.at[k])
        setattr(m, n, getattr(m, "v_" + n))
    out = types.SimpleNamespace(**outs)
    t, x, y, d = tp_peers()
    c = lax.axis_index("ctx")
    other = spot(c=1 - c)
    groups, count = m.xn.shape[0], m.xn.shape[1]
    step, nj, width = count // 8, m.damp.shape[0], m.damp.shape[1]
    B = 256
    half, nb, span = B // 2, count // B, count + B
    scale = 1.0 / math.sqrt(Z)

    def lanes(o):
        return pl.ds(pl.multiple_of(o * width, width), width)

    line = Line(
        kinds, sizes, line_count, [getattr(m, "s_" + w) for w in FRONT_WEIGHTS],
        [getattr(m, ("t_" if w in aside else "w_") + w) for w in FRONT_WEIGHTS],
        (m.z_here, m.z_up, m.z_down, m.z_core, m.z_recv, m.z_recv_core),
    )
    first_w, second_w, third_w = (0, 1, 2), (3, 4, 5), (6,)

    m.end_in[...] = jnp.zeros_like(m.end_in)
    value = m.tok[...].astype(F32)
    m.rows[t] = row_sums(value * value)
    greet([spot(t=x), spot(t=y), spot(t=d), other, line.up, line.down])
    sums = [
        remote(m.rows.at[t], m.rows.at[t], m.s_rows.at[k], m.r_rows.at[k], spot(t=p))
        for k, p in enumerate((x, y, d))
    ]
    for copy in sums:
        copy.start()
    line.own(first_w)
    line.own(second_w)
    for copy in sums:
        copy.wait()
    inv = lax.rsqrt((m.rows[0] + m.rows[1] + m.rows[2] + m.rows[3]) / D + EPSILON)
    m.inv_rows[...] = inv
    normed = m.tok[...].astype(F32) * inv.T[:, 0:1] * m.gain[...]
    m.low_n[...] = normed.astype(BF16)
    for g in range(groups):
        m.xn[g] = normed[:, g * 128 : (g + 1) * 128]
    out.xn.start()
    chunks = 8
    size = count // chunks

    def whole_run(low, place, base):
        return Gather(
            chunks,
            lambda i: low.at[pl.ds(i * size, size)],
            lambda o, i: place.at[pl.ds(i * size, size), lanes(o)],
            m.send, m.recv, base,
        )

    norm_run = whole_run(m.low_n, m.normed4, 0)
    cot_run = whole_run(m.cot, m.cot4, 24)
    mix_run = whole_run(m.low_m, m.mixed4, 48)
    norm_run.start()

    for g in range(groups):
        ln = pl.ds(g * 128, 128)
        decay = [wide(1.0 - m.damp[pl.ds(j, 1), ln]) for j in range(nj)]

        def scan(s, carry):
            states, chain = carry
            at = pl.ds(s, 8, stride=step)
            v, k = m.xn[g, at, :], m.keep[at, :]
            return tuple(v + (k * r) * a for r, a in zip(decay, states)), chain * k

        zero = jnp.zeros((8, 128), F32)
        states, chain = lax.fori_loop(0, step, scan, ((zero,) * nj, zero + 1.0), unroll=4)
        for j in range(nj):
            m.ends[0, j, :, ln] = states[j]
            m.ends[1, j, :, ln] = power(decay[j], step) * chain

    last = jnp.zeros((nj, width), F32)
    for q in range(8):
        last = m.ends[0, :, q, :] + m.ends[1, :, q, :] * last
    m.end_out[...] = last
    across = remote(m.end_out, m.end_in, m.s_core.at[0], m.r_core.at[0], other)
    across.start()
    line.pump(first_w)
    across.wait()
    last = jnp.where(c == 0, 0.0, m.end_in[...])
    for q in range(8):
        m.starts[:, q, :] = last
        last = m.ends[0, :, q, :] + m.ends[1, :, q, :] * last

    for g in range(groups):
        ln = pl.ds(g * 128, 128)
        decay = [wide(1.0 - m.damp[pl.ds(j, 1), ln]) for j in range(nj)]
        weight = [wide(m.damp[pl.ds(j, 1), ln] * m.eta[pl.ds(j, 1), ln]) for j in range(nj)]

        def scan(s, states):
            at = pl.ds(s, 8, stride=step)
            v, k = m.xn[g, at, :], m.keep[at, :]
            states = tuple(v + (k * r) * a for r, a in zip(decay, states))
            m.mix_pre[g, at, :] = v + tree_sum([w * a for w, a in zip(weight, states)])
            return states

        lax.fori_loop(0, step, scan, tuple(m.starts[j, :, ln] for j in range(nj)), unroll=4)
        pre = m.mix_pre[g]
        m.low_m[:, ln] = (pre * sigmoid(pre)).astype(BF16)
    norm_run.forward()
    mix_run.start()
    out.mix_pre.start()
    line.pump(first_w)
    line.pump(second_w)
    line.own(third_w)
    for o in range(4):

        @pl.when(t == o)
        def _():
            m.normed4[:, o * width : (o + 1) * width] = m.low_n[...]
            m.mixed4[:, o * width : (o + 1) * width] = m.low_m[...]
            m.cot4[:, o * width : (o + 1) * width] = m.cot[...]

    mix_run.forward()
    line.pump(first_w)
    line.pump(second_w)
    norm_run.finish()
    out.normed4.start()
    line.done(first_w)
    for copy in (out.w_shared, out.w_value, out.w_gate):
        copy.start()

    def rows(i):
        return at_block(i, B)

    def mine(i):
        return pl.ds(pl.multiple_of(count + i * B, B), B)

    def window(i):
        return pl.ds(pl.multiple_of(i * B, B), span)

    def kv_run(i):
        return [
            remote(m.keys.at[mine(i)], m.keys.at[rows(i)], m.s_kv.at[2 * i], m.r_kv.at[2 * i], other),
            remote(m.vals.at[mine(i)], m.vals.at[rows(i)], m.s_kv.at[2 * i + 1], m.r_kv.at[2 * i + 1], other),
        ]

    @pl.loop(0, nb)
    def _(i):
        value = dot(m.normed4[rows(i), :], m.w_value[...])
        m.v_pre[rows(i), :] = value.astype(BF16)
        m.vals[mine(i), :] = (value * sigmoid(value)).astype(BF16)
        kv_run(i)[1].start()

    out.v_pre.start()
    mix_run.finish()
    out.mixed4.start()
    cot_run.start()

    @pl.loop(0, nb)
    def _(i):
        pre = dot(m.mixed4[rows(i), :], m.w_shared[...])
        m.s_pre[rows(i), :] = pre
        shared = pre * sigmoid(pre)
        m.queries[rows(i), :] = (shared * m.q_gain[...]).astype(BF16)
        m.keys[mine(i), :] = (shared * m.k_gain[...]).astype(BF16)
        kv_run(i)[0].start()

    @pl.loop(0, nb)
    def _(i):
        m.g_pre[rows(i), :] = dot(m.mixed4[rows(i), :], m.w_gate[...])

    out.g_pre.start()
    line.pump(second_w)
    line.pump(third_w)
    for i in range(nb):
        for copy in kv_run(i):
            copy.wait()
    out.keys.start()
    out.vals.start()
    line.done(second_w)
    for w in aside:
        if w != "up":
            getattr(m, "w_" + w)[...] = getattr(m, "t_" + w)[...].astype(F32).T.astype(BF16)
    for copy in (out.w_hidden, out.w_attended):
        copy.start()
    upd = [
        remote(m.w_update.at[:, lanes(p)], m.rows_update.at[pl.ds(pl.multiple_of(t * width, width), width)],
               m.s_upd.at[n], m.r_upd.at[n], spot(t=p))
        for n, p in enumerate((x, y, d))
    ]
    for copy in upd:
        copy.start()
    for o in range(4):

        @pl.when(t == o)
        def _():
            m.rows_update[o * width : (o + 1) * width, :] = m.w_update[:, o * width : (o + 1) * width]

    def run_h(i):
        return Scatter(
            2,
            lambda o, n: m.part_h.at[o, pl.ds(pl.multiple_of(i * B + n * half, half), half)],
            lambda n: m.got_h.at[0, i * 2 + n],
            lambda n: m.got_h.at[1, i * 2 + n],
            lambda n: m.got_h.at[2, i * 2 + n],
            m.send, m.recv, 72 + i * 6,
        )

    def attend(i):
        raw = dot_t(m.queries[rows(i), :], m.keys[window(i), :]) * scale
        same = as_column(m.ids_row[:, mine(i)]) == m.ids_row[0:1, window(i)]
        place = lax.broadcasted_iota(jnp.int32, raw.shape, 1) - lax.broadcasted_iota(jnp.int32, raw.shape, 0)
        s = jnp.where(same & (place <= count), raw, -1e30)
        peak = jnp.max(s, axis=1, keepdims=True)
        e = jnp.exp(s - peak)
        total = jnp.sum(e, axis=1, keepdims=True)
        m.log_sum[rows(i), :] = jnp.broadcast_to(peak + jnp.log(total), (B, 128))
        attended = dot((e * (1.0 / total)).astype(BF16), m.vals[window(i), :])
        m.attended[rows(i), :] = attended.astype(BF16)
        gate = m.g_pre[rows(i), :]
        gated = (gate * sigmoid(gate) * attended).astype(BF16)
        m.gated[rows(i), :] = gated
        part = dot(m.mixed4[rows(i), lanes(t)], m.w_hidden[...]) + dot(gated, m.w_attended[...])
        part = part.astype(BF16)
        for o in range(4):
            m.part_h[o, rows(i), :] = part[:, o * width : (o + 1) * width]
        run_h(i).start()

    def collect(i):
        run = run_h(i)
        for n in range(2):
            m.hid_pre[pl.ds(i * B + n * half, half), :] = run.collect(n) + run.part(t, n)[...].astype(F32)
        run.finish()

    def attend_some(start, stop):
        @pl.loop(start, stop)
        def _(i):
            attend(i)

            @pl.when(i > 0)
            def _():
                run_h(i - 1).forward()

    attend_some(0, nb // 2)
    line.pump(third_w)
    cot_run.forward()
    attend_some(nb // 2, nb)
    line.pump(third_w)
    out.attended.start()
    out.gated.start()
    for copy in upd:
        copy.wait()

    @pl.loop(0, nb)
    def _(i):
        m.upd_pre[rows(i), :] = dot(m.mixed4[rows(i), :], m.rows_update[...])

    run_h(nb - 1).forward()
    out.upd_pre.start()
    out.rows_update.start()
    line.done(third_w)
    out.w_up.start()
    for i in range(nb):
        collect(i)
    out.hid_pre.start()
    cot_run.finish()
    out.cot4.start()
    for copy in outs.values():
        copy.wait()


def front(ident, line_count, tok, keep, gain, damp, eta, q_gain, k_gain, ids_row, cot, shards):
    count, width = tok.shape
    groups, nj = width // 128, damp.shape[0]
    nb = count // 256
    turns = [turned(k, s.shape[1]) for k, s in zip(KINDS, shards)]
    shards = [s.T if turn else s for turn, s in zip(turns, shards)]
    kinds = ["row" if turn else k for turn, k in zip(turns, KINDS)]
    sizes = [s.shape[0] if k == "row" else s.shape[1] for k, s in zip(kinds, shards)]
    full = 4 * width
    values = shards[1].shape[1]
    s = jax.ShapeDtypeStruct
    outs = dict(
        rows_update=s((full, width), BF16),
        normed4=s((count, full), BF16),
        mixed4=s((count, full), BF16),
        mix_pre=s((groups, count, 128), F32),
        xn=s((groups, count, 128), F32),
        inv_rows=s((8, count), F32),
        s_pre=s((count, Z), F32),
        v_pre=s((count, values), BF16),
        g_pre=s((count, values), F32),
        keys=s((2 * count, Z), BF16),
        vals=s((2 * count, values), BF16),
        queries=s((count, Z), BF16),
        log_sum=s((count, 128), F32),
        attended=s((count, values), BF16),
        gated=s((count, values), BF16),
        hid_pre=s((count, width), F32),
        upd_pre=s((count, width), F32),
        cot4=s((count, full), BF16),
    )
    aside = []
    for name, kind, size, shard in zip(FRONT_WEIGHTS, kinds, sizes, shards):
        shape = (2 * line_count * size, shard.shape[1]) if kind == "row" else (shard.shape[0], 2 * line_count * size)
        if kind == "row" and turns[FRONT_WEIGHTS.index(name)]:
            aside.append(pltpu.VMEM(shape, shard.dtype))
            shape = shape[::-1]
        outs["w_" + name] = s(shape, shard.dtype)
    v, dma, k = pltpu.VMEM, pltpu.SemaphoreType.DMA, len(FRONT_WEIGHTS)
    n = 72 + 6 * nb
    scratch = dict(
        low_n=v((count, width), BF16),
        low_m=v((count, width), BF16),
        rows=v((4, 8, count), F32),
        ends=v((2, nj, 8, width), F32),
        starts=v((nj, 8, width), F32),
        end_out=v((nj, width), F32),
        end_in=v((nj, width), F32),
        part_h=v((4, count, width), BF16),
        got_h=v((3, 2 * nb, 128, width), BF16),
        w_update=v(outs["w_update"].shape, BF16),
        send=dma((n,)), recv=dma((n,)), s_rows=dma((3,)), r_rows=dma((3,)), s_core=dma((1,)), r_core=dma((1,)),
        s_upd=dma((3,)), r_upd=dma((3,)), s_kv=dma((2 * nb,)), r_kv=dma((2 * nb,)), s_out=dma((len(A_HBM),)),
        z_here=dma((k,)), z_up=dma((k, line_count)), z_down=dma((k, line_count)), z_core=dma((k, line_count)),
        z_recv=dma((k, line_count)), z_recv_core=dma((k, line_count)),
    )
    got = pl.pallas_call(
        functools.partial(front_kernel, kinds, sizes, turns, line_count),
        out_shape=[outs[n] for n in A_OUT],
        in_specs=[VMEM] * len(A_IN),
        out_specs=[ANY if n in A_HBM else VMEM for n in A_OUT],
        scratch_shapes=[scratch[n] for n in A_SCRATCH] + [v(outs[n].shape, outs[n].dtype) for n in A_HBM] + aside,
        compiler_params=pltpu.CompilerParams(collective_id=ident, has_side_effects=True, vmem_limit_bytes=60 * 2**20),
        name="front",
    )(tok, keep, gain[None], damp, eta, q_gain[None], k_gain[None], ids_row, cot, *shards)
    return Named(A_OUT, got)


class LineSum:
    def __init__(self, kinds, sizes, count, sources, pair, line, outs, sems):
        self.kinds, self.sizes, self.count = kinds, sizes, count
        self.sources, self.pair, self.line, self.outs = sources, pair, line, outs
        self.send_core, self.recv_core, self.send, self.recv = sems
        self.z, self.c = lax.axis_index("fsdp"), lax.axis_index("ctx")
        self.other = spot(c=1 - self.c)

    def block(self, w, owner, core):
        return shard_at(self.sources[w], self.kinds[w], owner * 2 + core, self.sizes[w])

    def across(self, w, owner):
        return remote(
            self.block(w, owner, 1 - self.c), self.pair[w].at[owner],
            self.send_core.at[w, owner], self.recv_core.at[w, owner], self.other,
        )

    def along(self, w, k):
        owner = (self.z + k) % self.count
        return remote(
            self.pair[w].at[owner], self.line[w].at[self.z], self.send.at[w, k], self.recv.at[w, self.z],
            spot(f=owner),
        )

    def start(self, w):
        @pl.loop(1, self.count + 1)
        def _(k):
            self.across(w, (self.z + k) % self.count).start()

    def plus(self, w, owner):
        return self.pair[w][owner].astype(F32) + self.block(w, owner, self.c)[...].astype(F32)

    def send_on(self, w):
        @pl.loop(1, self.count)
        def _(k):
            owner = (self.z + k) % self.count
            self.across(w, owner).wait_recv()
            self.pair[w][owner] = self.plus(w, owner).astype(BF16)
            self.along(w, k).start()

    def end(self, w):
        self.across(w, self.z).wait_recv()
        self.outs[w][...] = self.plus(w, self.z)

        @pl.loop(1, self.count)
        def _(k):
            source = (self.z + k) % self.count
            got = self.line[w].at[source]
            remote(got, got, self.send.at[w, k], self.recv.at[w, source], self.other).wait_recv()
            self.outs[w][...] += got[...].astype(F32)
            self.along(w, k).wait_send()

        @pl.loop(0, self.count)
        def _(owner):
            self.across(w, owner).wait_send()


def line_plan(shapes, kinds, count):
    turns = [turned(k, s[1] // (2 * count)) for k, s in zip(kinds, shapes)]
    shapes = [s[::-1] if turn else s for turn, s in zip(turns, shapes)]
    kinds = ["row" if turn else k for turn, k in zip(turns, kinds)]
    sizes = [s[0 if k == "row" else 1] // (2 * count) for k, s in zip(kinds, shapes)]
    blocks = [(n, s[1]) if k == "row" else (s[0], n) for k, n, s in zip(kinds, sizes, shapes)]
    return turns, kinds, sizes, shapes, blocks


def line_peers(count):
    z = lax.axis_index("fsdp")
    return [spot(f=(z + k) % count) for k in range(1, count)]


MID_LOAD = named(
    lambda hid_pre, upd_pre, w_up, cot4, w_attended, g_pre, attended, w_gate, w_upd, w_hidden,
    queries, keys, vals, log_sum, v_pre: None
)
MID_IN = MID_LOAD + named(lambda tok, cot, f_gain, ids_row, s_down: None)
MID_STORE = named(
    lambda block, part_f, part_t, tok_grad, mix_grad, value_grad, hid4, upd_grad, gate_grad, g_up:
    None
)
MID_OUT = MID_STORE + named(lambda f_gain_grad, q_grad, k_grad, d_down: None)
MID_SCRATCH = named(
    lambda up_rows, up_grads, ffn4, att_grad, k_all, v_all, part_g, got_g, low, rows_a, rows_b,
    k_send, v_send, k_got, v_got, w_down, p_down, l_down, f_send, f_recv, f_core, f_recv_core, send,
    recv, s_rows, r_rows, s_gr, r_gr, s_in, s_out, c_send, c_recv, l_send, l_recv: None
)


def mid_kernel(kind, size, turn, line_count, *refs):
    m = Named(
        MID_IN + MID_OUT + MID_SCRATCH + ["i_" + n for n in MID_LOAD] + ["o_" + n for n in MID_STORE], refs
    )
    loads, stores = {}, {}
    for k, n in enumerate(MID_LOAD):
        loads[n] = Transfer(pltpu.make_async_copy(getattr(m, n), getattr(m, "i_" + n), m.s_in.at[k]))
        setattr(m, n, getattr(m, "i_" + n))
        loads[n].start()
    for k, n in enumerate(MID_STORE):
        stores[n] = pltpu.make_async_copy(getattr(m, "o_" + n), getattr(m, n), m.s_out.at[k])
        setattr(m, n, getattr(m, "o_" + n))
    load, store = types.SimpleNamespace(**loads), types.SimpleNamespace(**stores)
    t, x, y, d = tp_peers()
    other = spot(c=1 - lax.axis_index("ctx"))
    count, width = m.tok.shape
    hidden = m.w_up.shape[1]
    B = 256
    half, nb, span = B // 2, count // B, count + B
    scale = 1.0 / math.sqrt(Z)

    def rows(i):
        return at_block(i, B)

    def mine(i):
        return pl.ds(count + i * B, B)

    def window(i):
        return pl.ds(i * B, span)

    def lanes(o):
        return pl.ds(pl.multiple_of(o * width, width), width)

    greet([spot(t=x), spot(t=y), spot(t=d), other] + line_peers(line_count))
    fetch = Fetch(
        kind, size, line_count, m.s_down, m.w_down, (m.f_send, m.f_recv, m.f_core, m.f_recv_core)
    )
    fetch.start()
    m.f_gain_grad[...] = jnp.zeros_like(m.f_gain_grad)

    def gather_run(kind, i, low, place):
        return Gather(
            2,
            lambda n: low.at[pl.ds(i * B + n * half, half)],
            lambda o, n: place.at[pl.ds(i * B + n * half, half), lanes(o)],
            m.send, m.recv, (kind * nb + i) * 6,
        )

    def scatter_run(kind, i, part, got):
        return Scatter(
            2,
            lambda o, n: part.at[o, pl.ds(i * B + n * half, half)],
            lambda n: got.at[0, i * 2 + n],
            lambda n: got.at[1, i * 2 + n],
            lambda n: got.at[2, i * 2 + n],
            m.send, m.recv, (kind * nb + i) * 6,
        )

    run_p = [gather_run(0, i, m.low, m.ffn4) for i in range(nb)]
    run_gh = [gather_run(1, i, m.low, m.hid4) for i in range(nb)]
    run_g = [scatter_run(2, i, m.part_g, m.got_g) for i in range(nb)]
    line = LineSum(
        [kind], [size], line_count, [m.w_down], [m.p_down], [m.l_down], [m.d_down],
        (m.c_send, m.c_recv, m.l_send, m.l_recv),
    )

    def row_run(kind, i, buf):
        return [
            remote(
                buf.at[t, :, rows(i)], buf.at[t, :, rows(i)],
                m.s_rows.at[(kind * nb + i) * 3 + n], m.r_rows.at[(kind * nb + i) * 3 + n], spot(t=p),
            )
            for n, p in enumerate((x, y, d))
        ]

    def row_total(buf, i):
        return buf[0, :, rows(i)] + buf[1, :, rows(i)] + buf[2, :, rows(i)] + buf[3, :, rows(i)]

    def split(part, i, value):
        low = value.astype(BF16)
        for o in range(4):
            part[o, rows(i), :] = low[:, o * width : (o + 1) * width]

    def place_own(full_ref, i):
        for o in range(4):

            @pl.when(t == o)
            def _():
                full_ref[rows(i), o * width : (o + 1) * width] = m.low[rows(i), :]

    def joined(run):
        pieces = [run.collect(n) + run.part(t, n)[...].astype(F32) for n in range(2)]
        return jnp.concatenate(pieces, axis=0)

    def inverse_mid(i):
        return lax.rsqrt(row_total(m.rows_a, i) / D + EPSILON)

    def block_stage(i):
        need(load.hid_pre, load.upd_pre)
        hidden_pre, update = m.hid_pre[rows(i), :], sigmoid(m.upd_pre[rows(i), :])
        block = update * (hidden_pre * sigmoid(hidden_pre)) + (1.0 - update) * m.tok[rows(i), :].astype(F32)
        m.block[rows(i), :] = block
        m.low[rows(i), :] = (block * m.f_gain[...]).astype(BF16)
        run_p[i].start()
        m.rows_a[t, :, rows(i)] = as_rows(jnp.sum(block * block, axis=1, keepdims=True))
        for copy in row_run(0, i, m.rows_a):
            copy.start()
        place_own(m.ffn4, i)

    def up_stage(i):
        need(load.w_up)
        run_p[i].finish()
        raw = dot(m.ffn4[rows(i), :], m.w_up[...])
        part = m.v_all.shape[1]
        parts = hidden // part
        for k in range(parts):
            m.v_all[pl.ds((parts * i + k) * B, B), :] = raw[:, k * part : (k + 1) * part]

    down, down_t = (dot_t, dot) if turn else (dot, dot_t)

    def ffn_stage(i):
        need(load.cot4)
        back = down_t(m.cot4[rows(i), :], m.w_down[...])
        for copy in row_run(0, i, m.rows_a):
            copy.wait()
        inv = as_column(inverse_mid(i))
        parts = hidden // m.v_all.shape[1]
        raw = jnp.concatenate([m.v_all[pl.ds((parts * i + k) * B, B), :] for k in range(parts)], axis=1)
        up_pre = raw * inv
        sig = sigmoid(up_pre)
        grad_up = (back * d_silu(up_pre, sig)).astype(BF16)
        split(m.part_g, i, dot_t(grad_up, m.w_up[...]))
        run_g[i].start()
        wide_grad = grad_up.astype(F32)
        m.up_grads[rows(i), :] = (wide_grad * inv).astype(BF16)
        m.rows_b[t, :, rows(i)] = as_rows(jnp.sum(wide_grad * raw, axis=1, keepdims=True))
        for copy in row_run(1, i, m.rows_b):
            copy.start()
        up_rows = (up_pre * sig).astype(BF16)
        m.up_rows[rows(i), :] = up_rows
        split(m.part_f, i, down(up_rows, m.w_down[...]))

    def grad_stage(i):
        grad_ffn = joined(run_g[i])
        for copy in row_run(1, i, m.rows_b):
            copy.wait()
        block = m.block[rows(i), :]
        inv_rows = inverse_mid(i)
        factor = inv_rows * inv_rows * inv_rows * row_total(m.rows_b, i) / D
        inv = as_column(inv_rows)
        grad_block = (
            m.cot[rows(i), :].astype(F32) + inv * (grad_ffn * m.f_gain[...]) - block * as_column(factor)
        )
        m.f_gain_grad[...] += jnp.sum(grad_ffn * block * inv, axis=0, keepdims=True)
        hidden_pre, update = m.hid_pre[rows(i), :], sigmoid(m.upd_pre[rows(i), :])
        sig = sigmoid(hidden_pre)
        m.low[rows(i), :] = (grad_block * update * d_silu(hidden_pre, sig)).astype(BF16)
        run_gh[i].start()
        keep = grad_block * (1.0 - update)
        m.tok_grad[rows(i), :] = keep
        tokens = m.tok[rows(i), :].astype(F32)
        m.upd_grad[rows(i), :] = (keep * (hidden_pre * sig - tokens) * update).astype(BF16)
        place_own(m.hid4, i)
        run_g[i].finish()

    def gate_stage(i):
        need(load.w_attended, load.g_pre, load.attended, load.w_gate, load.w_upd, load.w_hidden)
        run_gh[i].finish()
        grad_hidden = m.hid4[rows(i), :]
        grad_gated = dot_t(grad_hidden, m.w_attended[...])
        gate = m.g_pre[rows(i), :]
        sig = sigmoid(gate)
        grad_gate = (grad_gated * m.attended[rows(i), :].astype(F32) * d_silu(gate, sig)).astype(BF16)
        m.gate_grad[rows(i), :] = grad_gate
        split(m.part_t, i, dot_t(grad_gate, m.w_gate[...]) + dot_t(m.upd_grad[rows(i), :], m.w_upd[...]))
        m.att_grad[rows(i), :] = (grad_gated * (gate * sig)).astype(BF16)
        m.mix_grad[rows(i), :] = dot_t(grad_hidden, m.w_hidden[...])

    def grads_run(i):
        return [
            remote(m.k_send.at[rows(i)], m.k_got.at[rows(i)], m.s_gr.at[2 * i], m.r_gr.at[2 * i], other),
            remote(m.v_send.at[rows(i)], m.v_got.at[rows(i)], m.s_gr.at[2 * i + 1], m.r_gr.at[2 * i + 1], other),
        ]

    def attend_back(i):
        need(load.queries, load.keys, load.vals, load.log_sum)
        raw = dot_t(m.queries[rows(i), :], m.keys[window(i), :]) * scale
        same = as_column(m.ids_row[:, mine(i)]) == m.ids_row[0:1, window(i)]
        place = lax.broadcasted_iota(jnp.int32, raw.shape, 1) - lax.broadcasted_iota(jnp.int32, raw.shape, 0)
        exact = jnp.exp(jnp.where(same & (place <= count), raw, -1e30) - m.log_sum[rows(i), 0:1])
        grad_rows = m.att_grad[rows(i), :]
        value_part = t_dot(exact.astype(BF16), grad_rows)
        grad_probs = dot_t(grad_rows, m.vals[window(i), :])
        inner = jnp.sum(exact * grad_probs, axis=1, keepdims=True)
        grad_scores = exact * (grad_probs - inner) * scale
        high = grad_scores.astype(BF16)
        rest = (grad_scores - high.astype(F32)).astype(BF16)
        keys, queries = m.keys[window(i), :], m.queries[rows(i), :]
        m.q_grad[rows(i), :] = dot(high, keys) + dot(rest, keys)
        key_part = t_dot(high, queries) + t_dot(rest, queries)
        if i == 0:
            m.v_all[window(0), :] = value_part
            m.k_all[window(0), :] = key_part
        else:
            old, new = pl.ds(i * B, span - B), pl.ds(span + (i - 1) * B, B)
            m.v_all[old, :] += value_part[: span - B]
            m.v_all[new, :] = value_part[span - B :]
            m.k_all[old, :] += key_part[: span - B]
            m.k_all[new, :] = key_part[span - B :]
        m.k_send[rows(i), :] = m.k_all[rows(i), :].astype(BF16)
        m.v_send[rows(i), :] = m.v_all[rows(i), :].astype(BF16)
        for copy in grads_run(i):
            copy.start()

    def product(dst, left, right):
        for k in range(right.shape[1] // B):
            at = slice(k * B, (k + 1) * B)
            dst[:, at] = t_dot(left[...], right[:, at]).astype(BF16)

    def key_end(i):
        need(load.v_pre)
        for copy in grads_run(i):
            copy.wait()
        m.k_grad[rows(i), :] = m.k_all[mine(i), :] + m.k_got[rows(i), :].astype(F32)
        value = m.v_pre[rows(i), :].astype(F32)
        grad = m.v_all[mine(i), :] + m.v_got[rows(i), :].astype(F32)
        m.value_grad[rows(i), :] = (grad * d_silu(value, sigmoid(value))).astype(BF16)

    block_stage(0)
    block_stage(1)
    run_p[0].forward()
    block_stage(2)
    run_p[1].forward()
    block_stage(3)
    run_p[2].forward()
    up_stage(0)
    run_p[3].forward()
    up_stage(1)
    up_stage(2)
    fetch.hand_on()
    ffn_stage(0)
    up_stage(3)
    ffn_stage(1)
    run_g[0].forward()
    ffn_stage(2)
    run_g[1].forward()
    grad_stage(0)
    ffn_stage(3)
    run_g[2].forward()
    grad_stage(1)
    run_gh[0].forward()
    store.block.start()
    store.part_f.start()
    if turn:
        product(m.w_down, m.cot4, m.up_rows)
    else:
        product(m.w_down, m.up_rows, m.cot4)
    line.start(0)
    run_g[3].forward()
    grad_stage(2)
    run_gh[1].forward()
    gate_stage(0)
    line.send_on(0)
    grad_stage(3)
    run_gh[2].forward()
    gate_stage(1)
    attend_back(0)
    run_gh[3].forward()
    gate_stage(2)
    attend_back(1)
    gate_stage(3)
    store.hid4.start()
    store.upd_grad.start()
    store.gate_grad.start()
    store.tok_grad.start()
    store.part_t.start()
    store.mix_grad.start()
    attend_back(2)
    product(m.g_up, m.ffn4, m.up_grads)
    store.g_up.start()
    attend_back(3)
    key_end(0)
    key_end(1)
    key_end(2)
    key_end(3)
    store.value_grad.start()
    line.end(0)
    for copy in stores.values():
        copy.wait()


def middle(ident, line_count, ins):
    tok, f_gain = ins["tok"], ins["f_gain"]
    count, width = tok.shape
    full = 4 * width
    values, hidden = ins["w_gate"].shape[1], ins["w_up"].shape[1]
    nb = count // 256
    (turn,), (kind,), (size,), (shape,), (block,) = line_plan([(hidden, full)], KINDS[-1:], line_count)
    if turn:
        ins["s_down"] = ins["s_down"].T
    dma, s, v = pltpu.SemaphoreType.DMA, jax.ShapeDtypeStruct, pltpu.VMEM
    outs = dict(
        block=s((count, width), F32),
        part_f=s((4, count, width), BF16),
        part_t=s((4, count, width), BF16),
        tok_grad=s((count, width), F32),
        mix_grad=s((count, width), F32),
        value_grad=s((count, values), BF16),
        hid4=s((count, full), BF16),
        upd_grad=s((count, width), BF16),
        gate_grad=s((count, values), BF16),
        f_gain_grad=s((1, width), F32),
        q_grad=s((count, Z), F32),
        k_grad=s((count, Z), F32),
        g_up=s((full, hidden), BF16),
        d_down=s(block, F32),
    )
    scratch = dict(
        up_rows=v((count, hidden), BF16),
        up_grads=v((count, hidden), BF16),
        ffn4=v((count, full), BF16),
        att_grad=v((count, values), BF16),
        k_all=v((2 * count, Z), F32),
        v_all=v((2 * count, values), F32),
        part_g=v((4, count, width), BF16),
        got_g=v((3, 2 * nb, 128, width), BF16),
        low=v((count, width), BF16),
        rows_a=v((4, 8, count), F32),
        rows_b=v((4, 8, count), F32),
        k_send=v((count, Z), BF16),
        v_send=v((count, values), BF16),
        k_got=v((count, Z), BF16),
        v_got=v((count, values), BF16),
        w_down=v(shape, BF16),
        p_down=v((line_count,) + block, BF16),
        l_down=v((line_count,) + block, BF16),
        f_send=dma((line_count,)), f_recv=dma((line_count,)),
        f_core=dma((line_count,)), f_recv_core=dma((line_count,)),
        c_send=dma((1, line_count)), c_recv=dma((1, line_count)),
        l_send=dma((1, line_count)), l_recv=dma((1, line_count)),
        send=dma((18 * nb,)), recv=dma((18 * nb,)),
        s_rows=dma((6 * nb,)), r_rows=dma((6 * nb,)),
        s_gr=dma((2 * nb,)), r_gr=dma((2 * nb,)),
        s_in=dma((len(MID_LOAD),)), s_out=dma((len(MID_STORE),)),
    )
    got_all = pl.pallas_call(
        functools.partial(mid_kernel, kind, size, turn, line_count),
        out_shape=[outs[n] for n in MID_OUT],
        in_specs=[ANY if n in MID_LOAD else VMEM for n in MID_IN],
        out_specs=[ANY if n in MID_STORE else VMEM for n in MID_OUT],
        scratch_shapes=[scratch[n] for n in MID_SCRATCH]
        + [v(ins[n].shape, ins[n].dtype) for n in MID_LOAD]
        + [v(outs[n].shape, outs[n].dtype) for n in MID_STORE],
        compiler_params=pltpu.CompilerParams(collective_id=ident, has_side_effects=True, vmem_limit_bytes=62 * 2**20),
        name="middle",
    )(*[ins[n] for n in MID_IN])
    got_all = Named(MID_OUT, got_all)
    if turn:
        got_all.d_down = got_all.d_down.T
    return got_all


REAR_LOAD = named(
    lambda part_t, g_up, value_grad, w_value, gated, hid4, mixed4, upd_grad, gate_grad, normed4,
    part_f, mix_grad, mix_pre, xn, tok_grad, block: None
)
REAR_IN = REAR_LOAD + named(
    lambda q_grad, k_grad, s_pre, w_shared, tok, inv_rows, keep_next, gain, damp, eta, q_gain,
    k_gain, f_gain_grad: None
)
REAR_WEIGHTS = WEIGHTS[:-1]
REAR_OUT = named(lambda grad_in, small, out: None) + ["d_" + w for w in REAR_WEIGHTS]
REAR_SCRATCH = named(
    lambda part_v, got_v, got_t, got_f, part_s, got_s, low_s, full_s, grad_mix, back, rows, ends,
    starts, end_out, end_in, small_core, small_all, own_q, all_q, upd_cols, send, recv, s_rows,
    r_rows, s_core, r_core, s_upd, r_upd, s_small, r_small, s_q, r_q, s_in, c_send, c_recv, l_send,
    l_recv: None
)


def rear_kernel(kinds, sizes, turns, line_count, *refs):
    groups_of = [p + w for p in ("p_", "l_") for w in REAR_WEIGHTS] + ["g_" + w for w in REAR_WEIGHTS[:-1]]
    m = Named(REAR_IN + REAR_OUT + REAR_SCRATCH + groups_of + ["i_" + n for n in REAR_LOAD], refs)
    loads = {}
    for k, n in enumerate(REAR_LOAD):
        loads[n] = Transfer(pltpu.make_async_copy(getattr(m, n), getattr(m, "i_" + n), m.s_in.at[k]))
        setattr(m, n, getattr(m, "i_" + n))
        loads[n].start()
    load = types.SimpleNamespace(**loads)
    t, x, y, d = tp_peers()
    z, c = lax.axis_index("fsdp"), lax.axis_index("ctx")
    other = spot(c=1 - c)
    groups, count = m.xn.shape[0], m.xn.shape[1]
    step, nj, width = count // 8, m.damp.shape[0], m.damp.shape[1]
    B = 256
    half, nb = B // 2, count // B
    part = 8
    zero = jnp.zeros((8, 128), F32)

    def lanes(o):
        return pl.ds(pl.multiple_of(o * width, width), width)

    line = LineSum(
        kinds, sizes, line_count,
        [getattr(m, "g_" + w) for w in REAR_WEIGHTS], [getattr(m, "p_" + w) for w in REAR_WEIGHTS],
        [getattr(m, "l_" + w) for w in REAR_WEIGHTS], [getattr(m, "d_" + w) for w in REAR_WEIGHTS],
        (m.c_send, m.c_recv, m.l_send, m.l_recv),
    )
    m.end_in[...] = jnp.zeros_like(m.end_in)
    greet([spot(t=x), spot(t=y), spot(t=d), other] + line_peers(line_count))

    run_s = Scatter(
        2,
        lambda o, n: m.part_s.at[pl.ds(pl.multiple_of(o * B + n * half, half), half)],
        lambda n: m.got_s.at[0, n], lambda n: m.got_s.at[1, n], lambda n: m.got_s.at[2, n],
        m.send, m.recv, 0,
    )
    run_full = Gather(
        2,
        lambda n: m.low_s.at[pl.ds(n * half, half)],
        lambda o, n: m.full_s.at[pl.ds(pl.multiple_of(o * B + n * half, half), half)],
        m.send, m.recv, 6,
    )

    def scatter_runs(kind, parts, got):
        return [
            Scatter(
                2,
                lambda o, n, i=i: parts.at[o, pl.ds(i * B + n * half, half)],
                lambda n, i=i: got.at[0, i * 2 + n],
                lambda n, i=i: got.at[1, i * 2 + n],
                lambda n, i=i: got.at[2, i * 2 + n],
                m.send, m.recv, 12 + 6 * (kind * nb + i),
            )
            for i in range(nb)
        ]

    run_t, run_v, run_f = (
        scatter_runs(k, parts, got)
        for k, (parts, got) in enumerate(((m.part_t, m.got_t), (m.part_v, m.got_v), (m.part_f, m.got_f)))
    )

    m.part_s[...] = (m.q_grad[...] * m.q_gain[...] + m.k_grad[...] * m.k_gain[...]).astype(BF16)
    run_s.start()
    shared = m.s_pre[...] * sigmoid(m.s_pre[...])
    m.own_q[...] = jnp.zeros_like(m.own_q)
    m.own_q[0:1, 0:Z] = jnp.sum(shared * m.q_grad[...], axis=0, keepdims=True)
    m.own_q[0:1, Z:] = jnp.sum(shared * m.k_grad[...], axis=0, keepdims=True)
    m.all_q[t] = m.own_q[...]
    gains = [
        remote(m.own_q, m.all_q.at[t], m.s_q.at[k], m.r_q.at[k], spot(t=p)) for k, p in enumerate((x, y, d))
    ]
    for copy in gains:
        copy.start()
    need(load.part_t)
    run_t[0].start()
    run_t[1].start()
    def value_part(i):
        rows = slice(i * B, (i + 1) * B)
        low = dot_t(m.value_grad[rows, :], m.w_value[...]).astype(BF16)
        for o in range(4):
            m.part_v[o, rows, :] = low[:, o * width : (o + 1) * width]

    def product(w, left, right):
        dst = getattr(m, "g_" + w)
        if turns[REAR_WEIGHTS.index(w)]:
            left, right = right, left
        size = min(256, right.shape[1])
        for k in range(right.shape[1] // size):
            at = slice(k * size, (k + 1) * size)
            dst[:, at] = t_dot(left, right[:, at]).astype(BF16)

    at_w = {w: k for k, w in enumerate(REAR_WEIGHTS)}

    need(load.value_grad, load.w_value)

    def value_part(i):
        rows = slice(i * B, (i + 1) * B)
        low = dot_t(m.value_grad[rows, :], m.w_value[...]).astype(BF16)
        for o in range(4):
            m.part_v[o, rows, :] = low[:, o * width : (o + 1) * width]

    need(load.g_up)
    line.start(at_w["up"])
    need(load.gated, load.hid4)
    product("attended", m.gated[...], m.hid4[...])
    line.start(at_w["attended"])
    run_s.forward()
    run_t[0].forward()
    run_t[2].start()
    line.send_on(at_w["up"])
    run_t[1].forward()
    run_t[3].start()
    need(load.mixed4, load.upd_grad)
    product("hidden", m.mixed4[:, lanes(t)], m.hid4[...])
    line.start(at_w["hidden"])
    quarter = pl.ds(pl.multiple_of(t * B, B), B)
    for n in range(2):
        total = run_s.collect(n) + run_s.part(t, n)[...].astype(F32)
        pre = m.s_pre[pl.ds(pl.multiple_of(t * B + n * half, half), half), :]
        m.low_s[n * half : (n + 1) * half, :] = (total * d_silu(pre, sigmoid(pre))).astype(BF16)
    run_full.start()
    m.full_s[quarter, :] = m.low_s[...]
    run_t[2].forward()
    line.send_on(at_w["attended"])
    turn_update = turns[at_w["update"]]
    if turn_update:
        m.upd_cols[...] = t_dot(m.upd_grad[...], m.mixed4[...]).astype(BF16)
    else:
        m.upd_cols[...] = t_dot(m.mixed4[...], m.upd_grad[...]).astype(BF16)

    def ends_of(p):
        if turn_update:
            return m.upd_cols.at[:, lanes(p)], m.g_update.at[lanes(t)]
        return m.upd_cols.at[lanes(p)], m.g_update.at[:, lanes(t)]

    turn_copies = [
        remote(*ends_of(p), m.s_upd.at[k], m.r_upd.at[k], spot(t=p)) for k, p in enumerate((x, y, d))
    ] + [pltpu.make_async_copy(*ends_of(t), m.s_upd.at[3])]
    for copy in turn_copies:
        copy.start()
    run_t[3].forward()
    run_full.forward()
    need(load.value_grad, load.w_value)
    value_part(0)
    run_v[0].start()
    value_part(1)
    run_v[1].start()
    line.send_on(at_w["hidden"])
    need(load.gate_grad, load.normed4)
    product("gate", m.mixed4[...], m.gate_grad[...])
    line.start(at_w["gate"])
    value_part(2)
    value_part(3)
    run_s.finish()
    run_full.finish()
    product("shared", m.mixed4[...], m.full_s[...])
    line.start(at_w["shared"])
    run_v[0].forward()
    run_v[2].start()
    for copy in turn_copies:
        copy.wait()
    line.start(at_w["update"])
    product("value", m.normed4[...], m.value_grad[...])
    line.start(at_w["value"])
    line.send_on(at_w["gate"])
    run_v[1].forward()
    run_v[3].start()
    line.send_on(at_w["update"])
    need(load.mix_grad, load.mix_pre, load.xn, load.tok_grad)
    own_shared = m.w_shared[lanes(t), :]
    for i in range(nb):
        for n in range(2):
            at = pl.ds(i * B + n * half, half)
            mix = m.mix_grad[at, :] + run_t[i].collect(n) + run_t[i].part(t, n)[...].astype(F32)
            mix = mix + dot_t(m.full_s[at, :], own_shared)
            for g in range(groups):
                pre = m.mix_pre[g, at, :]
                m.grad_mix[g, at, :] = mix[:, g * 128 : (g + 1) * 128] * d_silu(pre, sigmoid(pre))
        run_t[i].finish()
    line.send_on(at_w["shared"])
    line.send_on(at_w["value"])
    need(load.part_f, load.block)

    def later(*steps):
        return list(steps)

    waiting = later(
        run_v[2].forward, run_v[3].forward, run_f[0].start, run_f[1].start, run_f[0].forward, run_f[2].start,
        run_f[1].forward, run_f[3].start, run_f[2].forward, run_f[3].forward,
    )

    def go(count):
        for _ in range(min(count, len(waiting))):
            waiting.pop(0)()

    for g in range(groups):
        ln = pl.ds(g * 128, 128)
        for j0 in range(0, nj, part):
            decay = [wide(1.0 - m.damp[pl.ds(j, 1), ln]) for j in range(j0, j0 + part)]

            def scan(i, carry):
                a, w, chain = carry
                at = pl.ds(step - 1 - i, 8, stride=step)
                v, k = m.grad_mix[g, at, :], m.keep_next[at, :]
                held = [k * r for r in decay]
                w = tuple(k * p + r * q for p, r, q in zip(a, held, w))
                a = tuple(v + r * p for r, p in zip(held, a))
                return a, w, chain * k

            a, w, chain = lax.fori_loop(0, step, scan, ((zero,) * part, (zero,) * part, zero + 1.0), unroll=4)
            for n in range(part):
                less = power(decay[n], step - 1)
                m.ends[0, j0 + n, :, ln] = a[n]
                m.ends[1, j0 + n, :, ln] = w[n]
                m.ends[2, j0 + n, :, ln] = less * decay[n] * chain
                m.ends[3, j0 + n, :, ln] = float(step) * less * chain
            go(1)

    def merge(q, a, w):
        return (
            m.ends[0, :, q, :] + m.ends[2, :, q, :] * a,
            m.ends[1, :, q, :] + m.ends[2, :, q, :] * w + m.ends[3, :, q, :] * a,
        )

    a = w = jnp.zeros((nj, width), F32)
    for q in range(7, -1, -1):
        a, w = merge(q, a, w)
    m.end_out[0] = a
    m.end_out[1] = w
    across = remote(m.end_out, m.end_in, m.s_core.at[0], m.r_core.at[0], other)
    across.start()
    across.wait()
    a, w = jnp.where(c == 0, m.end_in[0], 0.0), jnp.where(c == 0, m.end_in[1], 0.0)
    for q in range(7, -1, -1):
        m.starts[0, :, q, :] = a
        m.starts[1, :, q, :] = w
        a, w = merge(q, a, w)

    for g in range(groups):
        ln = pl.ds(g * 128, 128)
        for j0 in range(0, nj, part):
            span = range(j0, j0 + part)
            decay = [wide(1.0 - m.damp[pl.ds(j, 1), ln]) for j in span]
            weight = [wide(m.damp[pl.ds(j, 1), ln] * m.eta[pl.ds(j, 1), ln]) for j in span]

            def scan(i, carry):
                a, w, sum_a, sum_w = carry
                at = pl.ds(step - 1 - i, 8, stride=step)
                v, k, u = m.grad_mix[g, at, :], m.keep_next[at, :], m.xn[g, at, :]
                held = [k * r for r in decay]
                w = tuple(k * p + r * q for p, r, q in zip(a, held, w))
                a = tuple(v + r * p for r, p in zip(held, a))
                sum_a = tuple(s + u * p for s, p in zip(sum_a, a))
                sum_w = tuple(s + u * p for s, p in zip(sum_w, w))
                base = v if j0 == 0 else m.back[g, at, :]
                m.back[g, at, :] = base + tree_sum([r * p for r, p in zip(weight, a)])
                return a, w, sum_a, sum_w

            first = (tuple(m.starts[0, j, :, ln] for j in span), tuple(m.starts[1, j, :, ln] for j in span))
            _, _, sum_a, sum_w = lax.fori_loop(
                0, step, scan, first + ((zero,) * part, (zero,) * part), unroll=4
            )
            for n, j in enumerate(span):
                at = pl.ds(j, 1)
                all_a = jnp.sum(sum_a[n], axis=0, keepdims=True)
                all_w = jnp.sum(sum_w[n], axis=0, keepdims=True)
                rate = m.damp[at, ln]
                m.small[at, ln] = m.eta[at, ln] * (all_a - rate * all_w)
                m.small[pl.ds(nj + j, 1), ln] = rate * all_a
            go(2)

    go(len(waiting))
    inv = m.inv_rows[...].T[:, 0:1]
    value = m.tok[...].astype(F32)
    for i in range(nb):
        for n in range(2):
            at = pl.ds(i * B + n * half, half)
            got = run_v[i].collect(n) + run_v[i].part(t, n)[...].astype(F32)
            m.grad_in[at, :] = got + jnp.concatenate([m.back[g, at, :] for g in range(groups)], axis=1)
        run_v[i].finish()
    grad_normed = m.grad_in[...]
    m.small[2 * nj :, :] = jnp.zeros((m.small.shape[0] - 2 * nj, width), F32)
    m.small[2 * nj : 2 * nj + 1, :] = jnp.sum(grad_normed * value * inv, axis=0, keepdims=True)
    m.small[2 * nj + 1 : 2 * nj + 2, :] = m.f_gain_grad[...]
    for copy in gains:
        copy.wait()
    m.small[2 * nj + 2 : 2 * nj + 3, :] = (
        m.all_q[0, 0:1] + m.all_q[1, 0:1] + m.all_q[2, 0:1] + m.all_q[3, 0:1]
    )
    scaled = grad_normed * m.gain[...]
    m.rows[t] = row_sums(scaled * value)
    sums = row_exchange(m.rows, m.s_rows, m.r_rows)
    pair = remote(m.small, m.small_core, m.s_small.at[0], m.r_small.at[0], other)
    for copy in sums + [pair]:
        copy.start()
    m.grad_in[...] = m.tok_grad[...] + inv * scaled
    pair.wait()
    m.small_all[z] = m.small[...] + m.small_core[...]
    wide_sums = [
        remote(
            m.small_all.at[z], m.small_all.at[z], m.s_small.at[k], m.r_small.at[k], spot(f=(z + k) % line_count)
        )
        for k in range(1, line_count)
    ]
    for copy in wide_sums:
        copy.start()
    for copy in sums:
        copy.wait()
    factor = m.inv_rows[...]
    factor = factor * factor * factor * (m.rows[0] + m.rows[1] + m.rows[2] + m.rows[3]) / D
    m.grad_in[...] -= value * factor.T[:, 0:1]
    for copy in wide_sums:
        copy.wait()
    total = m.small_all[0]
    for k in range(1, line_count):
        total = total + m.small_all[k]
    m.small[...] = total
    for i in range(nb):
        for n in range(2):
            at = pl.ds(i * B + n * half, half)
            got = run_f[i].collect(n) + run_f[i].part(t, n)[...].astype(F32)
            m.out[at, :] = (m.block[at, :] + got).astype(BF16)
        run_f[i].finish()
    for w in ("up", "attended", "hidden", "gate", "update", "shared", "value"):
        line.end(at_w[w])


def rear(ident, line_count, ins):
    count, width = ins["tok"].shape
    groups, nj = width // 128, ins["damp"].shape[0]
    full = 4 * width
    nb = count // 256
    values = ins["value_grad"].shape[1]
    shapes = [(full, Z), (full, values), (full, values), (width, full), (values, full), (width, full), (full, ins["g_up"].shape[1])]
    turns, kinds, sizes, shapes, blocks = line_plan(shapes, KINDS[:-1], line_count)
    dma, s, v, k = pltpu.SemaphoreType.DMA, jax.ShapeDtypeStruct, pltpu.VMEM, len(REAR_WEIGHTS)
    tall = 2 * nj + 8
    n = 12 + 18 * nb
    lanes = v((groups, count, 128), F32)
    got = v((3, 2 * nb, 128, width), BF16)
    scratch = dict(
        part_v=v((4, count, width), BF16),
        got_v=got, got_t=got, got_f=got,
        part_s=v((count, Z), BF16),
        got_s=v((3, 2, 128, Z), BF16),
        low_s=v((256, Z), BF16),
        full_s=v((count, Z), BF16),
        grad_mix=lanes, back=lanes,
        rows=v((4, 8, count), F32),
        ends=v((4, nj, 8, width), F32),
        starts=v((2, nj, 8, width), F32),
        end_out=v((2, nj, width), F32),
        end_in=v((2, nj, width), F32),
        small_core=v((tall, width), F32),
        small_all=v((line_count, tall, width), F32),
        own_q=v((8, width), F32),
        all_q=v((4, 8, width), F32),
        upd_cols=v((width, full) if turns[REAR_WEIGHTS.index("update")] else (full, width), BF16),
        send=dma((n,)), recv=dma((n,)), s_rows=dma((3,)), r_rows=dma((3,)), s_core=dma((1,)), r_core=dma((1,)),
        s_upd=dma((4,)), r_upd=dma((3,)), s_small=dma((line_count,)), r_small=dma((line_count,)),
        s_q=dma((3,)), r_q=dma((3,)), s_in=dma((len(REAR_LOAD),)),
        c_send=dma((k, line_count)), c_recv=dma((k, line_count)),
        l_send=dma((k, line_count)), l_recv=dma((k, line_count)),
    )
    got = pl.pallas_call(
        functools.partial(rear_kernel, kinds, sizes, turns, line_count),
        out_shape=[s((count, width), F32), s((tall, width), F32), s((count, width), BF16)] + [s(b, F32) for b in blocks],
        in_specs=[ANY if name in REAR_LOAD else VMEM for name in REAR_IN],
        out_specs=[VMEM] * len(REAR_OUT),
        scratch_shapes=[scratch[name] for name in REAR_SCRATCH]
        + [v((line_count,) + b, BF16) for b in blocks]
        + [v((line_count,) + b, BF16) for b in blocks]
        + [v(shape, BF16) for shape in shapes[:-1]]
        + [v(ins[name].shape, ins[name].dtype) for name in REAR_LOAD],
        compiler_params=pltpu.CompilerParams(collective_id=ident, has_side_effects=True, vmem_limit_bytes=62 * 2**20),
        name="rear",
    )(*[ins[name] for name in REAR_IN])
    grads = [g.T if turn else g for turn, g in zip(turns, got[3:])]
    return got[0], got[1], got[2], grads


def on_device(
    line_count,
    layer_input, segment_ids, cotangent, norm_gain, ema_damping, ema_eta, query_gain, key_gain,
    ffn_gain, *weights,
):
    tok, cot = layer_input[0], cotangent[0]
    segment = segment_ids[0]
    row_count = tok.shape[0]
    core = lax.axis_index("ctx")
    offset = core * row_count
    all_ids = lax.all_gather(segment, "ctx", axis=0, tiled=True)
    same = jnp.concatenate(
        [jnp.zeros((1,), F32), (all_ids[1:] == all_ids[:-1]).astype(F32), jnp.zeros((1,), F32)]
    )
    keep = lax.dynamic_slice_in_dim(same, offset, row_count, 0)
    keep_next = lax.dynamic_slice_in_dim(same, offset + 1, row_count, 0)
    keep_wide = jnp.broadcast_to(keep[:, None], (row_count, 128))
    next_wide = jnp.broadcast_to(keep_next[:, None], (row_count, 128))
    prev_ids = jnp.where(core > 0, all_ids[:row_count], -1)
    ids_row = jnp.broadcast_to(jnp.concatenate([prev_ids, segment]).astype(F32)[None], (8, 2 * row_count))
    a = front(
        1, line_count, tok, keep_wide, norm_gain, ema_damping, ema_eta, query_gain, key_gain, ids_row, cot, weights[:-1]
    )
    ins = {n: getattr(a, n) for n in MID_LOAD if n != "w_upd"}
    ins.update(w_upd=a.rows_update, tok=tok, cot=cot, f_gain=ffn_gain[None], ids_row=ids_row, s_down=weights[-1])
    m = middle(2, line_count, ins)
    ins = {n: getattr(m if n in MID_OUT else a, n) for n in REAR_IN if n in MID_OUT or n in A_OUT}
    ins.update(
        tok=tok, keep_next=next_wide, gain=norm_gain[None], damp=ema_damping, eta=ema_eta,
        q_gain=query_gain[None], k_gain=key_gain[None],
    )
    grad_in, small, out, grads = rear(3, line_count, ins)
    n = ema_damping.shape[0]
    return (
        out[None], grad_in[None], small[2 * n], small[:n], small[n : 2 * n],
        small[2 * n + 2, :Z], small[2 * n + 2, Z:], small[2 * n + 1], *grads, m.d_down,
    )


def solution(mesh):
    token = P("fsdp", "ctx", "tp")
    row, col = P(("fsdp", "ctx"), "tp"), P("tp", ("fsdp", "ctx"))
    shared = P(("fsdp", "ctx"), None)
    weights = (shared, row, row, col, col, col, row, col)
    small = P(None, "tp")
    return jax.shard_map(
        functools.partial(on_device, mesh.shape["fsdp"]),
        mesh=mesh,
        in_specs=(token, P("fsdp", "ctx"), token, P("tp"), small, small, P(), P(), P("tp")) + weights,
        out_specs=(token, token, P("tp"), small, small, P(), P(), P("tp")) + weights,
        check_vma=False,
    )
```

```python
import functools
import inspect
import math
import types

import jax
import jax.numpy as jnp
from jax import lax
from jax.experimental import pallas as pl
from jax.experimental.pallas import tpu as pltpu
from jax.sharding import PartitionSpec as P

D = 1024
Z = 128
EPSILON = 1e-06
MESH = pl.DeviceIdType.MESH
F32 = jnp.float32
BF16 = jnp.bfloat16
VMEM = pl.BlockSpec(memory_space=pltpu.VMEM)
ANY = pl.BlockSpec(memory_space=pl.ANY)
HIGH = lax.Precision.HIGHEST


def named(signature):
    return list(inspect.signature(signature).parameters)


def spot(f=None, c=None, t=None):
    return (
        lax.axis_index("fsdp") if f is None else f,
        lax.axis_index("ctx") if c is None else c,
        lax.axis_index("tp") if t is None else t,
    )


def greet(devices):
    barrier = pltpu.get_barrier_semaphore()
    for device in devices:
        pl.semaphore_signal(barrier, inc=1, device_id=device, device_id_type=MESH)
    pl.semaphore_wait(barrier, len(devices))


def tp_peers():
    t = lax.axis_index("tp")
    return t, t + 1 - 2 * (t % 2), (t + 2) % 4, 3 - t


def remote(src, dst, send, recv, device):
    return pltpu.make_async_remote_copy(
        src_ref=src, dst_ref=dst, send_sem=send, recv_sem=recv, device_id=device, device_id_type=MESH
    )


class Gather:
    def __init__(self, count, source, place, send, recv, base=0):
        self.count, self.half = count, count // 2
        self.source, self.place, self.send, self.recv, self.base = source, place, send, recv, base
        self.t, self.x, self.y, _ = tp_peers()

    def copy(self, src, owner, i, way, to):
        n = self.base + way * self.count + i
        return remote(src, self.place(owner, i), self.send.at[n], self.recv.at[n], spot(t=to))

    def first(self, i, way):
        return self.copy(self.source(i), self.t, i, way, self.x if way == 0 else self.y)

    def start(self):
        for k in range(self.half):
            self.first(k, 0).start()
            self.first(k + self.half, 1).start()
        for k in range(self.half):
            self.first(k + self.half, 0).start()
            self.first(k, 1).start()

    def onward(self, i):
        if i < self.half:
            return self.copy(self.place(self.x, i), self.x, i, 2, self.y)
        return self.copy(self.place(self.y, i), self.y, i, 2, self.x)

    def begin(self, k):
        self.first(k, 0).start()
        self.first(k + self.half, 1).start()
        self.first(k + self.half, 0).start()
        self.first(k, 1).start()

    def pass_on(self, k):
        self.first(k, 0).wait_recv()
        self.onward(k).start()
        self.first(k + self.half, 1).wait_recv()
        self.onward(k + self.half).start()

    def forward(self):
        for k in range(self.half):
            self.pass_on(k)

    def finish(self):
        for k in range(self.half):
            self.first(k + self.half, 0).wait_recv()
            self.first(k, 1).wait_recv()
        for i in range(self.count):
            self.onward(i).wait()
            self.first(i, 0).wait_send()
            self.first(i, 1).wait_send()


class Scatter:
    def __init__(self, count, part, first_diag, first_own, second, send, recv, base=0):
        self.count, self.part = count, part
        self.diag, self.own, self.second = first_diag, first_own, second
        self.send, self.recv, self.base = send, recv, base
        self.t, self.x, self.y, self.d = tp_peers()

    def ways(self, i):
        return (self.x, self.y) if i % 2 == 0 else (self.y, self.x)

    def copy(self, i, kind):
        near, far = self.ways(i)
        n = self.base + kind * self.count + i
        if kind == 0:
            src, dst, to = self.part(self.d, i), self.diag(i), near
        elif kind == 1:
            src, dst, to = self.part(near, i), self.own(i), near
        else:
            src, dst, to = self.part(far, i), self.second(i), far
        return remote(src, dst, self.send.at[n], self.recv.at[n], spot(t=to))

    def start(self):
        for i in range(self.count):
            self.copy(i, 0).start()
        for i in range(self.count):
            self.copy(i, 1).start()

    def forward(self):
        for i in range(self.count):
            self.copy(i, 0).wait_recv()
            mine = self.part(self.ways(i)[1], i)
            mine[...] = (mine[...].astype(F32) + self.diag(i)[...].astype(F32)).astype(BF16)
            self.copy(i, 2).start()

    def collect(self, i):
        self.copy(i, 1).wait_recv()
        self.copy(i, 2).wait_recv()
        return self.own(i)[...].astype(F32) + self.second(i)[...].astype(F32)

    def finish(self):
        for i in range(self.count):
            for kind in range(3):
                self.copy(i, kind).wait_send()


def shard_at(ref, kind, index, size):
    if kind == "row":
        return ref.at[pl.ds(pl.multiple_of(index * size, size), size)]
    return ref.at[:, pl.ds(pl.multiple_of(index * size, size), size)]


def turned(kind, size):
    return kind == "col" and size % 128 != 0


def row_exchange(rows, send, recv):
    t, x, y, d = tp_peers()
    return [
        remote(rows.at[t], rows.at[t], send.at[k], recv.at[k], spot(t=p))
        for k, p in enumerate((x, y, d))
    ]


class Named:
    def __init__(self, names, refs):
        for name, ref in zip(names, refs, strict=True):
            setattr(self, name, ref)


class Transfer:
    def __init__(self, copy):
        self.copy, self.waited = copy, False

    def start(self):
        self.copy.start()

    def wait(self):
        if not self.waited:
            self.waited = True
            self.copy.wait()


def need(*transfers):
    for transfer in transfers:
        transfer.wait()


def dot(left, right):
    return jnp.dot(left, right, preferred_element_type=F32)


def dot_t(left, right):
    return lax.dot_general(left, right, (((1,), (1,)), ((), ())), preferred_element_type=F32)


def t_dot(left, right):
    return lax.dot_general(left, right, (((0,), (0,)), ((), ())), preferred_element_type=F32)


def sigmoid(v):
    return 1.0 / (1.0 + jnp.exp(-v))


def d_silu(v, s):
    return s * (1.0 + v * (1.0 - s))


def as_rows(column):
    return jnp.broadcast_to(column, (column.shape[0], 128)).T[0:8]


def as_column(rows):
    return rows.T[:, 0:1]


def at_block(i, size):
    return pl.ds(i * size if isinstance(i, int) else pl.multiple_of(i * size, size), size)


def wide(row):
    return jnp.broadcast_to(row, (8, 128))


def tree_sum(terms):
    while len(terms) > 1:
        terms = [a + b for a, b in zip(terms[::2], terms[1::2])]
    return terms[0]


def power(base, exponent):
    result, square = None, base
    while exponent:
        if exponent & 1:
            result = square if result is None else result * square
        exponent >>= 1
        if exponent:
            square = square * square
    return result


def row_sums(values):
    return lax.dot_general(
        jnp.ones((8, values.shape[1]), F32), values, (((1,), (1,)), ((), ())),
        precision=HIGH, preferred_element_type=F32,
    )


class Line:
    def __init__(self, kinds, sizes, count, sources, places, sems):
        self.kinds, self.sizes, self.count = kinds, sizes, count
        self.sources, self.places = sources, places
        self.here, self.send_up, self.send_down, self.send_core, self.recv, self.recv_core = sems
        self.z, self.c = lax.axis_index("fsdp"), lax.axis_index("ctx")
        self.other = spot(c=1 - self.c)
        self.up = spot(f=(self.z + 1) % count)
        self.down = spot(f=(self.z + count - 1) % count)
        self.next = {}

    def slot(self, w, owner, core):
        return shard_at(self.places[w], self.kinds[w], owner * 2 + core, self.sizes[w])

    def to_core(self, w, owner, src):
        return remote(
            src, self.slot(w, owner, self.c), self.send_core.at[w, owner], self.recv_core.at[w, owner], self.other
        )

    def to_up(self, w, owner, src):
        return remote(src, self.slot(w, owner, self.c), self.send_up.at[w, owner], self.recv.at[w, owner], self.up)

    def to_down(self, w, owner, src):
        return remote(src, self.slot(w, owner, self.c), self.send_down.at[w, owner], self.recv.at[w, owner], self.down)

    def keep(self, w):
        return pltpu.make_async_copy(self.sources[w], self.slot(w, self.z, self.c), self.here.at[w])

    def own(self, group):
        for w in group:

            @pl.when(self.z + 1 < self.count)
            def _():
                self.to_up(w, self.z, self.sources[w]).start()

            @pl.when(self.z > 0)
            def _():
                self.to_down(w, self.z, self.sources[w]).start()

            self.to_core(w, self.z, self.sources[w]).start()
            self.keep(w).start()
            self.next[w] = 1

    def hand_on(self, w, step):
        low, high = self.z - step, self.z + step

        @pl.when(low >= 0)
        def _():
            got = self.slot(w, low, self.c)
            self.to_up(w, low, got).wait_recv()

            @pl.when(self.z + 1 < self.count)
            def _():
                self.to_up(w, low, got).start()

            self.to_core(w, low, got).start()

        @pl.when(high < self.count)
        def _():
            got = self.slot(w, high, self.c)
            self.to_down(w, high, got).wait_recv()

            @pl.when(self.z > 0)
            def _():
                self.to_down(w, high, got).start()

            self.to_core(w, high, got).start()

    def pump(self, group):
        for w in group:
            if self.next[w] < self.count:
                self.hand_on(w, self.next[w])
                self.next[w] += 1

    def done(self, group):
        for w in group:
            if self.next[w] < self.count:

                @pl.loop(self.next[w], self.count)
                def _(step):
                    self.hand_on(w, step)

            @pl.loop(0, self.count)
            def _(owner):
                got = self.slot(w, owner, self.c)
                self.to_core(w, owner, got).wait()

                @pl.when((owner <= self.z) & (self.z + 1 < self.count))
                def _():
                    self.to_up(w, owner, got).wait_send()

                @pl.when((owner >= self.z) & (self.z > 0))
                def _():
                    self.to_down(w, owner, got).wait_send()

            self.keep(w).wait()


WEIGHTS = named(lambda shared, value, gate, hidden, attended, update, up, down: None)
KINDS = ("row", "row", "row", "col", "col", "col", "row", "col")
FRONT_WEIGHTS = WEIGHTS
A_IN = named(lambda tok, keep, gain, damp, eta, q_gain, k_gain, ids_row, cot: None) + ["s_" + w for w in FRONT_WEIGHTS]
A_OUT = named(
    lambda rows_update, normed4, mixed4, mix_pre, xn, inv_rows, s_pre, v_pre, g_pre, keys, vals,
    queries, log_sum, attended, gated, hid_pre, upd_pre, cot4: None
) + ["w_" + w for w in FRONT_WEIGHTS if w != "update"]
A_HBM = named(
    lambda rows_update, normed4, mixed4, mix_pre, xn, v_pre, g_pre, keys, vals, attended, gated,
    hid_pre, upd_pre, cot4: None
) + [
    "w_" + w for w in FRONT_WEIGHTS if w != "update"
]
A_SCRATCH = named(
    lambda low_n, low_m, rows, ends, starts, end_out, end_in, part_h, got_h, w_update, send, recv,
    s_rows, r_rows, s_core, r_core, s_upd, r_upd, s_kv, r_kv, s_out, z_here, z_up, z_down, z_core,
    z_recv, z_recv_core: None
)


def front_kernel(kinds, sizes, turns, line_count, *refs):
    aside = [w for w, turn in zip(FRONT_WEIGHTS, turns) if turn and w != "down"]
    names = A_IN + A_OUT + A_SCRATCH + ["v_" + n for n in A_HBM] + ["t_" + w for w in aside]
    m = Named(names, refs)
    outs = {}
    for k, n in enumerate(A_HBM):
        outs[n] = pltpu.make_async_copy(getattr(m, "v_" + n), getattr(m, n), m.s_out.at[k])
        setattr(m, n, getattr(m, "v_" + n))
    out = types.SimpleNamespace(**outs)
    t, x, y, d = tp_peers()
    c = lax.axis_index("ctx")
    other = spot(c=1 - c)
    groups, count = m.xn.shape[0], m.xn.shape[1]
    step, nj, width = count // 8, m.damp.shape[0], m.damp.shape[1]
    B = 256
    half, nb, span = B // 2, count // B, count + B
    scale = 1.0 / math.sqrt(Z)

    def lanes(o):
        return pl.ds(pl.multiple_of(o * width, width), width)

    line = Line(
        kinds, sizes, line_count, [getattr(m, "s_" + w) for w in FRONT_WEIGHTS],
        [getattr(m, ("t_" if w in aside else "w_") + w) for w in FRONT_WEIGHTS],
        (m.z_here, m.z_up, m.z_down, m.z_core, m.z_recv, m.z_recv_core),
    )
    first_w, second_w, third_w, fourth_w = (0, 1, 2), (3, 4, 5), (6,), (7,)

    m.end_in[...] = jnp.zeros_like(m.end_in)
    value = m.tok[...].astype(F32)
    m.rows[t] = row_sums(value * value)
    greet([spot(t=x), spot(t=y), spot(t=d), other, line.up, line.down])
    sums = [
        remote(m.rows.at[t], m.rows.at[t], m.s_rows.at[k], m.r_rows.at[k], spot(t=p))
        for k, p in enumerate((x, y, d))
    ]
    for copy in sums:
        copy.start()
    line.own(first_w)
    line.own(second_w)
    for copy in sums:
        copy.wait()
    inv = lax.rsqrt((m.rows[0] + m.rows[1] + m.rows[2] + m.rows[3]) / D + EPSILON)
    m.inv_rows[...] = inv
    normed = m.tok[...].astype(F32) * inv.T[:, 0:1] * m.gain[...]
    m.low_n[...] = normed.astype(BF16)
    for g in range(groups):
        m.xn[g] = normed[:, g * 128 : (g + 1) * 128]
    out.xn.start()
    chunks = 8
    size = count // chunks

    def whole_run(low, place, base):
        return Gather(
            chunks,
            lambda i: low.at[pl.ds(i * size, size)],
            lambda o, i: place.at[pl.ds(i * size, size), lanes(o)],
            m.send, m.recv, base,
        )

    norm_run = whole_run(m.low_n, m.normed4, 0)
    cot_run = whole_run(m.cot, m.cot4, 24)
    mix_run = whole_run(m.low_m, m.mixed4, 48)
    norm_run.start()

    for g in range(groups):
        ln = pl.ds(g * 128, 128)
        decay = [wide(1.0 - m.damp[pl.ds(j, 1), ln]) for j in range(nj)]

        def scan(s, carry):
            states, chain = carry
            at = pl.ds(s, 8, stride=step)
            v, k = m.xn[g, at, :], m.keep[at, :]
            return tuple(v + (k * r) * a for r, a in zip(decay, states)), chain * k

        zero = jnp.zeros((8, 128), F32)
        states, chain = lax.fori_loop(0, step, scan, ((zero,) * nj, zero + 1.0), unroll=4)
        for j in range(nj):
            m.ends[0, j, :, ln] = states[j]
            m.ends[1, j, :, ln] = power(decay[j], step) * chain

    last = jnp.zeros((nj, width), F32)
    for q in range(8):
        last = m.ends[0, :, q, :] + m.ends[1, :, q, :] * last
    m.end_out[...] = last
    across = remote(m.end_out, m.end_in, m.s_core.at[0], m.r_core.at[0], other)
    across.start()
    line.pump(first_w)
    across.wait()
    last = jnp.where(c == 0, 0.0, m.end_in[...])
    for q in range(8):
        m.starts[:, q, :] = last
        last = m.ends[0, :, q, :] + m.ends[1, :, q, :] * last

    for g in range(groups):
        ln = pl.ds(g * 128, 128)
        decay = [wide(1.0 - m.damp[pl.ds(j, 1), ln]) for j in range(nj)]
        weight = [wide(m.damp[pl.ds(j, 1), ln] * m.eta[pl.ds(j, 1), ln]) for j in range(nj)]

        def scan(s, states):
            at = pl.ds(s, 8, stride=step)
            v, k = m.xn[g, at, :], m.keep[at, :]
            states = tuple(v + (k * r) * a for r, a in zip(decay, states))
            m.mix_pre[g, at, :] = v + tree_sum([w * a for w, a in zip(weight, states)])
            return states

        lax.fori_loop(0, step, scan, tuple(m.starts[j, :, ln] for j in range(nj)), unroll=4)
        pre = m.mix_pre[g]
        m.low_m[:, ln] = (pre * sigmoid(pre)).astype(BF16)
    norm_run.forward()
    mix_run.start()
    out.mix_pre.start()
    line.pump(first_w)
    line.pump(second_w)
    line.own(third_w)
    for o in range(4):

        @pl.when(t == o)
        def _():
            m.normed4[:, o * width : (o + 1) * width] = m.low_n[...]
            m.mixed4[:, o * width : (o + 1) * width] = m.low_m[...]
            m.cot4[:, o * width : (o + 1) * width] = m.cot[...]

    mix_run.forward()
    line.pump(first_w)
    line.pump(second_w)
    line.own(fourth_w)
    norm_run.finish()
    out.normed4.start()
    line.done(first_w)
    for copy in (out.w_shared, out.w_value, out.w_gate):
        copy.start()

    def rows(i):
        return at_block(i, B)

    def mine(i):
        return pl.ds(pl.multiple_of(count + i * B, B), B)

    def window(i):
        return pl.ds(pl.multiple_of(i * B, B), span)

    def kv_run(i):
        return [
            remote(m.keys.at[mine(i)], m.keys.at[rows(i)], m.s_kv.at[2 * i], m.r_kv.at[2 * i], other),
            remote(m.vals.at[mine(i)], m.vals.at[rows(i)], m.s_kv.at[2 * i + 1], m.r_kv.at[2 * i + 1], other),
        ]

    @pl.loop(0, nb)
    def _(i):
        value = dot(m.normed4[rows(i), :], m.w_value[...])
        m.v_pre[rows(i), :] = value.astype(BF16)
        m.vals[mine(i), :] = (value * sigmoid(value)).astype(BF16)
        kv_run(i)[1].start()

    out.v_pre.start()
    mix_run.finish()
    out.mixed4.start()
    cot_run.start()

    @pl.loop(0, nb)
    def _(i):
        pre = dot(m.mixed4[rows(i), :], m.w_shared[...])
        m.s_pre[rows(i), :] = pre
        shared = pre * sigmoid(pre)
        m.queries[rows(i), :] = (shared * m.q_gain[...]).astype(BF16)
        m.keys[mine(i), :] = (shared * m.k_gain[...]).astype(BF16)
        kv_run(i)[0].start()

    @pl.loop(0, nb)
    def _(i):
        m.g_pre[rows(i), :] = dot(m.mixed4[rows(i), :], m.w_gate[...])

    out.g_pre.start()
    line.pump(second_w)
    line.pump(third_w)
    line.pump(fourth_w)
    for i in range(nb):
        for copy in kv_run(i):
            copy.wait()
    out.keys.start()
    out.vals.start()
    line.done(second_w)
    for w in aside:
        if w != "up":
            getattr(m, "w_" + w)[...] = getattr(m, "t_" + w)[...].astype(F32).T.astype(BF16)
    for copy in (out.w_hidden, out.w_attended):
        copy.start()
    upd = [
        remote(m.w_update.at[:, lanes(p)], m.rows_update.at[pl.ds(pl.multiple_of(t * width, width), width)],
               m.s_upd.at[n], m.r_upd.at[n], spot(t=p))
        for n, p in enumerate((x, y, d))
    ]
    for copy in upd:
        copy.start()
    for o in range(4):

        @pl.when(t == o)
        def _():
            m.rows_update[o * width : (o + 1) * width, :] = m.w_update[:, o * width : (o + 1) * width]

    def run_h(i):
        return Scatter(
            2,
            lambda o, n: m.part_h.at[o, pl.ds(pl.multiple_of(i * B + n * half, half), half)],
            lambda n: m.got_h.at[0, i * 2 + n],
            lambda n: m.got_h.at[1, i * 2 + n],
            lambda n: m.got_h.at[2, i * 2 + n],
            m.send, m.recv, 72 + i * 6,
        )

    def attend(i):
        raw = dot_t(m.queries[rows(i), :], m.keys[window(i), :]) * scale
        same = as_column(m.ids_row[:, mine(i)]) == m.ids_row[0:1, window(i)]
        place = lax.broadcasted_iota(jnp.int32, raw.shape, 1) - lax.broadcasted_iota(jnp.int32, raw.shape, 0)
        s = jnp.where(same & (place <= count), raw, -1e30)
        peak = jnp.max(s, axis=1, keepdims=True)
        e = jnp.exp(s - peak)
        total = jnp.sum(e, axis=1, keepdims=True)
        m.log_sum[rows(i), :] = jnp.broadcast_to(peak + jnp.log(total), (B, 128))
        attended = dot((e * (1.0 / total)).astype(BF16), m.vals[window(i), :])
        m.attended[rows(i), :] = attended.astype(BF16)
        gate = m.g_pre[rows(i), :]
        gated = (gate * sigmoid(gate) * attended).astype(BF16)
        m.gated[rows(i), :] = gated
        part = dot(m.mixed4[rows(i), lanes(t)], m.w_hidden[...]) + dot(gated, m.w_attended[...])
        part = part.astype(BF16)
        for o in range(4):
            m.part_h[o, rows(i), :] = part[:, o * width : (o + 1) * width]
        run_h(i).start()

    def collect(i):
        run = run_h(i)
        for n in range(2):
            m.hid_pre[pl.ds(i * B + n * half, half), :] = run.collect(n) + run.part(t, n)[...].astype(F32)
        run.finish()

    def attend_some(start, stop):
        @pl.loop(start, stop)
        def _(i):
            attend(i)

            @pl.when(i > 0)
            def _():
                run_h(i - 1).forward()

    attend_some(0, nb // 2)
    line.pump(third_w)
    line.pump(fourth_w)
    cot_run.forward()
    attend_some(nb // 2, nb)
    line.pump(third_w)
    line.pump(fourth_w)
    out.attended.start()
    out.gated.start()
    for copy in upd:
        copy.wait()

    @pl.loop(0, nb)
    def _(i):
        m.upd_pre[rows(i), :] = dot(m.mixed4[rows(i), :], m.rows_update[...])

    run_h(nb - 1).forward()
    out.upd_pre.start()
    out.rows_update.start()
    line.done(third_w)
    out.w_up.start()
    line.done(fourth_w)
    out.w_down.start()
    for i in range(nb):
        collect(i)
    out.hid_pre.start()
    cot_run.finish()
    out.cot4.start()
    for copy in outs.values():
        copy.wait()


def front(ident, line_count, tok, keep, gain, damp, eta, q_gain, k_gain, ids_row, cot, shards):
    count, width = tok.shape
    groups, nj = width // 128, damp.shape[0]
    nb = count // 256
    turns = [turned(k, s.shape[1]) for k, s in zip(KINDS, shards)]
    shards = [s.T if turn else s for turn, s in zip(turns, shards)]
    kinds = ["row" if turn else k for turn, k in zip(turns, KINDS)]
    sizes = [s.shape[0] if k == "row" else s.shape[1] for k, s in zip(kinds, shards)]
    full = 4 * width
    values = shards[1].shape[1]
    s = jax.ShapeDtypeStruct
    outs = dict(
        rows_update=s((full, width), BF16),
        normed4=s((count, full), BF16),
        mixed4=s((count, full), BF16),
        mix_pre=s((groups, count, 128), F32),
        xn=s((groups, count, 128), F32),
        inv_rows=s((8, count), F32),
        s_pre=s((count, Z), F32),
        v_pre=s((count, values), BF16),
        g_pre=s((count, values), F32),
        keys=s((2 * count, Z), BF16),
        vals=s((2 * count, values), BF16),
        queries=s((count, Z), BF16),
        log_sum=s((count, 128), F32),
        attended=s((count, values), BF16),
        gated=s((count, values), BF16),
        hid_pre=s((count, width), F32),
        upd_pre=s((count, width), F32),
        cot4=s((count, full), BF16),
    )
    aside = []
    for name, kind, size, shard in zip(FRONT_WEIGHTS, kinds, sizes, shards):
        shape = (2 * line_count * size, shard.shape[1]) if kind == "row" else (shard.shape[0], 2 * line_count * size)
        if turns[FRONT_WEIGHTS.index(name)] and name != "down":
            aside.append(pltpu.VMEM(shape, shard.dtype))
            shape = shape[::-1]
        outs["w_" + name] = s(shape, shard.dtype)
    v, dma, k = pltpu.VMEM, pltpu.SemaphoreType.DMA, len(FRONT_WEIGHTS)
    n = 72 + 6 * nb
    scratch = dict(
        low_n=v((count, width), BF16),
        low_m=v((count, width), BF16),
        rows=v((4, 8, count), F32),
        ends=v((2, nj, 8, width), F32),
        starts=v((nj, 8, width), F32),
        end_out=v((nj, width), F32),
        end_in=v((nj, width), F32),
        part_h=v((4, count, width), BF16),
        got_h=v((3, 2 * nb, 128, width), BF16),
        w_update=v(outs["w_update"].shape, BF16),
        send=dma((n,)), recv=dma((n,)), s_rows=dma((3,)), r_rows=dma((3,)), s_core=dma((1,)), r_core=dma((1,)),
        s_upd=dma((3,)), r_upd=dma((3,)), s_kv=dma((2 * nb,)), r_kv=dma((2 * nb,)), s_out=dma((len(A_HBM),)),
        z_here=dma((k,)), z_up=dma((k, line_count)), z_down=dma((k, line_count)), z_core=dma((k, line_count)),
        z_recv=dma((k, line_count)), z_recv_core=dma((k, line_count)),
    )
    got = pl.pallas_call(
        functools.partial(front_kernel, kinds, sizes, turns, line_count),
        out_shape=[outs[n] for n in A_OUT],
        in_specs=[VMEM] * len(A_IN),
        out_specs=[ANY if n in A_HBM else VMEM for n in A_OUT],
        scratch_shapes=[scratch[n] for n in A_SCRATCH] + [v(outs[n].shape, outs[n].dtype) for n in A_HBM] + aside,
        compiler_params=pltpu.CompilerParams(collective_id=ident, has_side_effects=True, vmem_limit_bytes=60 * 2**20),
        name="front",
    )(tok, keep, gain[None], damp, eta, q_gain[None], k_gain[None], ids_row, cot, *shards)
    return Named(A_OUT, got)


class LineSum:
    def __init__(self, kinds, sizes, count, sources, pair, line, outs, sems):
        self.kinds, self.sizes, self.count = kinds, sizes, count
        self.sources, self.pair, self.line, self.outs = sources, pair, line, outs
        self.send_core, self.recv_core, self.send, self.recv = sems
        self.z, self.c = lax.axis_index("fsdp"), lax.axis_index("ctx")
        self.other = spot(c=1 - self.c)

    def block(self, w, owner, core):
        return shard_at(self.sources[w], self.kinds[w], owner * 2 + core, self.sizes[w])

    def across(self, w, owner):
        return remote(
            self.block(w, owner, 1 - self.c), self.pair[w].at[owner],
            self.send_core.at[w, owner], self.recv_core.at[w, owner], self.other,
        )

    def along(self, w, k):
        owner = (self.z + k) % self.count
        far = ((self.z == 0) & (owner == self.count - 1)) | ((self.z == self.count - 1) & (owner == 0))
        to = jnp.where(far, jnp.where(self.z == 0, 1, self.count - 2), owner)
        at = jnp.where(far, self.count, self.z)
        return remote(
            self.pair[w].at[owner], self.line[w].at[at], self.send.at[w, k], self.recv.at[w, at], spot(f=to)
        )

    def helps(self, owner):
        return ((self.z == 1) & (owner == self.count - 1)) | ((self.z == self.count - 2) & (owner == 0))

    def relay(self, w):
        @pl.loop(1, self.count)
        def _(k):
            owner = (self.z + k) % self.count

            @pl.when(self.helps(owner))
            def _():
                got = self.line[w].at[self.count]
                remote(got, got, self.send.at[w, k], self.recv.at[w, self.count], self.other).wait_recv()
                self.pair[w][owner] = (self.pair[w][owner].astype(F32) + got[...].astype(F32)).astype(BF16)
                self.along(w, k).start()

    def start(self, w):
        @pl.loop(1, self.count + 1)
        def _(k):
            self.across(w, (self.z + k) % self.count).start()

    def plus(self, w, owner):
        return self.pair[w][owner].astype(F32) + self.block(w, owner, self.c)[...].astype(F32)

    def send_on(self, w):
        @pl.loop(1, self.count)
        def _(i):
            k = jnp.where(self.z == 0, self.count - i, i)
            owner = (self.z + k) % self.count
            self.across(w, owner).wait_recv()
            self.pair[w][owner] = self.plus(w, owner).astype(BF16)

            @pl.when(jnp.logical_not(self.helps(owner)))
            def _():
                self.along(w, k).start()

    def end(self, w):
        self.across(w, self.z).wait_recv()
        self.outs[w][...] = self.plus(w, self.z)

        @pl.loop(1, self.count)
        def _(k):
            source = (self.z + k) % self.count
            got = self.line[w].at[source]
            merged = ((self.z == 0) & (source == self.count - 1)) | ((self.z == self.count - 1) & (source == 0))

            @pl.when(jnp.logical_not(merged))
            def _():
                remote(got, got, self.send.at[w, k], self.recv.at[w, source], self.other).wait_recv()
                self.outs[w][...] += got[...].astype(F32)

            self.along(w, k).wait_send()

        @pl.loop(0, self.count)
        def _(owner):
            self.across(w, owner).wait_send()


def line_plan(shapes, kinds, count):
    turns = [turned(k, s[1] // (2 * count)) for k, s in zip(kinds, shapes)]
    shapes = [s[::-1] if turn else s for turn, s in zip(turns, shapes)]
    kinds = ["row" if turn else k for turn, k in zip(turns, kinds)]
    sizes = [s[0 if k == "row" else 1] // (2 * count) for k, s in zip(kinds, shapes)]
    blocks = [(n, s[1]) if k == "row" else (s[0], n) for k, n, s in zip(kinds, sizes, shapes)]
    return turns, kinds, sizes, shapes, blocks


def line_peers(count):
    z = lax.axis_index("fsdp")
    return [spot(f=(z + k) % count) for k in range(1, count)]


MID_LOAD = named(
    lambda hid_pre, upd_pre, w_up, w_down, cot4, w_attended, g_pre, attended, w_gate, w_upd,
    w_hidden, queries, keys, vals, log_sum, v_pre: None
)
MID_IN = MID_LOAD + named(lambda tok, cot, f_gain, ids_row: None)
MID_STORE = named(lambda out, part_t, tok_grad, mix_grad, value_grad, hid4, upd_grad, gate_grad: None)
MID_OUT = MID_STORE + named(lambda f_gain_grad, q_grad, k_grad, d_up, d_down: None)
MID_SCRATCH = named(
    lambda block, part_f, up_rows, up_grads, ffn4, att_grad, k_all, v_all, part_g, got_g, low,
    rows_a, rows_b, k_send, v_send, k_got, v_got, p_up, p_down, l_up, l_down, send, recv, s_rows,
    r_rows, s_gr, r_gr, s_in, s_out, c_send, c_recv, l_send, l_recv: None
)


def mid_kernel(kinds, sizes, turn, line_count, *refs):
    m = Named(
        MID_IN + MID_OUT + MID_SCRATCH + ["i_" + n for n in MID_LOAD] + ["o_" + n for n in MID_STORE], refs
    )
    loads, stores = {}, {}
    for k, n in enumerate(MID_LOAD):
        loads[n] = Transfer(pltpu.make_async_copy(getattr(m, n), getattr(m, "i_" + n), m.s_in.at[k]))
        setattr(m, n, getattr(m, "i_" + n))
        loads[n].start()
    for k, n in enumerate(MID_STORE):
        stores[n] = pltpu.make_async_copy(getattr(m, "o_" + n), getattr(m, n), m.s_out.at[k])
        setattr(m, n, getattr(m, "o_" + n))
    load, store = types.SimpleNamespace(**loads), types.SimpleNamespace(**stores)
    t, x, y, d = tp_peers()
    other = spot(c=1 - lax.axis_index("ctx"))
    count, width = m.tok.shape
    hidden = m.w_up.shape[1]
    B = 256
    half, nb, span = B // 2, count // B, count + B
    scale = 1.0 / math.sqrt(Z)

    def rows(i):
        return at_block(i, B)

    def mine(i):
        return pl.ds(count + i * B, B)

    def window(i):
        return pl.ds(i * B, span)

    def lanes(o):
        return pl.ds(pl.multiple_of(o * width, width), width)

    greet([spot(t=x), spot(t=y), spot(t=d), other] + line_peers(line_count))
    m.f_gain_grad[...] = jnp.zeros_like(m.f_gain_grad)

    def gather_run(kind, i, low, place):
        return Gather(
            2,
            lambda n: low.at[pl.ds(i * B + n * half, half)],
            lambda o, n: place.at[pl.ds(i * B + n * half, half), lanes(o)],
            m.send, m.recv, (kind * nb + i) * 6,
        )

    def scatter_run(kind, i, part, got):
        return Scatter(
            2,
            lambda o, n: part.at[o, pl.ds(i * B + n * half, half)],
            lambda n: got.at[0, i * 2 + n],
            lambda n: got.at[1, i * 2 + n],
            lambda n: got.at[2, i * 2 + n],
            m.send, m.recv, (kind * nb + i) * 6,
        )

    run_p = [gather_run(0, i, m.low, m.ffn4) for i in range(nb)]
    run_gh = [gather_run(1, i, m.low, m.hid4) for i in range(nb)]
    run_g = [scatter_run(2, i, m.part_g, m.got_g) for i in range(nb)]
    run_f = [scatter_run(3, i, m.part_f, m.got_g) for i in range(nb)]
    line = LineSum(
        kinds, sizes, line_count, [m.w_up, m.w_down], [m.p_up, m.p_down], [m.l_up, m.l_down], [m.d_up, m.d_down],
        (m.c_send, m.c_recv, m.l_send, m.l_recv),
    )

    def row_run(kind, i, buf):
        return [
            remote(
                buf.at[t, :, rows(i)], buf.at[t, :, rows(i)],
                m.s_rows.at[(kind * nb + i) * 3 + n], m.r_rows.at[(kind * nb + i) * 3 + n], spot(t=p),
            )
            for n, p in enumerate((x, y, d))
        ]

    def row_total(buf, i):
        return buf[0, :, rows(i)] + buf[1, :, rows(i)] + buf[2, :, rows(i)] + buf[3, :, rows(i)]

    def split(part, i, value):
        low = value.astype(BF16)
        for o in range(4):
            part[o, rows(i), :] = low[:, o * width : (o + 1) * width]

    def place_own(full_ref, i):
        for o in range(4):

            @pl.when(t == o)
            def _():
                full_ref[rows(i), o * width : (o + 1) * width] = m.low[rows(i), :]

    def joined(run):
        pieces = [run.collect(n) + run.part(t, n)[...].astype(F32) for n in range(2)]
        return jnp.concatenate(pieces, axis=0)

    def inverse_mid(i):
        return lax.rsqrt(row_total(m.rows_a, i) / D + EPSILON)

    def block_stage(i):
        need(load.hid_pre, load.upd_pre)
        hidden_pre, update = m.hid_pre[rows(i), :], sigmoid(m.upd_pre[rows(i), :])
        block = update * (hidden_pre * sigmoid(hidden_pre)) + (1.0 - update) * m.tok[rows(i), :].astype(F32)
        m.block[rows(i), :] = block
        m.low[rows(i), :] = (block * m.f_gain[...]).astype(BF16)
        run_p[i].start()
        m.rows_a[t, :, rows(i)] = as_rows(jnp.sum(block * block, axis=1, keepdims=True))
        for copy in row_run(0, i, m.rows_a):
            copy.start()
        place_own(m.ffn4, i)

    def up_stage(i):
        need(load.w_up)
        run_p[i].finish()
        raw = dot(m.ffn4[rows(i), :], m.w_up[...])
        part = m.v_all.shape[1]
        parts = hidden // part
        for k in range(parts):
            m.v_all[pl.ds((parts * i + k) * B, B), :] = raw[:, k * part : (k + 1) * part]

    down, down_t = (dot_t, dot) if turn else (dot, dot_t)

    def ffn_stage(i):
        need(load.w_down, load.cot4)
        back = down_t(m.cot4[rows(i), :], m.w_down[...])
        for copy in row_run(0, i, m.rows_a):
            copy.wait()
        inv = as_column(inverse_mid(i))
        parts = hidden // m.v_all.shape[1]
        raw = jnp.concatenate([m.v_all[pl.ds((parts * i + k) * B, B), :] for k in range(parts)], axis=1)
        up_pre = raw * inv
        sig = sigmoid(up_pre)
        grad_up = (back * d_silu(up_pre, sig)).astype(BF16)
        split(m.part_g, i, dot_t(grad_up, m.w_up[...]))
        run_g[i].start()
        wide_grad = grad_up.astype(F32)
        m.up_grads[rows(i), :] = (wide_grad * inv).astype(BF16)
        m.rows_b[t, :, rows(i)] = as_rows(jnp.sum(wide_grad * raw, axis=1, keepdims=True))
        for copy in row_run(1, i, m.rows_b):
            copy.start()
        up_rows = (up_pre * sig).astype(BF16)
        m.up_rows[rows(i), :] = up_rows
        split(m.part_f, i, down(up_rows, m.w_down[...]))

    def grad_stage(i):
        grad_ffn = joined(run_g[i])
        for copy in row_run(1, i, m.rows_b):
            copy.wait()
        block = m.block[rows(i), :]
        inv_rows = inverse_mid(i)
        factor = inv_rows * inv_rows * inv_rows * row_total(m.rows_b, i) / D
        inv = as_column(inv_rows)
        grad_block = (
            m.cot[rows(i), :].astype(F32) + inv * (grad_ffn * m.f_gain[...]) - block * as_column(factor)
        )
        m.f_gain_grad[...] += jnp.sum(grad_ffn * block * inv, axis=0, keepdims=True)
        hidden_pre, update = m.hid_pre[rows(i), :], sigmoid(m.upd_pre[rows(i), :])
        sig = sigmoid(hidden_pre)
        m.low[rows(i), :] = (grad_block * update * d_silu(hidden_pre, sig)).astype(BF16)
        run_gh[i].start()
        keep = grad_block * (1.0 - update)
        m.tok_grad[rows(i), :] = keep
        tokens = m.tok[rows(i), :].astype(F32)
        m.upd_grad[rows(i), :] = (keep * (hidden_pre * sig - tokens) * update).astype(BF16)
        place_own(m.hid4, i)
        run_g[i].finish()

    def gate_stage(i):
        need(load.w_attended, load.g_pre, load.attended, load.w_gate, load.w_upd, load.w_hidden)
        run_gh[i].finish()
        grad_hidden = m.hid4[rows(i), :]
        grad_gated = dot_t(grad_hidden, m.w_attended[...])
        gate = m.g_pre[rows(i), :]
        sig = sigmoid(gate)
        grad_gate = (grad_gated * m.attended[rows(i), :].astype(F32) * d_silu(gate, sig)).astype(BF16)
        m.gate_grad[rows(i), :] = grad_gate
        split(m.part_t, i, dot_t(grad_gate, m.w_gate[...]) + dot_t(m.upd_grad[rows(i), :], m.w_upd[...]))
        m.att_grad[rows(i), :] = (grad_gated * (gate * sig)).astype(BF16)
        m.mix_grad[rows(i), :] = dot_t(grad_hidden, m.w_hidden[...])

    def grads_run(i):
        return [
            remote(m.k_send.at[rows(i)], m.k_got.at[rows(i)], m.s_gr.at[2 * i], m.r_gr.at[2 * i], other),
            remote(m.v_send.at[rows(i)], m.v_got.at[rows(i)], m.s_gr.at[2 * i + 1], m.r_gr.at[2 * i + 1], other),
        ]

    def attend_back(i):
        need(load.queries, load.keys, load.vals, load.log_sum)
        raw = dot_t(m.queries[rows(i), :], m.keys[window(i), :]) * scale
        same = as_column(m.ids_row[:, mine(i)]) == m.ids_row[0:1, window(i)]
        place = lax.broadcasted_iota(jnp.int32, raw.shape, 1) - lax.broadcasted_iota(jnp.int32, raw.shape, 0)
        exact = jnp.exp(jnp.where(same & (place <= count), raw, -1e30) - m.log_sum[rows(i), 0:1])
        grad_rows = m.att_grad[rows(i), :]
        value_part = t_dot(exact.astype(BF16), grad_rows)
        grad_probs = dot_t(grad_rows, m.vals[window(i), :])
        inner = jnp.sum(exact * grad_probs, axis=1, keepdims=True)
        grad_scores = exact * (grad_probs - inner) * scale
        high = grad_scores.astype(BF16)
        rest = (grad_scores - high.astype(F32)).astype(BF16)
        keys, queries = m.keys[window(i), :], m.queries[rows(i), :]
        m.q_grad[rows(i), :] = dot(high, keys) + dot(rest, keys)
        key_part = t_dot(high, queries) + t_dot(rest, queries)
        if i == 0:
            m.v_all[window(0), :] = value_part
            m.k_all[window(0), :] = key_part
        else:
            old, new = pl.ds(i * B, span - B), pl.ds(span + (i - 1) * B, B)
            m.v_all[old, :] += value_part[: span - B]
            m.v_all[new, :] = value_part[span - B :]
            m.k_all[old, :] += key_part[: span - B]
            m.k_all[new, :] = key_part[span - B :]
        m.k_send[rows(i), :] = m.k_all[rows(i), :].astype(BF16)
        m.v_send[rows(i), :] = m.v_all[rows(i), :].astype(BF16)
        for copy in grads_run(i):
            copy.start()

    def product(dst, left, right):
        for k in range(right.shape[1] // B):
            at = slice(k * B, (k + 1) * B)
            dst[:, at] = t_dot(left[...], right[:, at]).astype(BF16)

    def key_end(i):
        need(load.v_pre)
        for copy in grads_run(i):
            copy.wait()
        m.k_grad[rows(i), :] = m.k_all[mine(i), :] + m.k_got[rows(i), :].astype(F32)
        value = m.v_pre[rows(i), :].astype(F32)
        grad = m.v_all[mine(i), :] + m.v_got[rows(i), :].astype(F32)
        m.value_grad[rows(i), :] = (grad * d_silu(value, sigmoid(value))).astype(BF16)

    block_stage(0)
    block_stage(1)
    run_p[0].forward()
    block_stage(2)
    run_p[1].forward()
    block_stage(3)
    run_p[2].forward()
    up_stage(0)
    ffn_stage(0)
    run_p[3].forward()
    up_stage(1)
    ffn_stage(1)
    run_g[0].forward()
    up_stage(2)
    ffn_stage(2)
    up_stage(3)
    run_g[1].forward()
    grad_stage(0)
    ffn_stage(3)
    run_g[2].forward()
    grad_stage(1)
    run_gh[0].forward()
    if turn:
        product(m.w_down, m.cot4, m.up_rows)
    else:
        product(m.w_down, m.up_rows, m.cot4)
    line.start(1)
    run_g[3].forward()
    grad_stage(2)
    run_gh[1].forward()
    product(m.w_up, m.ffn4, m.up_grads)
    line.start(0)
    line.send_on(1)
    grad_stage(3)
    run_gh[2].forward()
    gate_stage(0)
    line.send_on(0)
    run_gh[3].forward()
    run_f[0].start()
    run_f[1].start()
    gate_stage(1)
    attend_back(0)
    gate_stage(2)
    run_f[0].forward()
    run_f[2].start()
    line.relay(1)
    gate_stage(3)
    store.hid4.start()
    store.upd_grad.start()
    store.gate_grad.start()
    store.tok_grad.start()
    store.part_t.start()
    store.mix_grad.start()
    run_f[1].forward()
    run_f[3].start()
    attend_back(1)
    run_f[2].forward()
    attend_back(2)
    run_f[3].forward()
    line.relay(0)
    attend_back(3)
    key_end(0)
    key_end(1)
    key_end(2)
    key_end(3)
    store.value_grad.start()
    for i in range(nb):
        m.out[rows(i), :] = (m.block[rows(i), :] + joined(run_f[i])).astype(BF16)
        run_f[i].finish()
    store.out.start()
    line.end(1)
    line.end(0)
    for copy in stores.values():
        copy.wait()


def middle(ident, line_count, ins):
    tok, f_gain = ins["tok"], ins["f_gain"]
    count, width = tok.shape
    full = 4 * width
    values, hidden = ins["w_gate"].shape[1], ins["w_up"].shape[1]
    nb = count // 256
    (_, turn), kinds, sizes, _, blocks = line_plan([(full, hidden), (hidden, full)], KINDS[-2:], line_count)
    dma, s, v = pltpu.SemaphoreType.DMA, jax.ShapeDtypeStruct, pltpu.VMEM
    outs = dict(
        out=s((count, width), BF16),
        part_t=s((4, count, width), BF16),
        tok_grad=s((count, width), F32),
        mix_grad=s((count, width), F32),
        value_grad=s((count, values), BF16),
        hid4=s((count, full), BF16),
        upd_grad=s((count, width), BF16),
        gate_grad=s((count, values), BF16),
        f_gain_grad=s((1, width), F32),
        q_grad=s((count, Z), F32),
        k_grad=s((count, Z), F32),
        d_up=s(blocks[0], F32),
        d_down=s(blocks[1], F32),
    )
    scratch = dict(
        block=v((count, width), F32),
        part_f=v((4, count, width), BF16),
        up_rows=v((count, hidden), BF16),
        up_grads=v((count, hidden), BF16),
        ffn4=v((count, full), BF16),
        att_grad=v((count, values), BF16),
        k_all=v((2 * count, Z), F32),
        v_all=v((2 * count, values), F32),
        part_g=v((4, count, width), BF16),
        got_g=v((3, 2 * nb, 128, width), BF16),
        low=v((count, width), BF16),
        rows_a=v((4, 8, count), F32),
        rows_b=v((4, 8, count), F32),
        k_send=v((count, Z), BF16),
        v_send=v((count, values), BF16),
        k_got=v((count, Z), BF16),
        v_got=v((count, values), BF16),
        p_up=v((line_count,) + blocks[0], BF16),
        p_down=v((line_count,) + blocks[1], BF16),
        l_up=v((line_count + 1,) + blocks[0], BF16),
        l_down=v((line_count + 1,) + blocks[1], BF16),
        c_send=dma((2, line_count)), c_recv=dma((2, line_count)),
        l_send=dma((2, line_count)), l_recv=dma((2, line_count + 1)),
        send=dma((24 * nb,)), recv=dma((24 * nb,)),
        s_rows=dma((6 * nb,)), r_rows=dma((6 * nb,)),
        s_gr=dma((2 * nb,)), r_gr=dma((2 * nb,)),
        s_in=dma((len(MID_LOAD),)), s_out=dma((len(MID_STORE),)),
    )
    got_all = pl.pallas_call(
        functools.partial(mid_kernel, kinds, sizes, turn, line_count),
        out_shape=[outs[n] for n in MID_OUT],
        in_specs=[ANY if n in MID_LOAD else VMEM for n in MID_IN],
        out_specs=[ANY if n in MID_STORE else VMEM for n in MID_OUT],
        scratch_shapes=[scratch[n] for n in MID_SCRATCH]
        + [v(ins[n].shape, ins[n].dtype) for n in MID_LOAD]
        + [v(outs[n].shape, outs[n].dtype) for n in MID_STORE],
        compiler_params=pltpu.CompilerParams(collective_id=ident, has_side_effects=True, vmem_limit_bytes=62 * 2**20),
        name="middle",
    )(*[ins[n] for n in MID_IN])
    got_all = Named(MID_OUT, got_all)
    if turn:
        got_all.d_down = got_all.d_down.T
    return got_all


REAR_LOAD = named(
    lambda part_t, value_grad, w_value, gated, hid4, mixed4, upd_grad, gate_grad, normed4, mix_grad,
    mix_pre, xn, tok_grad: None
)
REAR_IN = REAR_LOAD + named(
    lambda q_grad, k_grad, s_pre, w_shared, tok, inv_rows, keep_next, gain, damp, eta, q_gain,
    k_gain, f_gain_grad: None
)
REAR_WEIGHTS = WEIGHTS[:-2]
REAR_OUT = named(lambda grad_in, small: None) + ["d_" + w for w in REAR_WEIGHTS]
REAR_SCRATCH = named(
    lambda part_v, got_v, got_t, part_s, got_s, low_s, full_s, grad_mix, back, rows, ends, starts,
    end_out, end_in, small_core, small_all, own_q, all_q, upd_cols, send, recv, s_rows, r_rows,
    s_core, r_core, s_upd, r_upd, s_small, r_small, s_q, r_q, s_in, c_send, c_recv, l_send, l_recv:
    None
)


def rear_kernel(kinds, sizes, turns, line_count, *refs):
    groups_of = [p + w for p in ("p_", "l_", "g_") for w in REAR_WEIGHTS]
    m = Named(REAR_IN + REAR_OUT + REAR_SCRATCH + groups_of + ["i_" + n for n in REAR_LOAD], refs)
    loads = {}
    for k, n in enumerate(REAR_LOAD):
        loads[n] = Transfer(pltpu.make_async_copy(getattr(m, n), getattr(m, "i_" + n), m.s_in.at[k]))
        setattr(m, n, getattr(m, "i_" + n))
        loads[n].start()
    load = types.SimpleNamespace(**loads)
    t, x, y, d = tp_peers()
    z, c = lax.axis_index("fsdp"), lax.axis_index("ctx")
    other = spot(c=1 - c)
    groups, count = m.xn.shape[0], m.xn.shape[1]
    step, nj, width = count // 8, m.damp.shape[0], m.damp.shape[1]
    B = 256
    half, nb = B // 2, count // B
    part = min(16, nj)
    zero = jnp.zeros((8, 128), F32)

    def lanes(o):
        return pl.ds(pl.multiple_of(o * width, width), width)

    line = LineSum(
        kinds, sizes, line_count,
        [getattr(m, "g_" + w) for w in REAR_WEIGHTS], [getattr(m, "p_" + w) for w in REAR_WEIGHTS],
        [getattr(m, "l_" + w) for w in REAR_WEIGHTS], [getattr(m, "d_" + w) for w in REAR_WEIGHTS],
        (m.c_send, m.c_recv, m.l_send, m.l_recv),
    )
    m.end_in[...] = jnp.zeros_like(m.end_in)
    greet([spot(t=x), spot(t=y), spot(t=d), other] + line_peers(line_count))

    run_s = Scatter(
        2,
        lambda o, n: m.part_s.at[pl.ds(pl.multiple_of(o * B + n * half, half), half)],
        lambda n: m.got_s.at[0, n], lambda n: m.got_s.at[1, n], lambda n: m.got_s.at[2, n],
        m.send, m.recv, 0,
    )
    run_full = Gather(
        2,
        lambda n: m.low_s.at[pl.ds(n * half, half)],
        lambda o, n: m.full_s.at[pl.ds(pl.multiple_of(o * B + n * half, half), half)],
        m.send, m.recv, 6,
    )

    def scatter_runs(kind, parts, got):
        return [
            Scatter(
                2,
                lambda o, n, i=i: parts.at[o, pl.ds(i * B + n * half, half)],
                lambda n, i=i: got.at[0, i * 2 + n],
                lambda n, i=i: got.at[1, i * 2 + n],
                lambda n, i=i: got.at[2, i * 2 + n],
                m.send, m.recv, 12 + 6 * (kind * nb + i),
            )
            for i in range(nb)
        ]

    run_t, run_v = (
        scatter_runs(k, parts, got)
        for k, (parts, got) in enumerate(((m.part_t, m.got_t), (m.part_v, m.got_v)))
    )

    m.part_s[...] = (m.q_grad[...] * m.q_gain[...] + m.k_grad[...] * m.k_gain[...]).astype(BF16)
    run_s.start()
    shared = m.s_pre[...] * sigmoid(m.s_pre[...])
    m.own_q[...] = jnp.zeros_like(m.own_q)
    m.own_q[0:1, 0:Z] = jnp.sum(shared * m.q_grad[...], axis=0, keepdims=True)
    m.own_q[0:1, Z:] = jnp.sum(shared * m.k_grad[...], axis=0, keepdims=True)
    m.all_q[t] = m.own_q[...]
    gains = [
        remote(m.own_q, m.all_q.at[t], m.s_q.at[k], m.r_q.at[k], spot(t=p)) for k, p in enumerate((x, y, d))
    ]
    for copy in gains:
        copy.start()
    need(load.part_t)
    run_t[0].start()
    run_t[1].start()
    def value_part(i):
        rows = slice(i * B, (i + 1) * B)
        low = dot_t(m.value_grad[rows, :], m.w_value[...]).astype(BF16)
        for o in range(4):
            m.part_v[o, rows, :] = low[:, o * width : (o + 1) * width]

    def product(w, left, right):
        dst = getattr(m, "g_" + w)
        if turns[REAR_WEIGHTS.index(w)]:
            left, right = right, left
        size = min(256, right.shape[1])
        for k in range(right.shape[1] // size):
            at = slice(k * size, (k + 1) * size)
            dst[:, at] = t_dot(left, right[:, at]).astype(BF16)

    at_w = {w: k for k, w in enumerate(REAR_WEIGHTS)}

    need(load.value_grad, load.w_value)

    def value_part(i):
        rows = slice(i * B, (i + 1) * B)
        low = dot_t(m.value_grad[rows, :], m.w_value[...]).astype(BF16)
        for o in range(4):
            m.part_v[o, rows, :] = low[:, o * width : (o + 1) * width]

    need(load.gated, load.hid4)
    product("attended", m.gated[...], m.hid4[...])
    line.start(at_w["attended"])
    run_s.forward()
    run_t[0].forward()
    run_t[2].start()
    run_t[1].forward()
    run_t[3].start()
    need(load.mixed4, load.upd_grad)
    product("hidden", m.mixed4[:, lanes(t)], m.hid4[...])
    line.start(at_w["hidden"])
    quarter = pl.ds(pl.multiple_of(t * B, B), B)
    for n in range(2):
        total = run_s.collect(n) + run_s.part(t, n)[...].astype(F32)
        pre = m.s_pre[pl.ds(pl.multiple_of(t * B + n * half, half), half), :]
        m.low_s[n * half : (n + 1) * half, :] = (total * d_silu(pre, sigmoid(pre))).astype(BF16)
    run_full.start()
    m.full_s[quarter, :] = m.low_s[...]
    run_t[2].forward()
    line.send_on(at_w["attended"])
    turn_update = turns[at_w["update"]]
    if turn_update:
        m.upd_cols[...] = t_dot(m.upd_grad[...], m.mixed4[...]).astype(BF16)
    else:
        m.upd_cols[...] = t_dot(m.mixed4[...], m.upd_grad[...]).astype(BF16)

    def ends_of(p):
        if turn_update:
            return m.upd_cols.at[:, lanes(p)], m.g_update.at[lanes(t)]
        return m.upd_cols.at[lanes(p)], m.g_update.at[:, lanes(t)]

    turn_copies = [
        remote(*ends_of(p), m.s_upd.at[k], m.r_upd.at[k], spot(t=p)) for k, p in enumerate((x, y, d))
    ] + [pltpu.make_async_copy(*ends_of(t), m.s_upd.at[3])]
    for copy in turn_copies:
        copy.start()
    run_t[3].forward()
    run_full.forward()
    need(load.value_grad, load.w_value)
    value_part(0)
    run_v[0].start()
    value_part(1)
    run_v[1].start()
    line.send_on(at_w["hidden"])
    need(load.gate_grad, load.normed4)
    product("gate", m.mixed4[...], m.gate_grad[...])
    line.start(at_w["gate"])
    value_part(2)
    value_part(3)
    run_s.finish()
    run_full.finish()
    product("shared", m.mixed4[...], m.full_s[...])
    line.start(at_w["shared"])
    run_v[0].forward()
    run_v[2].start()
    for copy in turn_copies:
        copy.wait()
    line.start(at_w["update"])
    product("value", m.normed4[...], m.value_grad[...])
    line.start(at_w["value"])
    line.send_on(at_w["gate"])
    run_v[1].forward()
    run_v[3].start()
    line.send_on(at_w["update"])
    need(load.mix_grad, load.mix_pre, load.xn, load.tok_grad)
    own_shared = m.w_shared[lanes(t), :]
    for i in range(nb):
        for n in range(2):
            at = pl.ds(i * B + n * half, half)
            mix = m.mix_grad[at, :] + run_t[i].collect(n) + run_t[i].part(t, n)[...].astype(F32)
            mix = mix + dot_t(m.full_s[at, :], own_shared)
            for g in range(groups):
                pre = m.mix_pre[g, at, :]
                m.grad_mix[g, at, :] = mix[:, g * 128 : (g + 1) * 128] * d_silu(pre, sigmoid(pre))
        run_t[i].finish()
    line.send_on(at_w["shared"])
    line.send_on(at_w["value"])

    def later(*steps):
        return list(steps)

    def relay(*names):
        def run():
            for name in names:
                line.relay(at_w[name])

        return run

    waiting = later(
        run_v[2].forward, run_v[3].forward, relay("attended"), relay("hidden"), relay("gate"),
        relay("update"), relay("shared"), relay("value"),
    )

    def go(count):
        for _ in range(min(count, len(waiting))):
            waiting.pop(0)()

    for g in range(groups):
        ln = pl.ds(g * 128, 128)
        for j0 in range(0, nj, part):
            decay = [wide(1.0 - m.damp[pl.ds(j, 1), ln]) for j in range(j0, j0 + part)]

            def scan(i, carry):
                a, w, chain = carry
                at = pl.ds(step - 1 - i, 8, stride=step)
                v, k = m.grad_mix[g, at, :], m.keep_next[at, :]
                held = [k * r for r in decay]
                w = tuple(k * p + r * q for p, r, q in zip(a, held, w))
                a = tuple(v + r * p for r, p in zip(held, a))
                return a, w, chain * k

            a, w, chain = lax.fori_loop(0, step, scan, ((zero,) * part, (zero,) * part, zero + 1.0), unroll=8)
            for n in range(part):
                less = power(decay[n], step - 1)
                m.ends[0, j0 + n, :, ln] = a[n]
                m.ends[1, j0 + n, :, ln] = w[n]
                m.ends[2, j0 + n, :, ln] = less * decay[n] * chain
                m.ends[3, j0 + n, :, ln] = float(step) * less * chain
            go(2)

    def merge(q, a, w):
        return (
            m.ends[0, :, q, :] + m.ends[2, :, q, :] * a,
            m.ends[1, :, q, :] + m.ends[2, :, q, :] * w + m.ends[3, :, q, :] * a,
        )

    a = w = jnp.zeros((nj, width), F32)
    for q in range(7, -1, -1):
        a, w = merge(q, a, w)
    m.end_out[0] = a
    m.end_out[1] = w
    across = remote(m.end_out, m.end_in, m.s_core.at[0], m.r_core.at[0], other)
    across.start()
    across.wait()
    a, w = jnp.where(c == 0, m.end_in[0], 0.0), jnp.where(c == 0, m.end_in[1], 0.0)
    for q in range(7, -1, -1):
        m.starts[0, :, q, :] = a
        m.starts[1, :, q, :] = w
        a, w = merge(q, a, w)

    for g in range(groups):
        ln = pl.ds(g * 128, 128)
        for j0 in range(0, nj, part):
            span = range(j0, j0 + part)
            decay = [wide(1.0 - m.damp[pl.ds(j, 1), ln]) for j in span]
            weight = [wide(m.damp[pl.ds(j, 1), ln] * m.eta[pl.ds(j, 1), ln]) for j in span]

            def scan(i, carry):
                a, w, sum_a, sum_w = carry
                at = pl.ds(step - 1 - i, 8, stride=step)
                v, k, u = m.grad_mix[g, at, :], m.keep_next[at, :], m.xn[g, at, :]
                held = [k * r for r in decay]
                w = tuple(k * p + r * q for p, r, q in zip(a, held, w))
                a = tuple(v + r * p for r, p in zip(held, a))
                sum_a = tuple(s + u * p for s, p in zip(sum_a, a))
                sum_w = tuple(s + u * p for s, p in zip(sum_w, w))
                base = v if j0 == 0 else m.back[g, at, :]
                m.back[g, at, :] = base + tree_sum([r * p for r, p in zip(weight, a)])
                return a, w, sum_a, sum_w

            first = (tuple(m.starts[0, j, :, ln] for j in span), tuple(m.starts[1, j, :, ln] for j in span))
            _, _, sum_a, sum_w = lax.fori_loop(
                0, step, scan, first + ((zero,) * part, (zero,) * part), unroll=8
            )
            for n, j in enumerate(span):
                at = pl.ds(j, 1)
                all_a = jnp.sum(sum_a[n], axis=0, keepdims=True)
                all_w = jnp.sum(sum_w[n], axis=0, keepdims=True)
                rate = m.damp[at, ln]
                m.small[at, ln] = m.eta[at, ln] * (all_a - rate * all_w)
                m.small[pl.ds(nj + j, 1), ln] = rate * all_a
            go(2)

    go(len(waiting))
    inv = m.inv_rows[...].T[:, 0:1]
    value = m.tok[...].astype(F32)
    for i in range(nb):
        for n in range(2):
            at = pl.ds(i * B + n * half, half)
            got = run_v[i].collect(n) + run_v[i].part(t, n)[...].astype(F32)
            m.grad_in[at, :] = got + jnp.concatenate([m.back[g, at, :] for g in range(groups)], axis=1)
        run_v[i].finish()
    grad_normed = m.grad_in[...]
    m.small[2 * nj :, :] = jnp.zeros((m.small.shape[0] - 2 * nj, width), F32)
    m.small[2 * nj : 2 * nj + 1, :] = jnp.sum(grad_normed * value * inv, axis=0, keepdims=True)
    m.small[2 * nj + 1 : 2 * nj + 2, :] = m.f_gain_grad[...]
    for copy in gains:
        copy.wait()
    m.small[2 * nj + 2 : 2 * nj + 3, :] = (
        m.all_q[0, 0:1] + m.all_q[1, 0:1] + m.all_q[2, 0:1] + m.all_q[3, 0:1]
    )
    scaled = grad_normed * m.gain[...]
    m.rows[t] = row_sums(scaled * value)
    sums = row_exchange(m.rows, m.s_rows, m.r_rows)
    pair = remote(m.small, m.small_core, m.s_small.at[0], m.r_small.at[0], other)
    for copy in sums + [pair]:
        copy.start()
    m.grad_in[...] = m.tok_grad[...] + inv * scaled
    pair.wait()
    m.small_all[z] = m.small[...] + m.small_core[...]
    wide_sums = [
        remote(
            m.small_all.at[z], m.small_all.at[z], m.s_small.at[k], m.r_small.at[k], spot(f=(z + k) % line_count)
        )
        for k in range(1, line_count)
    ]
    for copy in wide_sums:
        copy.start()
    for copy in sums:
        copy.wait()
    factor = m.inv_rows[...]
    factor = factor * factor * factor * (m.rows[0] + m.rows[1] + m.rows[2] + m.rows[3]) / D
    m.grad_in[...] -= value * factor.T[:, 0:1]
    for copy in wide_sums:
        copy.wait()
    total = m.small_all[0]
    for k in range(1, line_count):
        total = total + m.small_all[k]
    m.small[...] = total
    for w in ("attended", "hidden", "gate", "update", "shared", "value"):
        line.end(at_w[w])


def rear(ident, line_count, ins):
    count, width = ins["tok"].shape
    groups, nj = width // 128, ins["damp"].shape[0]
    full = 4 * width
    nb = count // 256
    values = ins["value_grad"].shape[1]
    shapes = [(full, Z), (full, values), (full, values), (width, full), (values, full), (width, full)]
    turns, kinds, sizes, shapes, blocks = line_plan(shapes, KINDS[:-2], line_count)
    dma, s, v, k = pltpu.SemaphoreType.DMA, jax.ShapeDtypeStruct, pltpu.VMEM, len(REAR_WEIGHTS)
    tall = 2 * nj + 8
    n = 12 + 12 * nb
    lanes = v((groups, count, 128), F32)
    got = v((3, 2 * nb, 128, width), BF16)
    scratch = dict(
        part_v=v((4, count, width), BF16),
        got_v=got, got_t=got,
        part_s=v((count, Z), BF16),
        got_s=v((3, 2, 128, Z), BF16),
        low_s=v((256, Z), BF16),
        full_s=v((count, Z), BF16),
        grad_mix=lanes, back=lanes,
        rows=v((4, 8, count), F32),
        ends=v((4, nj, 8, width), F32),
        starts=v((2, nj, 8, width), F32),
        end_out=v((2, nj, width), F32),
        end_in=v((2, nj, width), F32),
        small_core=v((tall, width), F32),
        small_all=v((line_count, tall, width), F32),
        own_q=v((8, width), F32),
        all_q=v((4, 8, width), F32),
        upd_cols=v((width, full) if turns[REAR_WEIGHTS.index("update")] else (full, width), BF16),
        send=dma((n,)), recv=dma((n,)), s_rows=dma((3,)), r_rows=dma((3,)), s_core=dma((1,)), r_core=dma((1,)),
        s_upd=dma((4,)), r_upd=dma((3,)), s_small=dma((line_count,)), r_small=dma((line_count,)),
        s_q=dma((3,)), r_q=dma((3,)), s_in=dma((len(REAR_LOAD),)),
        c_send=dma((k, line_count)), c_recv=dma((k, line_count)),
        l_send=dma((k, line_count)), l_recv=dma((k, line_count + 1)),
    )
    got = pl.pallas_call(
        functools.partial(rear_kernel, kinds, sizes, turns, line_count),
        out_shape=[s((count, width), F32), s((tall, width), F32)] + [s(b, F32) for b in blocks],
        in_specs=[ANY if name in REAR_LOAD else VMEM for name in REAR_IN],
        out_specs=[VMEM] * len(REAR_OUT),
        scratch_shapes=[scratch[name] for name in REAR_SCRATCH]
        + [v((line_count,) + b, BF16) for b in blocks]
        + [v((line_count + 1,) + b, BF16) for b in blocks]
        + [v(shape, BF16) for shape in shapes]
        + [v(ins[name].shape, ins[name].dtype) for name in REAR_LOAD],
        compiler_params=pltpu.CompilerParams(collective_id=ident, has_side_effects=True, vmem_limit_bytes=62 * 2**20),
        name="rear",
    )(*[ins[name] for name in REAR_IN])
    grads = [g.T if turn else g for turn, g in zip(turns, got[2:])]
    return got[0], got[1], grads


def on_device(
    line_count,
    layer_input, segment_ids, cotangent, norm_gain, ema_damping, ema_eta, query_gain, key_gain,
    ffn_gain, *weights,
):
    tok, cot = layer_input[0], cotangent[0]
    segment = segment_ids[0]
    row_count = tok.shape[0]
    core = lax.axis_index("ctx")
    offset = core * row_count
    all_ids = lax.all_gather(segment, "ctx", axis=0, tiled=True)
    same = jnp.concatenate(
        [jnp.zeros((1,), F32), (all_ids[1:] == all_ids[:-1]).astype(F32), jnp.zeros((1,), F32)]
    )
    keep = lax.dynamic_slice_in_dim(same, offset, row_count, 0)
    keep_next = lax.dynamic_slice_in_dim(same, offset + 1, row_count, 0)
    keep_wide = jnp.broadcast_to(keep[:, None], (row_count, 128))
    next_wide = jnp.broadcast_to(keep_next[:, None], (row_count, 128))
    prev_ids = jnp.where(core > 0, all_ids[:row_count], -1)
    ids_row = jnp.broadcast_to(jnp.concatenate([prev_ids, segment]).astype(F32)[None], (8, 2 * row_count))
    a = front(
        1, line_count, tok, keep_wide, norm_gain, ema_damping, ema_eta, query_gain, key_gain, ids_row, cot, weights
    )
    ins = {n: getattr(a, n) for n in MID_LOAD if n != "w_upd"}
    ins.update(w_upd=a.rows_update, tok=tok, cot=cot, f_gain=ffn_gain[None], ids_row=ids_row)
    m = middle(2, line_count, ins)
    ins = {n: getattr(m if n in MID_OUT else a, n) for n in REAR_IN if n in MID_OUT or n in A_OUT}
    ins.update(
        tok=tok, keep_next=next_wide, gain=norm_gain[None], damp=ema_damping, eta=ema_eta,
        q_gain=query_gain[None], k_gain=key_gain[None],
    )
    grad_in, small, grads = rear(3, line_count, ins)
    n = ema_damping.shape[0]
    return (
        m.out[None], grad_in[None], small[2 * n], small[:n], small[n : 2 * n],
        small[2 * n + 2, :Z], small[2 * n + 2, Z:], small[2 * n + 1], *grads, m.d_up, m.d_down,
    )


def solution(mesh):
    token = P("fsdp", "ctx", "tp")
    row, col = P(("fsdp", "ctx"), "tp"), P("tp", ("fsdp", "ctx"))
    shared = P(("fsdp", "ctx"), None)
    weights = (shared, row, row, col, col, col, row, col)
    small = P(None, "tp")
    return jax.shard_map(
        functools.partial(on_device, mesh.shape["fsdp"]),
        mesh=mesh,
        in_specs=(token, P("fsdp", "ctx"), token, P("tp"), small, small, P(), P(), P("tp")) + weights,
        out_specs=(token, token, P("tp"), small, small, P(), P(), P("tp")) + weights,
        check_vma=False,
    )
```

```python
import functools
import inspect
import math
import types

import jax
import jax.numpy as jnp
from jax import lax
from jax.experimental import pallas as pl
from jax.experimental.pallas import tpu as pltpu
from jax.sharding import PartitionSpec as P

D = 1024
Z = 128
EPSILON = 1e-06
MESH = pl.DeviceIdType.MESH
F32 = jnp.float32
BF16 = jnp.bfloat16
VMEM = pl.BlockSpec(memory_space=pltpu.VMEM)
ANY = pl.BlockSpec(memory_space=pl.ANY)
HIGH = lax.Precision.HIGHEST


def named(signature):
    return list(inspect.signature(signature).parameters)


def spot(f=None, c=None, t=None):
    return (
        lax.axis_index("fsdp") if f is None else f,
        lax.axis_index("ctx") if c is None else c,
        lax.axis_index("tp") if t is None else t,
    )


def greet(devices):
    barrier = pltpu.get_barrier_semaphore()
    for device in devices:
        pl.semaphore_signal(barrier, inc=1, device_id=device, device_id_type=MESH)
    pl.semaphore_wait(barrier, len(devices))


def tp_peers():
    t = lax.axis_index("tp")
    return t, t + 1 - 2 * (t % 2), (t + 2) % 4, 3 - t


def remote(src, dst, send, recv, device):
    return pltpu.make_async_remote_copy(
        src_ref=src, dst_ref=dst, send_sem=send, recv_sem=recv, device_id=device, device_id_type=MESH
    )


class Gather:
    def __init__(self, count, source, place, send, recv, base=0):
        self.count, self.half = count, count // 2
        self.source, self.place, self.send, self.recv, self.base = source, place, send, recv, base
        self.t, self.x, self.y, _ = tp_peers()

    def copy(self, src, owner, i, way, to):
        n = self.base + way * self.count + i
        return remote(src, self.place(owner, i), self.send.at[n], self.recv.at[n], spot(t=to))

    def first(self, i, way):
        return self.copy(self.source(i), self.t, i, way, self.x if way == 0 else self.y)

    def start(self):
        for k in range(self.half):
            self.first(k, 0).start()
            self.first(k + self.half, 1).start()
        for k in range(self.half):
            self.first(k + self.half, 0).start()
            self.first(k, 1).start()

    def onward(self, i):
        if i < self.half:
            return self.copy(self.place(self.x, i), self.x, i, 2, self.y)
        return self.copy(self.place(self.y, i), self.y, i, 2, self.x)

    def begin(self, k):
        self.first(k, 0).start()
        self.first(k + self.half, 1).start()
        self.first(k + self.half, 0).start()
        self.first(k, 1).start()

    def pass_on(self, k):
        self.first(k, 0).wait_recv()
        self.onward(k).start()
        self.first(k + self.half, 1).wait_recv()
        self.onward(k + self.half).start()

    def forward(self):
        for k in range(self.half):
            self.pass_on(k)

    def finish(self):
        for k in range(self.half):
            self.first(k + self.half, 0).wait_recv()
            self.first(k, 1).wait_recv()
        for i in range(self.count):
            self.onward(i).wait()
            self.first(i, 0).wait_send()
            self.first(i, 1).wait_send()


class Scatter:
    def __init__(self, count, part, first_diag, first_own, second, send, recv, base=0):
        self.count, self.part = count, part
        self.diag, self.own, self.second = first_diag, first_own, second
        self.send, self.recv, self.base = send, recv, base
        self.t, self.x, self.y, self.d = tp_peers()

    def ways(self, i):
        return (self.x, self.y) if i % 2 == 0 else (self.y, self.x)

    def copy(self, i, kind):
        near, far = self.ways(i)
        n = self.base + kind * self.count + i
        if kind == 0:
            src, dst, to = self.part(self.d, i), self.diag(i), near
        elif kind == 1:
            src, dst, to = self.part(near, i), self.own(i), near
        else:
            src, dst, to = self.part(far, i), self.second(i), far
        return remote(src, dst, self.send.at[n], self.recv.at[n], spot(t=to))

    def start(self):
        for i in range(self.count):
            self.copy(i, 0).start()
        for i in range(self.count):
            self.copy(i, 1).start()

    def forward(self):
        for i in range(self.count):
            self.copy(i, 0).wait_recv()
            mine = self.part(self.ways(i)[1], i)
            mine[...] = (mine[...].astype(F32) + self.diag(i)[...].astype(F32)).astype(BF16)
            self.copy(i, 2).start()

    def collect(self, i):
        self.copy(i, 1).wait_recv()
        self.copy(i, 2).wait_recv()
        return self.own(i)[...].astype(F32) + self.second(i)[...].astype(F32)

    def finish(self):
        for i in range(self.count):
            for kind in range(3):
                self.copy(i, kind).wait_send()


def shard_at(ref, kind, index, size):
    if kind == "row":
        return ref.at[pl.ds(pl.multiple_of(index * size, size), size)]
    return ref.at[:, pl.ds(pl.multiple_of(index * size, size), size)]


def turned(kind, size):
    return kind == "col" and size % 128 != 0


def row_exchange(rows, send, recv):
    t, x, y, d = tp_peers()
    return [
        remote(rows.at[t], rows.at[t], send.at[k], recv.at[k], spot(t=p))
        for k, p in enumerate((x, y, d))
    ]


class Named:
    def __init__(self, names, refs):
        for name, ref in zip(names, refs, strict=True):
            setattr(self, name, ref)


class Transfer:
    def __init__(self, copy):
        self.copy, self.waited = copy, False

    def start(self):
        self.copy.start()

    def wait(self):
        if not self.waited:
            self.waited = True
            self.copy.wait()


def need(*transfers):
    for transfer in transfers:
        transfer.wait()


def dot(left, right):
    return jnp.dot(left, right, preferred_element_type=F32)


def dot_t(left, right):
    return lax.dot_general(left, right, (((1,), (1,)), ((), ())), preferred_element_type=F32)


def t_dot(left, right):
    return lax.dot_general(left, right, (((0,), (0,)), ((), ())), preferred_element_type=F32)


def sigmoid(v):
    return 1.0 / (1.0 + jnp.exp(-v))


def d_silu(v, s):
    return s * (1.0 + v * (1.0 - s))


def as_rows(column):
    return jnp.broadcast_to(column, (column.shape[0], 128)).T[0:8]


def as_column(rows):
    return rows.T[:, 0:1]


def at_block(i, size):
    return pl.ds(i * size if isinstance(i, int) else pl.multiple_of(i * size, size), size)


def wide(row):
    return jnp.broadcast_to(row, (8, 128))


def tree_sum(terms):
    while len(terms) > 1:
        terms = [a + b for a, b in zip(terms[::2], terms[1::2])]
    return terms[0]


def power(base, exponent):
    result, square = None, base
    while exponent:
        if exponent & 1:
            result = square if result is None else result * square
        exponent >>= 1
        if exponent:
            square = square * square
    return result


def row_sums(values):
    return lax.dot_general(
        jnp.ones((8, values.shape[1]), F32), values, (((1,), (1,)), ((), ())),
        precision=HIGH, preferred_element_type=F32,
    )


class Line:
    def __init__(self, kinds, sizes, count, sources, places, sems):
        self.kinds, self.sizes, self.count = kinds, sizes, count
        self.sources, self.places = sources, places
        self.here, self.send_up, self.send_down, self.send_core, self.recv, self.recv_core = sems
        self.z, self.c = lax.axis_index("fsdp"), lax.axis_index("ctx")
        self.other = spot(c=1 - self.c)
        self.up = spot(f=(self.z + 1) % count)
        self.down = spot(f=(self.z + count - 1) % count)
        self.next = {}

    def slot(self, w, owner, core):
        return shard_at(self.places[w], self.kinds[w], owner * 2 + core, self.sizes[w])

    def to_core(self, w, owner, src):
        return remote(
            src, self.slot(w, owner, self.c), self.send_core.at[w, owner], self.recv_core.at[w, owner], self.other
        )

    def to_up(self, w, owner, src):
        return remote(src, self.slot(w, owner, self.c), self.send_up.at[w, owner], self.recv.at[w, owner], self.up)

    def to_down(self, w, owner, src):
        return remote(src, self.slot(w, owner, self.c), self.send_down.at[w, owner], self.recv.at[w, owner], self.down)

    def keep(self, w):
        return pltpu.make_async_copy(self.sources[w], self.slot(w, self.z, self.c), self.here.at[w])

    def own(self, group):
        for w in group:

            @pl.when(self.z + 1 < self.count)
            def _():
                self.to_up(w, self.z, self.sources[w]).start()

            @pl.when(self.z > 0)
            def _():
                self.to_down(w, self.z, self.sources[w]).start()

            self.to_core(w, self.z, self.sources[w]).start()
            self.keep(w).start()
            self.next[w] = 1

    def hand_on(self, w, step):
        low, high = self.z - step, self.z + step

        @pl.when(low >= 0)
        def _():
            got = self.slot(w, low, self.c)
            self.to_up(w, low, got).wait_recv()

            @pl.when(self.z + 1 < self.count)
            def _():
                self.to_up(w, low, got).start()

            self.to_core(w, low, got).start()

        @pl.when(high < self.count)
        def _():
            got = self.slot(w, high, self.c)
            self.to_down(w, high, got).wait_recv()

            @pl.when(self.z > 0)
            def _():
                self.to_down(w, high, got).start()

            self.to_core(w, high, got).start()

    def pump(self, group):
        for w in group:
            if self.next[w] < self.count:
                self.hand_on(w, self.next[w])
                self.next[w] += 1

    def done(self, group):
        for w in group:
            if self.next[w] < self.count:

                @pl.loop(self.next[w], self.count)
                def _(step):
                    self.hand_on(w, step)

            @pl.loop(0, self.count)
            def _(owner):
                got = self.slot(w, owner, self.c)
                self.to_core(w, owner, got).wait()

                @pl.when((owner <= self.z) & (self.z + 1 < self.count))
                def _():
                    self.to_up(w, owner, got).wait_send()

                @pl.when((owner >= self.z) & (self.z > 0))
                def _():
                    self.to_down(w, owner, got).wait_send()

            self.keep(w).wait()


WEIGHTS = named(lambda shared, value, gate, hidden, attended, update, up, down: None)
KINDS = ("row", "row", "row", "col", "col", "col", "row", "col")
FRONT_WEIGHTS = WEIGHTS
A_IN = named(lambda tok, keep, gain, damp, eta, q_gain, k_gain, ids_row, cot: None) + ["s_" + w for w in FRONT_WEIGHTS]
A_OUT = named(
    lambda rows_update, normed4, mixed4, mix_pre, xn, inv_rows, s_pre, v_pre, g_pre, keys, vals,
    queries, log_sum, attended, gated, hid_pre, upd_pre, cot4: None
) + ["w_" + w for w in FRONT_WEIGHTS if w != "update"]
A_HBM = named(
    lambda rows_update, normed4, mixed4, mix_pre, xn, v_pre, g_pre, keys, vals, attended, gated,
    hid_pre, upd_pre, cot4: None
) + [
    "w_" + w for w in FRONT_WEIGHTS if w != "update"
]
A_SCRATCH = named(
    lambda low_n, low_m, rows, ends, starts, end_out, end_in, part_h, got_h, w_update, send, recv,
    s_rows, r_rows, s_core, r_core, s_upd, r_upd, s_kv, r_kv, s_out, z_here, z_up, z_down, z_core,
    z_recv, z_recv_core: None
)


def front_kernel(kinds, sizes, turns, line_count, *refs):
    aside = [w for w, turn in zip(FRONT_WEIGHTS, turns) if turn and w != "down"]
    names = A_IN + A_OUT + A_SCRATCH + ["v_" + n for n in A_HBM] + ["t_" + w for w in aside]
    m = Named(names, refs)
    outs = {}
    for k, n in enumerate(A_HBM):
        outs[n] = pltpu.make_async_copy(getattr(m, "v_" + n), getattr(m, n), m.s_out.at[k])
        setattr(m, n, getattr(m, "v_" + n))
    out = types.SimpleNamespace(**outs)
    t, x, y, d = tp_peers()
    c = lax.axis_index("ctx")
    other = spot(c=1 - c)
    groups, count = m.xn.shape[0], m.xn.shape[1]
    step, nj, width = count // 8, m.damp.shape[0], m.damp.shape[1]
    B = 256
    half, nb, span = B // 2, count // B, count + B
    scale = 1.0 / math.sqrt(Z)

    def lanes(o):
        return pl.ds(pl.multiple_of(o * width, width), width)

    line = Line(
        kinds, sizes, line_count, [getattr(m, "s_" + w) for w in FRONT_WEIGHTS],
        [getattr(m, ("t_" if w in aside else "w_") + w) for w in FRONT_WEIGHTS],
        (m.z_here, m.z_up, m.z_down, m.z_core, m.z_recv, m.z_recv_core),
    )
    first_w, second_w, third_w, fourth_w = (0, 1, 2), (3, 4, 5), (6,), (7,)

    m.end_in[...] = jnp.zeros_like(m.end_in)
    value = m.tok[...].astype(F32)
    m.rows[t] = row_sums(value * value)
    greet([spot(t=x), spot(t=y), spot(t=d), other, line.up, line.down])
    sums = [
        remote(m.rows.at[t], m.rows.at[t], m.s_rows.at[k], m.r_rows.at[k], spot(t=p))
        for k, p in enumerate((x, y, d))
    ]
    for copy in sums:
        copy.start()
    line.own(first_w)
    line.own(second_w)
    for copy in sums:
        copy.wait()
    inv = lax.rsqrt((m.rows[0] + m.rows[1] + m.rows[2] + m.rows[3]) / D + EPSILON)
    m.inv_rows[...] = inv
    normed = m.tok[...].astype(F32) * inv.T[:, 0:1] * m.gain[...]
    m.low_n[...] = normed.astype(BF16)
    for g in range(groups):
        m.xn[g] = normed[:, g * 128 : (g + 1) * 128]
    out.xn.start()
    chunks = 8
    size = count // chunks

    def whole_run(low, place, base):
        return Gather(
            chunks,
            lambda i: low.at[pl.ds(i * size, size)],
            lambda o, i: place.at[pl.ds(i * size, size), lanes(o)],
            m.send, m.recv, base,
        )

    norm_run = whole_run(m.low_n, m.normed4, 0)
    cot_run = whole_run(m.cot, m.cot4, 24)
    mix_run = whole_run(m.low_m, m.mixed4, 48)
    norm_run.start()

    for g in range(groups):
        ln = pl.ds(g * 128, 128)
        decay = [wide(1.0 - m.damp[pl.ds(j, 1), ln]) for j in range(nj)]

        def scan(s, carry):
            states, chain = carry
            at = pl.ds(s, 8, stride=step)
            v, k = m.xn[g, at, :], m.keep[at, :]
            return tuple(v + (k * r) * a for r, a in zip(decay, states)), chain * k

        zero = jnp.zeros((8, 128), F32)
        states, chain = lax.fori_loop(0, step, scan, ((zero,) * nj, zero + 1.0), unroll=4)
        for j in range(nj):
            m.ends[0, j, :, ln] = states[j]
            m.ends[1, j, :, ln] = power(decay[j], step) * chain

    last = jnp.zeros((nj, width), F32)
    for q in range(8):
        last = m.ends[0, :, q, :] + m.ends[1, :, q, :] * last
    m.end_out[...] = last
    across = remote(m.end_out, m.end_in, m.s_core.at[0], m.r_core.at[0], other)
    across.start()
    line.pump(first_w)
    across.wait()
    last = jnp.where(c == 0, 0.0, m.end_in[...])
    for q in range(8):
        m.starts[:, q, :] = last
        last = m.ends[0, :, q, :] + m.ends[1, :, q, :] * last

    for g in range(groups):
        ln = pl.ds(g * 128, 128)
        decay = [wide(1.0 - m.damp[pl.ds(j, 1), ln]) for j in range(nj)]
        weight = [wide(m.damp[pl.ds(j, 1), ln] * m.eta[pl.ds(j, 1), ln]) for j in range(nj)]

        def scan(s, states):
            at = pl.ds(s, 8, stride=step)
            v, k = m.xn[g, at, :], m.keep[at, :]
            states = tuple(v + (k * r) * a for r, a in zip(decay, states))
            m.mix_pre[g, at, :] = v + tree_sum([w * a for w, a in zip(weight, states)])
            return states

        lax.fori_loop(0, step, scan, tuple(m.starts[j, :, ln] for j in range(nj)), unroll=4)
        pre = m.mix_pre[g]
        m.low_m[:, ln] = (pre * sigmoid(pre)).astype(BF16)
    norm_run.forward()
    mix_run.start()
    out.mix_pre.start()
    line.pump(first_w)
    line.pump(second_w)
    line.own(third_w)
    for o in range(4):

        @pl.when(t == o)
        def _():
            m.normed4[:, o * width : (o + 1) * width] = m.low_n[...]
            m.mixed4[:, o * width : (o + 1) * width] = m.low_m[...]
            m.cot4[:, o * width : (o + 1) * width] = m.cot[...]

    mix_run.forward()
    line.pump(first_w)
    line.pump(second_w)
    line.own(fourth_w)
    norm_run.finish()
    out.normed4.start()
    line.done(first_w)
    for copy in (out.w_shared, out.w_value, out.w_gate):
        copy.start()

    def rows(i):
        return at_block(i, B)

    def mine(i):
        return pl.ds(pl.multiple_of(count + i * B, B), B)

    def window(i):
        return pl.ds(pl.multiple_of(i * B, B), span)

    def kv_run(i):
        return [
            remote(m.keys.at[mine(i)], m.keys.at[rows(i)], m.s_kv.at[2 * i], m.r_kv.at[2 * i], other),
            remote(m.vals.at[mine(i)], m.vals.at[rows(i)], m.s_kv.at[2 * i + 1], m.r_kv.at[2 * i + 1], other),
        ]

    @pl.loop(0, nb)
    def _(i):
        value = dot(m.normed4[rows(i), :], m.w_value[...])
        m.v_pre[rows(i), :] = value.astype(BF16)
        m.vals[mine(i), :] = (value * sigmoid(value)).astype(BF16)
        kv_run(i)[1].start()

    out.v_pre.start()
    mix_run.finish()
    out.mixed4.start()
    cot_run.start()

    @pl.loop(0, nb)
    def _(i):
        pre = dot(m.mixed4[rows(i), :], m.w_shared[...])
        m.s_pre[rows(i), :] = pre
        shared = pre * sigmoid(pre)
        m.queries[rows(i), :] = (shared * m.q_gain[...]).astype(BF16)
        m.keys[mine(i), :] = (shared * m.k_gain[...]).astype(BF16)
        kv_run(i)[0].start()

    @pl.loop(0, nb)
    def _(i):
        m.g_pre[rows(i), :] = dot(m.mixed4[rows(i), :], m.w_gate[...])

    out.g_pre.start()
    line.pump(second_w)
    line.pump(third_w)
    line.pump(fourth_w)
    for i in range(nb):
        for copy in kv_run(i):
            copy.wait()
    out.keys.start()
    out.vals.start()
    line.done(second_w)
    for w in aside:
        if w != "up":
            getattr(m, "w_" + w)[...] = getattr(m, "t_" + w)[...].astype(F32).T.astype(BF16)
    for copy in (out.w_hidden, out.w_attended):
        copy.start()
    upd = [
        remote(m.w_update.at[:, lanes(p)], m.rows_update.at[pl.ds(pl.multiple_of(t * width, width), width)],
               m.s_upd.at[n], m.r_upd.at[n], spot(t=p))
        for n, p in enumerate((x, y, d))
    ]
    for copy in upd:
        copy.start()
    for o in range(4):

        @pl.when(t == o)
        def _():
            m.rows_update[o * width : (o + 1) * width, :] = m.w_update[:, o * width : (o + 1) * width]

    def run_h(i):
        return Scatter(
            2,
            lambda o, n: m.part_h.at[o, pl.ds(pl.multiple_of(i * B + n * half, half), half)],
            lambda n: m.got_h.at[0, i * 2 + n],
            lambda n: m.got_h.at[1, i * 2 + n],
            lambda n: m.got_h.at[2, i * 2 + n],
            m.send, m.recv, 72 + i * 6,
        )

    def attend(i):
        raw = dot_t(m.queries[rows(i), :], m.keys[window(i), :]) * scale
        same = as_column(m.ids_row[:, mine(i)]) == m.ids_row[0:1, window(i)]
        place = lax.broadcasted_iota(jnp.int32, raw.shape, 1) - lax.broadcasted_iota(jnp.int32, raw.shape, 0)
        s = jnp.where(same & (place <= count), raw, -1e30)
        peak = jnp.max(s, axis=1, keepdims=True)
        e = jnp.exp(s - peak)
        total = jnp.sum(e, axis=1, keepdims=True)
        m.log_sum[rows(i), :] = jnp.broadcast_to(peak + jnp.log(total), (B, 128))
        attended = dot((e * (1.0 / total)).astype(BF16), m.vals[window(i), :])
        m.attended[rows(i), :] = attended.astype(BF16)
        gate = m.g_pre[rows(i), :]
        gated = (gate * sigmoid(gate) * attended).astype(BF16)
        m.gated[rows(i), :] = gated
        part = dot(m.mixed4[rows(i), lanes(t)], m.w_hidden[...]) + dot(gated, m.w_attended[...])
        part = part.astype(BF16)
        for o in range(4):
            m.part_h[o, rows(i), :] = part[:, o * width : (o + 1) * width]
        run_h(i).start()

    def collect(i):
        run = run_h(i)
        for n in range(2):
            m.hid_pre[pl.ds(i * B + n * half, half), :] = run.collect(n) + run.part(t, n)[...].astype(F32)
        run.finish()

    def attend_some(start, stop):
        @pl.loop(start, stop)
        def _(i):
            attend(i)

            @pl.when(i > 0)
            def _():
                run_h(i - 1).forward()

    attend_some(0, nb // 2)
    line.pump(third_w)
    line.pump(fourth_w)
    cot_run.forward()
    attend_some(nb // 2, nb)
    line.pump(third_w)
    line.pump(fourth_w)
    out.attended.start()
    out.gated.start()
    for copy in upd:
        copy.wait()

    @pl.loop(0, nb)
    def _(i):
        m.upd_pre[rows(i), :] = dot(m.mixed4[rows(i), :], m.rows_update[...])

    run_h(nb - 1).forward()
    out.upd_pre.start()
    out.rows_update.start()
    line.done(third_w)
    out.w_up.start()
    line.done(fourth_w)
    out.w_down.start()
    for i in range(nb):
        collect(i)
    out.hid_pre.start()
    cot_run.finish()
    out.cot4.start()
    for copy in outs.values():
        copy.wait()


def front(ident, line_count, tok, keep, gain, damp, eta, q_gain, k_gain, ids_row, cot, shards):
    count, width = tok.shape
    groups, nj = width // 128, damp.shape[0]
    nb = count // 256
    turns = [turned(k, s.shape[1]) for k, s in zip(KINDS, shards)]
    shards = [s.T if turn else s for turn, s in zip(turns, shards)]
    kinds = ["row" if turn else k for turn, k in zip(turns, KINDS)]
    sizes = [s.shape[0] if k == "row" else s.shape[1] for k, s in zip(kinds, shards)]
    full = 4 * width
    values = shards[1].shape[1]
    s = jax.ShapeDtypeStruct
    outs = dict(
        rows_update=s((full, width), BF16),
        normed4=s((count, full), BF16),
        mixed4=s((count, full), BF16),
        mix_pre=s((groups, count, 128), F32),
        xn=s((groups, count, 128), F32),
        inv_rows=s((8, count), F32),
        s_pre=s((count, Z), F32),
        v_pre=s((count, values), BF16),
        g_pre=s((count, values), F32),
        keys=s((2 * count, Z), BF16),
        vals=s((2 * count, values), BF16),
        queries=s((count, Z), BF16),
        log_sum=s((count, 128), F32),
        attended=s((count, values), BF16),
        gated=s((count, values), BF16),
        hid_pre=s((count, width), F32),
        upd_pre=s((count, width), F32),
        cot4=s((count, full), BF16),
    )
    aside = []
    for name, kind, size, shard in zip(FRONT_WEIGHTS, kinds, sizes, shards):
        shape = (2 * line_count * size, shard.shape[1]) if kind == "row" else (shard.shape[0], 2 * line_count * size)
        if turns[FRONT_WEIGHTS.index(name)] and name != "down":
            aside.append(pltpu.VMEM(shape, shard.dtype))
            shape = shape[::-1]
        outs["w_" + name] = s(shape, shard.dtype)
    v, dma, k = pltpu.VMEM, pltpu.SemaphoreType.DMA, len(FRONT_WEIGHTS)
    n = 72 + 6 * nb
    scratch = dict(
        low_n=v((count, width), BF16),
        low_m=v((count, width), BF16),
        rows=v((4, 8, count), F32),
        ends=v((2, nj, 8, width), F32),
        starts=v((nj, 8, width), F32),
        end_out=v((nj, width), F32),
        end_in=v((nj, width), F32),
        part_h=v((4, count, width), BF16),
        got_h=v((3, 2 * nb, 128, width), BF16),
        w_update=v(outs["w_update"].shape, BF16),
        send=dma((n,)), recv=dma((n,)), s_rows=dma((3,)), r_rows=dma((3,)), s_core=dma((1,)), r_core=dma((1,)),
        s_upd=dma((3,)), r_upd=dma((3,)), s_kv=dma((2 * nb,)), r_kv=dma((2 * nb,)), s_out=dma((len(A_HBM),)),
        z_here=dma((k,)), z_up=dma((k, line_count)), z_down=dma((k, line_count)), z_core=dma((k, line_count)),
        z_recv=dma((k, line_count)), z_recv_core=dma((k, line_count)),
    )
    got = pl.pallas_call(
        functools.partial(front_kernel, kinds, sizes, turns, line_count),
        out_shape=[outs[n] for n in A_OUT],
        in_specs=[VMEM] * len(A_IN),
        out_specs=[ANY if n in A_HBM else VMEM for n in A_OUT],
        scratch_shapes=[scratch[n] for n in A_SCRATCH] + [v(outs[n].shape, outs[n].dtype) for n in A_HBM] + aside,
        compiler_params=pltpu.CompilerParams(collective_id=ident, has_side_effects=True, vmem_limit_bytes=60 * 2**20),
        name="front",
    )(tok, keep, gain[None], damp, eta, q_gain[None], k_gain[None], ids_row, cot, *shards)
    return Named(A_OUT, got)


class LineSum:
    def __init__(self, kinds, sizes, count, sources, pair, line, outs, sems):
        self.kinds, self.sizes, self.count = kinds, sizes, count
        self.sources, self.pair, self.line, self.outs = sources, pair, line, outs
        self.send_core, self.recv_core, self.send, self.recv = sems
        self.z, self.c = lax.axis_index("fsdp"), lax.axis_index("ctx")
        self.other = spot(c=1 - self.c)

    def block(self, w, owner, core):
        return shard_at(self.sources[w], self.kinds[w], owner * 2 + core, self.sizes[w])

    def across(self, w, owner):
        return remote(
            self.block(w, owner, 1 - self.c), self.pair[w].at[owner],
            self.send_core.at[w, owner], self.recv_core.at[w, owner], self.other,
        )

    def along(self, w, k):
        owner = (self.z + k) % self.count
        far = ((self.z == 0) & (owner == self.count - 1)) | ((self.z == self.count - 1) & (owner == 0))
        to = jnp.where(far, jnp.where(self.z == 0, 1, self.count - 2), owner)
        at = jnp.where(far, self.count, self.z)
        return remote(
            self.pair[w].at[owner], self.line[w].at[at], self.send.at[w, k], self.recv.at[w, at], spot(f=to)
        )

    def helps(self, owner):
        return ((self.z == 1) & (owner == self.count - 1)) | ((self.z == self.count - 2) & (owner == 0))

    def relay(self, w):
        @pl.loop(1, self.count)
        def _(k):
            owner = (self.z + k) % self.count

            @pl.when(self.helps(owner))
            def _():
                got = self.line[w].at[self.count]
                remote(got, got, self.send.at[w, k], self.recv.at[w, self.count], self.other).wait_recv()
                self.pair[w][owner] = (self.pair[w][owner].astype(F32) + got[...].astype(F32)).astype(BF16)
                self.along(w, k).start()

    def start(self, w):
        @pl.loop(1, self.count + 1)
        def _(k):
            self.across(w, (self.z + k) % self.count).start()

    def plus(self, w, owner):
        return self.pair[w][owner].astype(F32) + self.block(w, owner, self.c)[...].astype(F32)

    def send_on(self, w):
        @pl.loop(1, self.count)
        def _(i):
            k = jnp.where(self.z == 0, self.count - i, i)
            owner = (self.z + k) % self.count
            self.across(w, owner).wait_recv()
            self.pair[w][owner] = self.plus(w, owner).astype(BF16)

            @pl.when(jnp.logical_not(self.helps(owner)))
            def _():
                self.along(w, k).start()

    def end(self, w):
        self.across(w, self.z).wait_recv()
        self.outs[w][...] = self.plus(w, self.z)

        @pl.loop(1, self.count)
        def _(k):
            source = (self.z + k) % self.count
            got = self.line[w].at[source]
            merged = ((self.z == 0) & (source == self.count - 1)) | ((self.z == self.count - 1) & (source == 0))

            @pl.when(jnp.logical_not(merged))
            def _():
                remote(got, got, self.send.at[w, k], self.recv.at[w, source], self.other).wait_recv()
                self.outs[w][...] += got[...].astype(F32)

            self.along(w, k).wait_send()

        @pl.loop(0, self.count)
        def _(owner):
            self.across(w, owner).wait_send()


def line_plan(shapes, kinds, count):
    turns = [turned(k, s[1] // (2 * count)) for k, s in zip(kinds, shapes)]
    shapes = [s[::-1] if turn else s for turn, s in zip(turns, shapes)]
    kinds = ["row" if turn else k for turn, k in zip(turns, kinds)]
    sizes = [s[0 if k == "row" else 1] // (2 * count) for k, s in zip(kinds, shapes)]
    blocks = [(n, s[1]) if k == "row" else (s[0], n) for k, n, s in zip(kinds, sizes, shapes)]
    return turns, kinds, sizes, shapes, blocks


def line_peers(count):
    z = lax.axis_index("fsdp")
    return [spot(f=(z + k) % count) for k in range(1, count)]


MID_LOAD = named(
    lambda hid_pre, upd_pre, w_up, w_down, cot4, w_attended, g_pre, attended, w_gate, w_upd,
    w_hidden, queries, keys, vals, log_sum, v_pre: None
)
MID_IN = MID_LOAD + named(lambda tok, cot, f_gain, ids_row: None)
MID_STORE = named(lambda out, part_t, tok_grad, mix_grad, value_grad, hid4, upd_grad, gate_grad: None)
MID_OUT = MID_STORE + named(lambda f_gain_grad, q_grad, k_grad, d_up, d_down: None)
MID_SCRATCH = named(
    lambda block, part_f, up_rows, up_grads, ffn4, att_grad, k_all, v_all, part_g, got_g, low,
    rows_a, rows_b, k_send, v_send, k_got, v_got, p_up, p_down, l_up, l_down, send, recv, s_rows,
    r_rows, s_gr, r_gr, s_in, s_out, c_send, c_recv, l_send, l_recv: None
)


def mid_kernel(kinds, sizes, turn, line_count, *refs):
    m = Named(
        MID_IN + MID_OUT + MID_SCRATCH + ["i_" + n for n in MID_LOAD] + ["o_" + n for n in MID_STORE], refs
    )
    loads, stores = {}, {}
    for k, n in enumerate(MID_LOAD):
        loads[n] = Transfer(pltpu.make_async_copy(getattr(m, n), getattr(m, "i_" + n), m.s_in.at[k]))
        setattr(m, n, getattr(m, "i_" + n))
        loads[n].start()
    for k, n in enumerate(MID_STORE):
        stores[n] = pltpu.make_async_copy(getattr(m, "o_" + n), getattr(m, n), m.s_out.at[k])
        setattr(m, n, getattr(m, "o_" + n))
    load, store = types.SimpleNamespace(**loads), types.SimpleNamespace(**stores)
    t, x, y, d = tp_peers()
    other = spot(c=1 - lax.axis_index("ctx"))
    count, width = m.tok.shape
    hidden = m.w_up.shape[1]
    B = 256
    half, nb, span = B // 2, count // B, count + B
    scale = 1.0 / math.sqrt(Z)

    def rows(i):
        return at_block(i, B)

    def mine(i):
        return pl.ds(count + i * B, B)

    def window(i):
        return pl.ds(i * B, span)

    def lanes(o):
        return pl.ds(pl.multiple_of(o * width, width), width)

    greet([spot(t=x), spot(t=y), spot(t=d), other] + line_peers(line_count))
    m.f_gain_grad[...] = jnp.zeros_like(m.f_gain_grad)

    def gather_run(kind, i, low, place):
        return Gather(
            2,
            lambda n: low.at[pl.ds(i * B + n * half, half)],
            lambda o, n: place.at[pl.ds(i * B + n * half, half), lanes(o)],
            m.send, m.recv, (kind * nb + i) * 6,
        )

    def scatter_run(kind, i, part, got):
        return Scatter(
            2,
            lambda o, n: part.at[o, pl.ds(i * B + n * half, half)],
            lambda n: got.at[0, i * 2 + n],
            lambda n: got.at[1, i * 2 + n],
            lambda n: got.at[2, i * 2 + n],
            m.send, m.recv, (kind * nb + i) * 6,
        )

    run_p = [gather_run(0, i, m.low, m.ffn4) for i in range(nb)]
    run_gh = [gather_run(1, i, m.low, m.hid4) for i in range(nb)]
    run_g = [scatter_run(2, i, m.part_g, m.got_g) for i in range(nb)]
    run_f = [scatter_run(3, i, m.part_f, m.got_g) for i in range(nb)]
    line = LineSum(
        kinds, sizes, line_count, [m.w_up, m.w_down], [m.p_up, m.p_down], [m.l_up, m.l_down], [m.d_up, m.d_down],
        (m.c_send, m.c_recv, m.l_send, m.l_recv),
    )

    def row_run(kind, i, buf):
        return [
            remote(
                buf.at[t, :, rows(i)], buf.at[t, :, rows(i)],
                m.s_rows.at[(kind * nb + i) * 3 + n], m.r_rows.at[(kind * nb + i) * 3 + n], spot(t=p),
            )
            for n, p in enumerate((x, y, d))
        ]

    def row_total(buf, i):
        return buf[0, :, rows(i)] + buf[1, :, rows(i)] + buf[2, :, rows(i)] + buf[3, :, rows(i)]

    def split(part, i, value):
        low = value.astype(BF16)
        for o in range(4):
            part[o, rows(i), :] = low[:, o * width : (o + 1) * width]

    def place_own(full_ref, i):
        for o in range(4):

            @pl.when(t == o)
            def _():
                full_ref[rows(i), o * width : (o + 1) * width] = m.low[rows(i), :]

    def joined(run):
        pieces = [run.collect(n) + run.part(t, n)[...].astype(F32) for n in range(2)]
        return jnp.concatenate(pieces, axis=0)

    def inverse_mid(i):
        return lax.rsqrt(row_total(m.rows_a, i) / D + EPSILON)

    def block_stage(i):
        need(load.hid_pre, load.upd_pre)
        hidden_pre, update = m.hid_pre[rows(i), :], sigmoid(m.upd_pre[rows(i), :])
        block = update * (hidden_pre * sigmoid(hidden_pre)) + (1.0 - update) * m.tok[rows(i), :].astype(F32)
        m.block[rows(i), :] = block
        m.low[rows(i), :] = (block * m.f_gain[...]).astype(BF16)
        run_p[i].start()
        m.rows_a[t, :, rows(i)] = as_rows(jnp.sum(block * block, axis=1, keepdims=True))
        for copy in row_run(0, i, m.rows_a):
            copy.start()
        place_own(m.ffn4, i)

    def up_stage(i):
        need(load.w_up)
        run_p[i].finish()
        raw = dot(m.ffn4[rows(i), :], m.w_up[...])
        part = m.v_all.shape[1]
        parts = hidden // part
        for k in range(parts):
            m.v_all[pl.ds((parts * i + k) * B, B), :] = raw[:, k * part : (k + 1) * part]

    down, down_t = (dot_t, dot) if turn else (dot, dot_t)

    def ffn_stage(i):
        need(load.w_down, load.cot4)
        back = down_t(m.cot4[rows(i), :], m.w_down[...])
        for copy in row_run(0, i, m.rows_a):
            copy.wait()
        inv = as_column(inverse_mid(i))
        parts = hidden // m.v_all.shape[1]
        raw = jnp.concatenate([m.v_all[pl.ds((parts * i + k) * B, B), :] for k in range(parts)], axis=1)
        up_pre = raw * inv
        sig = sigmoid(up_pre)
        grad_up = (back * d_silu(up_pre, sig)).astype(BF16)
        split(m.part_g, i, dot_t(grad_up, m.w_up[...]))
        run_g[i].start()
        wide_grad = grad_up.astype(F32)
        m.up_grads[rows(i), :] = (wide_grad * inv).astype(BF16)
        m.rows_b[t, :, rows(i)] = as_rows(jnp.sum(wide_grad * raw, axis=1, keepdims=True))
        for copy in row_run(1, i, m.rows_b):
            copy.start()
        up_rows = (up_pre * sig).astype(BF16)
        m.up_rows[rows(i), :] = up_rows
        split(m.part_f, i, down(up_rows, m.w_down[...]))

    def grad_stage(i):
        grad_ffn = joined(run_g[i])
        for copy in row_run(1, i, m.rows_b):
            copy.wait()
        block = m.block[rows(i), :]
        inv_rows = inverse_mid(i)
        factor = inv_rows * inv_rows * inv_rows * row_total(m.rows_b, i) / D
        inv = as_column(inv_rows)
        grad_block = (
            m.cot[rows(i), :].astype(F32) + inv * (grad_ffn * m.f_gain[...]) - block * as_column(factor)
        )
        m.f_gain_grad[...] += jnp.sum(grad_ffn * block * inv, axis=0, keepdims=True)
        hidden_pre, update = m.hid_pre[rows(i), :], sigmoid(m.upd_pre[rows(i), :])
        sig = sigmoid(hidden_pre)
        m.low[rows(i), :] = (grad_block * update * d_silu(hidden_pre, sig)).astype(BF16)
        run_gh[i].start()
        keep = grad_block * (1.0 - update)
        m.tok_grad[rows(i), :] = keep
        tokens = m.tok[rows(i), :].astype(F32)
        m.upd_grad[rows(i), :] = (keep * (hidden_pre * sig - tokens) * update).astype(BF16)
        place_own(m.hid4, i)
        run_g[i].finish()

    def gate_stage(i):
        need(load.w_attended, load.g_pre, load.attended, load.w_gate, load.w_upd, load.w_hidden)
        run_gh[i].finish()
        grad_hidden = m.hid4[rows(i), :]
        grad_gated = dot_t(grad_hidden, m.w_attended[...])
        gate = m.g_pre[rows(i), :]
        sig = sigmoid(gate)
        grad_gate = (grad_gated * m.attended[rows(i), :].astype(F32) * d_silu(gate, sig)).astype(BF16)
        m.gate_grad[rows(i), :] = grad_gate
        split(m.part_t, i, dot_t(grad_gate, m.w_gate[...]) + dot_t(m.upd_grad[rows(i), :], m.w_upd[...]))
        m.att_grad[rows(i), :] = (grad_gated * (gate * sig)).astype(BF16)
        m.mix_grad[rows(i), :] = dot_t(grad_hidden, m.w_hidden[...])

    def grads_run(i):
        return [
            remote(m.k_send.at[rows(i)], m.k_got.at[rows(i)], m.s_gr.at[2 * i], m.r_gr.at[2 * i], other),
            remote(m.v_send.at[rows(i)], m.v_got.at[rows(i)], m.s_gr.at[2 * i + 1], m.r_gr.at[2 * i + 1], other),
        ]

    def attend_back(i):
        need(load.queries, load.keys, load.vals, load.log_sum)
        raw = dot_t(m.queries[rows(i), :], m.keys[window(i), :]) * scale
        same = as_column(m.ids_row[:, mine(i)]) == m.ids_row[0:1, window(i)]
        place = lax.broadcasted_iota(jnp.int32, raw.shape, 1) - lax.broadcasted_iota(jnp.int32, raw.shape, 0)
        exact = jnp.exp(jnp.where(same & (place <= count), raw, -1e30) - m.log_sum[rows(i), 0:1])
        grad_rows = m.att_grad[rows(i), :]
        value_part = t_dot(exact.astype(BF16), grad_rows)
        grad_probs = dot_t(grad_rows, m.vals[window(i), :])
        inner = jnp.sum(exact * grad_probs, axis=1, keepdims=True)
        grad_scores = exact * (grad_probs - inner) * scale
        high = grad_scores.astype(BF16)
        rest = (grad_scores - high.astype(F32)).astype(BF16)
        keys, queries = m.keys[window(i), :], m.queries[rows(i), :]
        m.q_grad[rows(i), :] = dot(high, keys) + dot(rest, keys)
        key_part = t_dot(high, queries) + t_dot(rest, queries)
        if i == 0:
            m.v_all[window(0), :] = value_part
            m.k_all[window(0), :] = key_part
        else:
            old, new = pl.ds(i * B, span - B), pl.ds(span + (i - 1) * B, B)
            m.v_all[old, :] += value_part[: span - B]
            m.v_all[new, :] = value_part[span - B :]
            m.k_all[old, :] += key_part[: span - B]
            m.k_all[new, :] = key_part[span - B :]
        m.k_send[rows(i), :] = m.k_all[rows(i), :].astype(BF16)
        m.v_send[rows(i), :] = m.v_all[rows(i), :].astype(BF16)
        for copy in grads_run(i):
            copy.start()

    def product(dst, left, right):
        for k in range(right.shape[1] // B):
            at = slice(k * B, (k + 1) * B)
            dst[:, at] = t_dot(left[...], right[:, at]).astype(BF16)

    def key_end(i):
        need(load.v_pre)
        for copy in grads_run(i):
            copy.wait()
        m.k_grad[rows(i), :] = m.k_all[mine(i), :] + m.k_got[rows(i), :].astype(F32)
        value = m.v_pre[rows(i), :].astype(F32)
        grad = m.v_all[mine(i), :] + m.v_got[rows(i), :].astype(F32)
        m.value_grad[rows(i), :] = (grad * d_silu(value, sigmoid(value))).astype(BF16)

    block_stage(0)
    block_stage(1)
    run_p[0].forward()
    block_stage(2)
    run_p[1].forward()
    block_stage(3)
    run_p[2].forward()
    up_stage(0)
    ffn_stage(0)
    run_p[3].forward()
    up_stage(1)
    ffn_stage(1)
    run_g[0].forward()
    up_stage(2)
    ffn_stage(2)
    up_stage(3)
    run_g[1].forward()
    grad_stage(0)
    ffn_stage(3)
    run_g[2].forward()
    grad_stage(1)
    run_gh[0].forward()
    if turn:
        product(m.w_down, m.cot4, m.up_rows)
    else:
        product(m.w_down, m.up_rows, m.cot4)
    line.start(1)
    run_g[3].forward()
    grad_stage(2)
    run_gh[1].forward()
    product(m.w_up, m.ffn4, m.up_grads)
    line.start(0)
    line.send_on(1)
    grad_stage(3)
    run_gh[2].forward()
    gate_stage(0)
    line.send_on(0)
    run_gh[3].forward()
    run_f[0].start()
    run_f[1].start()
    gate_stage(1)
    attend_back(0)
    gate_stage(2)
    run_f[0].forward()
    run_f[2].start()
    line.relay(1)
    gate_stage(3)
    store.hid4.start()
    store.upd_grad.start()
    store.gate_grad.start()
    store.tok_grad.start()
    store.part_t.start()
    store.mix_grad.start()
    run_f[1].forward()
    run_f[3].start()
    attend_back(1)
    run_f[2].forward()
    attend_back(2)
    run_f[3].forward()
    line.relay(0)
    attend_back(3)
    key_end(0)
    key_end(1)
    key_end(2)
    key_end(3)
    store.value_grad.start()
    for i in range(nb):
        m.out[rows(i), :] = (m.block[rows(i), :] + joined(run_f[i])).astype(BF16)
        run_f[i].finish()
    store.out.start()
    line.end(1)
    line.end(0)
    for copy in stores.values():
        copy.wait()


def middle(ident, line_count, ins):
    tok, f_gain = ins["tok"], ins["f_gain"]
    count, width = tok.shape
    full = 4 * width
    values, hidden = ins["w_gate"].shape[1], ins["w_up"].shape[1]
    nb = count // 256
    (_, turn), kinds, sizes, _, blocks = line_plan([(full, hidden), (hidden, full)], KINDS[-2:], line_count)
    dma, s, v = pltpu.SemaphoreType.DMA, jax.ShapeDtypeStruct, pltpu.VMEM
    outs = dict(
        out=s((count, width), BF16),
        part_t=s((4, count, width), BF16),
        tok_grad=s((count, width), F32),
        mix_grad=s((count, width), F32),
        value_grad=s((count, values), BF16),
        hid4=s((count, full), BF16),
        upd_grad=s((count, width), BF16),
        gate_grad=s((count, values), BF16),
        f_gain_grad=s((1, width), F32),
        q_grad=s((count, Z), F32),
        k_grad=s((count, Z), F32),
        d_up=s(blocks[0], F32),
        d_down=s(blocks[1], F32),
    )
    scratch = dict(
        block=v((count, width), F32),
        part_f=v((4, count, width), BF16),
        up_rows=v((count, hidden), BF16),
        up_grads=v((count, hidden), BF16),
        ffn4=v((count, full), BF16),
        att_grad=v((count, values), BF16),
        k_all=v((2 * count, Z), F32),
        v_all=v((2 * count, values), F32),
        part_g=v((4, count, width), BF16),
        got_g=v((3, 2 * nb, 128, width), BF16),
        low=v((count, width), BF16),
        rows_a=v((4, 8, count), F32),
        rows_b=v((4, 8, count), F32),
        k_send=v((count, Z), BF16),
        v_send=v((count, values), BF16),
        k_got=v((count, Z), BF16),
        v_got=v((count, values), BF16),
        p_up=v((line_count,) + blocks[0], BF16),
        p_down=v((line_count,) + blocks[1], BF16),
        l_up=v((line_count + 1,) + blocks[0], BF16),
        l_down=v((line_count + 1,) + blocks[1], BF16),
        c_send=dma((2, line_count)), c_recv=dma((2, line_count)),
        l_send=dma((2, line_count)), l_recv=dma((2, line_count + 1)),
        send=dma((24 * nb,)), recv=dma((24 * nb,)),
        s_rows=dma((6 * nb,)), r_rows=dma((6 * nb,)),
        s_gr=dma((2 * nb,)), r_gr=dma((2 * nb,)),
        s_in=dma((len(MID_LOAD),)), s_out=dma((len(MID_STORE),)),
    )
    got_all = pl.pallas_call(
        functools.partial(mid_kernel, kinds, sizes, turn, line_count),
        out_shape=[outs[n] for n in MID_OUT],
        in_specs=[ANY if n in MID_LOAD else VMEM for n in MID_IN],
        out_specs=[ANY if n in MID_STORE else VMEM for n in MID_OUT],
        scratch_shapes=[scratch[n] for n in MID_SCRATCH]
        + [v(ins[n].shape, ins[n].dtype) for n in MID_LOAD]
        + [v(outs[n].shape, outs[n].dtype) for n in MID_STORE],
        compiler_params=pltpu.CompilerParams(collective_id=ident, has_side_effects=True, vmem_limit_bytes=62 * 2**20),
        name="middle",
    )(*[ins[n] for n in MID_IN])
    got_all = Named(MID_OUT, got_all)
    if turn:
        got_all.d_down = got_all.d_down.T
    return got_all


REAR_LOAD = named(
    lambda part_t, value_grad, w_value, gated, hid4, mixed4, upd_grad, gate_grad, normed4, mix_grad,
    mix_pre, xn, tok_grad: None
)
REAR_IN = REAR_LOAD + named(
    lambda q_grad, k_grad, s_pre, w_shared, tok, inv_rows, keep_next, gain, damp, eta, q_gain,
    k_gain, f_gain_grad: None
)
REAR_WEIGHTS = WEIGHTS[:-2]
REAR_OUT = named(lambda grad_in, small: None) + ["d_" + w for w in REAR_WEIGHTS]
REAR_SCRATCH = named(
    lambda part_v, got_v, got_t, part_s, got_s, low_s, full_s, grad_mix, back, rows, ends, starts,
    end_out, end_in, small_core, small_all, own_q, all_q, upd_cols, send, recv, s_rows, r_rows,
    s_core, r_core, s_upd, r_upd, s_small, r_small, s_q, r_q, s_in, c_send, c_recv, l_send, l_recv:
    None
)


def rear_kernel(kinds, sizes, turns, line_count, *refs):
    groups_of = [p + w for p in ("p_", "l_", "g_") for w in REAR_WEIGHTS]
    m = Named(REAR_IN + REAR_OUT + REAR_SCRATCH + groups_of + ["i_" + n for n in REAR_LOAD], refs)
    loads = {}
    for k, n in enumerate(REAR_LOAD):
        loads[n] = Transfer(pltpu.make_async_copy(getattr(m, n), getattr(m, "i_" + n), m.s_in.at[k]))
        setattr(m, n, getattr(m, "i_" + n))
        loads[n].start()
    load = types.SimpleNamespace(**loads)
    t, x, y, d = tp_peers()
    z, c = lax.axis_index("fsdp"), lax.axis_index("ctx")
    other = spot(c=1 - c)
    groups, count = m.xn.shape[0], m.xn.shape[1]
    step, nj, width = count // 8, m.damp.shape[0], m.damp.shape[1]
    B = 256
    half, nb = B // 2, count // B
    part = min(16, nj)
    zero = jnp.zeros((8, 128), F32)

    def lanes(o):
        return pl.ds(pl.multiple_of(o * width, width), width)

    line = LineSum(
        kinds, sizes, line_count,
        [getattr(m, "g_" + w) for w in REAR_WEIGHTS], [getattr(m, "p_" + w) for w in REAR_WEIGHTS],
        [getattr(m, "l_" + w) for w in REAR_WEIGHTS], [getattr(m, "d_" + w) for w in REAR_WEIGHTS],
        (m.c_send, m.c_recv, m.l_send, m.l_recv),
    )
    m.end_in[...] = jnp.zeros_like(m.end_in)
    greet([spot(t=x), spot(t=y), spot(t=d), other] + line_peers(line_count))

    run_s = Scatter(
        2,
        lambda o, n: m.part_s.at[pl.ds(pl.multiple_of(o * B + n * half, half), half)],
        lambda n: m.got_s.at[0, n], lambda n: m.got_s.at[1, n], lambda n: m.got_s.at[2, n],
        m.send, m.recv, 0,
    )
    run_full = Gather(
        2,
        lambda n: m.low_s.at[pl.ds(n * half, half)],
        lambda o, n: m.full_s.at[pl.ds(pl.multiple_of(o * B + n * half, half), half)],
        m.send, m.recv, 6,
    )

    def scatter_runs(kind, parts, got):
        return [
            Scatter(
                2,
                lambda o, n, i=i: parts.at[o, pl.ds(i * B + n * half, half)],
                lambda n, i=i: got.at[0, i * 2 + n],
                lambda n, i=i: got.at[1, i * 2 + n],
                lambda n, i=i: got.at[2, i * 2 + n],
                m.send, m.recv, 12 + 6 * (kind * nb + i),
            )
            for i in range(nb)
        ]

    run_t, run_v = (
        scatter_runs(k, parts, got)
        for k, (parts, got) in enumerate(((m.part_t, m.got_t), (m.part_v, m.got_v)))
    )

    m.part_s[...] = (m.q_grad[...] * m.q_gain[...] + m.k_grad[...] * m.k_gain[...]).astype(BF16)
    run_s.start()
    shared = m.s_pre[...] * sigmoid(m.s_pre[...])
    m.own_q[...] = jnp.zeros_like(m.own_q)
    m.own_q[0:1, 0:Z] = jnp.sum(shared * m.q_grad[...], axis=0, keepdims=True)
    m.own_q[0:1, Z:] = jnp.sum(shared * m.k_grad[...], axis=0, keepdims=True)
    m.all_q[t] = m.own_q[...]
    gains = [
        remote(m.own_q, m.all_q.at[t], m.s_q.at[k], m.r_q.at[k], spot(t=p)) for k, p in enumerate((x, y, d))
    ]
    for copy in gains:
        copy.start()
    need(load.part_t)
    run_t[0].start()
    run_t[1].start()
    def value_part(i):
        rows = slice(i * B, (i + 1) * B)
        low = dot_t(m.value_grad[rows, :], m.w_value[...]).astype(BF16)
        for o in range(4):
            m.part_v[o, rows, :] = low[:, o * width : (o + 1) * width]

    def product(w, left, right):
        dst = getattr(m, "g_" + w)
        if turns[REAR_WEIGHTS.index(w)]:
            left, right = right, left
        size = min(256, right.shape[1])
        for k in range(right.shape[1] // size):
            at = slice(k * size, (k + 1) * size)
            dst[:, at] = t_dot(left, right[:, at]).astype(BF16)

    at_w = {w: k for k, w in enumerate(REAR_WEIGHTS)}

    need(load.value_grad, load.w_value)

    def value_part(i):
        rows = slice(i * B, (i + 1) * B)
        low = dot_t(m.value_grad[rows, :], m.w_value[...]).astype(BF16)
        for o in range(4):
            m.part_v[o, rows, :] = low[:, o * width : (o + 1) * width]

    need(load.gated, load.hid4)
    product("attended", m.gated[...], m.hid4[...])
    line.start(at_w["attended"])
    run_s.forward()
    run_t[0].forward()
    run_t[2].start()
    run_t[1].forward()
    run_t[3].start()
    need(load.mixed4, load.upd_grad)
    product("hidden", m.mixed4[:, lanes(t)], m.hid4[...])
    line.start(at_w["hidden"])
    quarter = pl.ds(pl.multiple_of(t * B, B), B)
    for n in range(2):
        total = run_s.collect(n) + run_s.part(t, n)[...].astype(F32)
        pre = m.s_pre[pl.ds(pl.multiple_of(t * B + n * half, half), half), :]
        m.low_s[n * half : (n + 1) * half, :] = (total * d_silu(pre, sigmoid(pre))).astype(BF16)
    run_full.start()
    m.full_s[quarter, :] = m.low_s[...]
    run_t[2].forward()
    line.send_on(at_w["attended"])
    turn_update = turns[at_w["update"]]
    if turn_update:
        m.upd_cols[...] = t_dot(m.upd_grad[...], m.mixed4[...]).astype(BF16)
    else:
        m.upd_cols[...] = t_dot(m.mixed4[...], m.upd_grad[...]).astype(BF16)

    def ends_of(p):
        if turn_update:
            return m.upd_cols.at[:, lanes(p)], m.g_update.at[lanes(t)]
        return m.upd_cols.at[lanes(p)], m.g_update.at[:, lanes(t)]

    turn_copies = [
        remote(*ends_of(p), m.s_upd.at[k], m.r_upd.at[k], spot(t=p)) for k, p in enumerate((x, y, d))
    ] + [pltpu.make_async_copy(*ends_of(t), m.s_upd.at[3])]
    for copy in turn_copies:
        copy.start()
    run_t[3].forward()
    run_full.forward()
    need(load.value_grad, load.w_value)
    value_part(0)
    run_v[0].start()
    value_part(1)
    run_v[1].start()
    line.send_on(at_w["hidden"])
    need(load.gate_grad, load.normed4)
    product("gate", m.mixed4[...], m.gate_grad[...])
    line.start(at_w["gate"])
    value_part(2)
    value_part(3)
    run_s.finish()
    run_full.finish()
    product("shared", m.mixed4[...], m.full_s[...])
    line.start(at_w["shared"])
    run_v[0].forward()
    run_v[2].start()
    for copy in turn_copies:
        copy.wait()
    line.start(at_w["update"])
    product("value", m.normed4[...], m.value_grad[...])
    line.start(at_w["value"])
    line.send_on(at_w["gate"])
    run_v[1].forward()
    run_v[3].start()
    line.send_on(at_w["update"])
    need(load.mix_grad, load.mix_pre, load.xn, load.tok_grad)
    own_shared = m.w_shared[lanes(t), :]
    for i in range(nb):
        for n in range(2):
            at = pl.ds(i * B + n * half, half)
            mix = m.mix_grad[at, :] + run_t[i].collect(n) + run_t[i].part(t, n)[...].astype(F32)
            mix = mix + dot_t(m.full_s[at, :], own_shared)
            for g in range(groups):
                pre = m.mix_pre[g, at, :]
                m.grad_mix[g, at, :] = mix[:, g * 128 : (g + 1) * 128] * d_silu(pre, sigmoid(pre))
        run_t[i].finish()
    line.send_on(at_w["shared"])
    line.send_on(at_w["value"])

    def later(*steps):
        return list(steps)

    def relay(*names):
        def run():
            for name in names:
                line.relay(at_w[name])

        return run

    waiting = later(
        run_v[2].forward, run_v[3].forward, relay("attended"), relay("hidden"), relay("gate"),
        relay("update"), relay("shared"), relay("value"),
    )

    def go(count):
        for _ in range(min(count, len(waiting))):
            waiting.pop(0)()

    for g in range(groups):
        ln = pl.ds(g * 128, 128)
        for j0 in range(0, nj, part):
            decay = [wide(1.0 - m.damp[pl.ds(j, 1), ln]) for j in range(j0, j0 + part)]

            def scan(i, carry):
                a, w, chain = carry
                at, after = pl.ds(step - 1 - i, 8, stride=step), pl.ds(step - i, 8, stride=step)
                v, k = m.grad_mix[g, at, :], m.keep_next[after, :]
                held = [k * r for r in decay]
                w = tuple(k * p + r * q for p, r, q in zip(a, held, w))
                a = tuple(v + r * p for r, p in zip(held, a))
                return a, w, chain * k

            a, w, chain = lax.fori_loop(0, step, scan, ((zero,) * part, (zero,) * part, zero + 1.0), unroll=8)
            for n in range(part):
                less = power(decay[n], step - 1)
                m.ends[0, j0 + n, :, ln] = a[n]
                m.ends[1, j0 + n, :, ln] = w[n]
                m.ends[2, j0 + n, :, ln] = less * decay[n] * chain
                m.ends[3, j0 + n, :, ln] = float(step) * less * chain
            go(2)

    def merge(q, a, w):
        return (
            m.ends[0, :, q, :] + m.ends[2, :, q, :] * a,
            m.ends[1, :, q, :] + m.ends[2, :, q, :] * w + m.ends[3, :, q, :] * a,
        )

    a = w = jnp.zeros((nj, width), F32)
    for q in range(7, -1, -1):
        a, w = merge(q, a, w)
    m.end_out[0] = a
    m.end_out[1] = w
    across = remote(m.end_out, m.end_in, m.s_core.at[0], m.r_core.at[0], other)
    across.start()
    across.wait()
    a, w = jnp.where(c == 0, m.end_in[0], 0.0), jnp.where(c == 0, m.end_in[1], 0.0)
    for q in range(7, -1, -1):
        m.starts[0, :, q, :] = a
        m.starts[1, :, q, :] = w
        a, w = merge(q, a, w)

    for g in range(groups):
        ln = pl.ds(g * 128, 128)
        for j0 in range(0, nj, part):
            span = range(j0, j0 + part)
            decay = [wide(1.0 - m.damp[pl.ds(j, 1), ln]) for j in span]
            weight = [wide(m.damp[pl.ds(j, 1), ln] * m.eta[pl.ds(j, 1), ln]) for j in span]

            def scan(i, carry):
                a, w, sum_a, sum_w = carry
                at, after = pl.ds(step - 1 - i, 8, stride=step), pl.ds(step - i, 8, stride=step)
                v, k, u = m.grad_mix[g, at, :], m.keep_next[after, :], m.xn[g, at, :]
                held = [k * r for r in decay]
                w = tuple(k * p + r * q for p, r, q in zip(a, held, w))
                a = tuple(v + r * p for r, p in zip(held, a))
                sum_a = tuple(s + u * p for s, p in zip(sum_a, a))
                sum_w = tuple(s + u * p for s, p in zip(sum_w, w))
                base = v if j0 == 0 else m.back[g, at, :]
                m.back[g, at, :] = base + tree_sum([r * p for r, p in zip(weight, a)])
                return a, w, sum_a, sum_w

            first = (tuple(m.starts[0, j, :, ln] for j in span), tuple(m.starts[1, j, :, ln] for j in span))
            _, _, sum_a, sum_w = lax.fori_loop(
                0, step, scan, first + ((zero,) * part, (zero,) * part), unroll=8
            )
            for n, j in enumerate(span):
                at = pl.ds(j, 1)
                all_a = jnp.sum(sum_a[n], axis=0, keepdims=True)
                all_w = jnp.sum(sum_w[n], axis=0, keepdims=True)
                rate = m.damp[at, ln]
                m.small[at, ln] = m.eta[at, ln] * (all_a - rate * all_w)
                m.small[pl.ds(nj + j, 1), ln] = rate * all_a
            go(2)

    go(len(waiting))
    inv = m.inv_rows[...].T[:, 0:1]
    value = m.tok[...].astype(F32)
    for i in range(nb):
        for n in range(2):
            at = pl.ds(i * B + n * half, half)
            got = run_v[i].collect(n) + run_v[i].part(t, n)[...].astype(F32)
            m.grad_in[at, :] = got + jnp.concatenate([m.back[g, at, :] for g in range(groups)], axis=1)
        run_v[i].finish()
    grad_normed = m.grad_in[...]
    m.small[2 * nj :, :] = jnp.zeros((m.small.shape[0] - 2 * nj, width), F32)
    m.small[2 * nj : 2 * nj + 1, :] = jnp.sum(grad_normed * value * inv, axis=0, keepdims=True)
    m.small[2 * nj + 1 : 2 * nj + 2, :] = m.f_gain_grad[...]
    for copy in gains:
        copy.wait()
    m.small[2 * nj + 2 : 2 * nj + 3, :] = (
        m.all_q[0, 0:1] + m.all_q[1, 0:1] + m.all_q[2, 0:1] + m.all_q[3, 0:1]
    )
    scaled = grad_normed * m.gain[...]
    m.rows[t] = row_sums(scaled * value)
    sums = row_exchange(m.rows, m.s_rows, m.r_rows)
    pair = remote(m.small, m.small_core, m.s_small.at[0], m.r_small.at[0], other)
    for copy in sums + [pair]:
        copy.start()
    m.grad_in[...] = m.tok_grad[...] + inv * scaled
    pair.wait()
    m.small_all[z] = m.small[...] + m.small_core[...]
    wide_sums = [
        remote(
            m.small_all.at[z], m.small_all.at[z], m.s_small.at[k], m.r_small.at[k], spot(f=(z + k) % line_count)
        )
        for k in range(1, line_count)
    ]
    for copy in wide_sums:
        copy.start()
    for copy in sums:
        copy.wait()
    factor = m.inv_rows[...]
    factor = factor * factor * factor * (m.rows[0] + m.rows[1] + m.rows[2] + m.rows[3]) / D
    m.grad_in[...] -= value * factor.T[:, 0:1]
    for copy in wide_sums:
        copy.wait()
    total = m.small_all[0]
    for k in range(1, line_count):
        total = total + m.small_all[k]
    m.small[...] = total
    for w in ("attended", "hidden", "gate", "update", "shared", "value"):
        line.end(at_w[w])


def rear(ident, line_count, ins):
    count, width = ins["tok"].shape
    groups, nj = width // 128, ins["damp"].shape[0]
    full = 4 * width
    nb = count // 256
    values = ins["value_grad"].shape[1]
    shapes = [(full, Z), (full, values), (full, values), (width, full), (values, full), (width, full)]
    turns, kinds, sizes, shapes, blocks = line_plan(shapes, KINDS[:-2], line_count)
    dma, s, v, k = pltpu.SemaphoreType.DMA, jax.ShapeDtypeStruct, pltpu.VMEM, len(REAR_WEIGHTS)
    tall = 2 * nj + 8
    n = 12 + 12 * nb
    lanes = v((groups, count, 128), F32)
    got = v((3, 2 * nb, 128, width), BF16)
    scratch = dict(
        part_v=v((4, count, width), BF16),
        got_v=got, got_t=got,
        part_s=v((count, Z), BF16),
        got_s=v((3, 2, 128, Z), BF16),
        low_s=v((256, Z), BF16),
        full_s=v((count, Z), BF16),
        grad_mix=lanes, back=lanes,
        rows=v((4, 8, count), F32),
        ends=v((4, nj, 8, width), F32),
        starts=v((2, nj, 8, width), F32),
        end_out=v((2, nj, width), F32),
        end_in=v((2, nj, width), F32),
        small_core=v((tall, width), F32),
        small_all=v((line_count, tall, width), F32),
        own_q=v((8, width), F32),
        all_q=v((4, 8, width), F32),
        upd_cols=v((width, full) if turns[REAR_WEIGHTS.index("update")] else (full, width), BF16),
        send=dma((n,)), recv=dma((n,)), s_rows=dma((3,)), r_rows=dma((3,)), s_core=dma((1,)), r_core=dma((1,)),
        s_upd=dma((4,)), r_upd=dma((3,)), s_small=dma((line_count,)), r_small=dma((line_count,)),
        s_q=dma((3,)), r_q=dma((3,)), s_in=dma((len(REAR_LOAD),)),
        c_send=dma((k, line_count)), c_recv=dma((k, line_count)),
        l_send=dma((k, line_count)), l_recv=dma((k, line_count + 1)),
    )
    got = pl.pallas_call(
        functools.partial(rear_kernel, kinds, sizes, turns, line_count),
        out_shape=[s((count, width), F32), s((tall, width), F32)] + [s(b, F32) for b in blocks],
        in_specs=[ANY if name in REAR_LOAD else VMEM for name in REAR_IN],
        out_specs=[VMEM] * len(REAR_OUT),
        scratch_shapes=[scratch[name] for name in REAR_SCRATCH]
        + [v((line_count,) + b, BF16) for b in blocks]
        + [v((line_count + 1,) + b, BF16) for b in blocks]
        + [v(shape, BF16) for shape in shapes]
        + [v(ins[name].shape, ins[name].dtype) for name in REAR_LOAD],
        compiler_params=pltpu.CompilerParams(collective_id=ident, has_side_effects=True, vmem_limit_bytes=62 * 2**20),
        name="rear",
    )(*[ins[name] for name in REAR_IN])
    grads = [g.T if turn else g for turn, g in zip(turns, got[2:])]
    return got[0], got[1], grads


def finish_kernel(count, nj, *refs):
    small, sources, (norm, damp, eta, query, key, ffn) = refs[0], refs[1 : 1 + count], refs[1 + count : 7 + count]
    places, held, sem = refs[7 + count : 7 + 2 * count], refs[7 + 2 * count : -1], refs[-1]
    copies = [pltpu.make_async_copy(src, dst, sem.at[0, k]) for k, (src, dst) in enumerate(zip(sources, held))]
    for copy in copies:
        copy.start()
    damp[...] = small[0:nj, :]
    eta[...] = small[nj : 2 * nj, :]
    norm[...] = small[2 * nj : 2 * nj + 1, :]
    ffn[...] = small[2 * nj + 1 : 2 * nj + 2, :]
    query[...] = small[2 * nj + 2 : 2 * nj + 3, 0:Z]
    key[...] = small[2 * nj + 2 : 2 * nj + 3, Z : 2 * Z]
    outs = [pltpu.make_async_copy(src, dst, sem.at[1, k]) for k, (src, dst) in enumerate(zip(held, places))]
    for copy, out in zip(copies, outs):
        copy.wait()
        out.start()
    for out in outs:
        out.wait()


def finish(small, nj, arrays):
    s, width, k = jax.ShapeDtypeStruct, small.shape[1], len(arrays)
    row, table, unit = s((1, width), F32), s((nj, width), F32), s((1, Z), F32)
    got = pl.pallas_call(
        functools.partial(finish_kernel, k, nj),
        out_shape=[row, table, table, unit, unit, row] + [s(a.shape, a.dtype) for a in arrays],
        in_specs=[VMEM] + [ANY] * k,
        out_specs=[VMEM] * 6 + [ANY] * k,
        scratch_shapes=[pltpu.VMEM(a.shape, a.dtype) for a in arrays] + [pltpu.SemaphoreType.DMA((2, k))],
        compiler_params=pltpu.CompilerParams(vmem_limit_bytes=60 * 2**20),
        name="finish",
    )(small, *arrays)
    return got[:6], got[6:]


def on_device(
    line_count,
    layer_input, segment_ids, cotangent, norm_gain, ema_damping, ema_eta, query_gain, key_gain,
    ffn_gain, *weights,
):
    tok, cot = layer_input[0], cotangent[0]
    segment = segment_ids[0]
    row_count = tok.shape[0]
    core = lax.axis_index("ctx")
    offset = core * row_count
    all_ids = lax.all_gather(segment, "ctx", axis=0, tiled=True)
    same = jnp.concatenate(
        [jnp.zeros((1,), F32), (all_ids[1:] == all_ids[:-1]).astype(F32), jnp.zeros((8,), F32)]
    )
    keep_wide = jnp.broadcast_to(lax.dynamic_slice_in_dim(same, offset, row_count + 8, 0)[:, None], (row_count + 8, 128))
    prev_ids = jnp.where(core > 0, all_ids[:row_count], -1)
    ids_row = jnp.broadcast_to(jnp.concatenate([prev_ids, segment]).astype(F32)[None], (8, 2 * row_count))
    a = front(
        1, line_count, tok, keep_wide, norm_gain, ema_damping, ema_eta, query_gain, key_gain, ids_row, cot, weights
    )
    ins = {n: getattr(a, n) for n in MID_LOAD if n != "w_upd"}
    ins.update(w_upd=a.rows_update, tok=tok, cot=cot, f_gain=ffn_gain[None], ids_row=ids_row)
    m = middle(2, line_count, ins)
    ins = {n: getattr(m if n in MID_OUT else a, n) for n in REAR_IN if n in MID_OUT or n in A_OUT}
    ins.update(
        tok=tok, keep_next=keep_wide, gain=norm_gain[None], damp=ema_damping, eta=ema_eta,
        q_gain=query_gain[None], k_gain=key_gain[None],
    )
    grad_in, small, grads = rear(3, line_count, ins)
    (norm, damp, eta, query, key, ffn), (out, grad_in, *grads) = finish(
        small, ema_damping.shape[0], [m.out, grad_in, *grads, m.d_up, m.d_down]
    )
    return (out[None], grad_in[None], norm[0], damp, eta, query[0], key[0], ffn[0], *grads)


def solution(mesh):
    token = P("fsdp", "ctx", "tp")
    row, col = P(("fsdp", "ctx"), "tp"), P("tp", ("fsdp", "ctx"))
    shared = P(("fsdp", "ctx"), None)
    weights = (shared, row, row, col, col, col, row, col)
    small = P(None, "tp")
    return jax.shard_map(
        functools.partial(on_device, mesh.shape["fsdp"]),
        mesh=mesh,
        in_specs=(token, P("fsdp", "ctx"), token, P("tp"), small, small, P(), P(), P("tp")) + weights,
        out_specs=(token, token, P("tp"), small, small, P(), P(), P("tp")) + weights,
        check_vma=False,
    )
```

```python
import functools
import inspect
import math
import types

import jax
import jax.numpy as jnp
from jax import lax
from jax.experimental import pallas as pl
from jax.experimental.pallas import tpu as pltpu
from jax.sharding import PartitionSpec as P

D = 1024
Z = 128
EPSILON = 1e-06
MESH = pl.DeviceIdType.MESH
F32 = jnp.float32
BF16 = jnp.bfloat16
VMEM = pl.BlockSpec(memory_space=pltpu.VMEM)
ANY = pl.BlockSpec(memory_space=pl.ANY)
HIGH = lax.Precision.HIGHEST


def named(signature):
    return list(inspect.signature(signature).parameters)


def spot(f=None, c=None, t=None):
    return (
        lax.axis_index("fsdp") if f is None else f,
        lax.axis_index("ctx") if c is None else c,
        lax.axis_index("tp") if t is None else t,
    )


def greet(devices):
    barrier = pltpu.get_barrier_semaphore()
    for device in devices:
        pl.semaphore_signal(barrier, inc=1, device_id=device, device_id_type=MESH)
    pl.semaphore_wait(barrier, len(devices))


def tp_peers():
    t = lax.axis_index("tp")
    return t, t + 1 - 2 * (t % 2), (t + 2) % 4, 3 - t


def remote(src, dst, send, recv, device):
    return pltpu.make_async_remote_copy(
        src_ref=src, dst_ref=dst, send_sem=send, recv_sem=recv, device_id=device, device_id_type=MESH
    )


class Gather:
    def __init__(self, count, source, place, send, recv, base=0):
        self.count, self.half = count, count // 2
        self.source, self.place, self.send, self.recv, self.base = source, place, send, recv, base
        self.t, self.x, self.y, _ = tp_peers()

    def copy(self, src, owner, i, way, to):
        n = self.base + way * self.count + i
        return remote(src, self.place(owner, i), self.send.at[n], self.recv.at[n], spot(t=to))

    def first(self, i, way):
        return self.copy(self.source(i), self.t, i, way, self.x if way == 0 else self.y)

    def start(self):
        for k in range(self.half):
            self.first(k, 0).start()
            self.first(k + self.half, 1).start()
        for k in range(self.half):
            self.first(k + self.half, 0).start()
            self.first(k, 1).start()

    def onward(self, i):
        if i < self.half:
            return self.copy(self.place(self.x, i), self.x, i, 2, self.y)
        return self.copy(self.place(self.y, i), self.y, i, 2, self.x)

    def begin(self, k):
        self.first(k, 0).start()
        self.first(k + self.half, 1).start()
        self.first(k + self.half, 0).start()
        self.first(k, 1).start()

    def pass_on(self, k):
        self.first(k, 0).wait_recv()
        self.onward(k).start()
        self.first(k + self.half, 1).wait_recv()
        self.onward(k + self.half).start()

    def forward(self):
        for k in range(self.half):
            self.pass_on(k)

    def finish(self):
        for k in range(self.half):
            self.first(k + self.half, 0).wait_recv()
            self.first(k, 1).wait_recv()
        for i in range(self.count):
            self.onward(i).wait()
            self.first(i, 0).wait_send()
            self.first(i, 1).wait_send()


class Scatter:
    def __init__(self, count, part, first_diag, first_own, second, send, recv, base=0):
        self.count, self.part = count, part
        self.diag, self.own, self.second = first_diag, first_own, second
        self.send, self.recv, self.base = send, recv, base
        self.t, self.x, self.y, self.d = tp_peers()

    def ways(self, i):
        return (self.x, self.y) if i % 2 == 0 else (self.y, self.x)

    def copy(self, i, kind):
        near, far = self.ways(i)
        n = self.base + kind * self.count + i
        if kind == 0:
            src, dst, to = self.part(self.d, i), self.diag(i), near
        elif kind == 1:
            src, dst, to = self.part(near, i), self.own(i), near
        else:
            src, dst, to = self.part(far, i), self.second(i), far
        return remote(src, dst, self.send.at[n], self.recv.at[n], spot(t=to))

    def start(self):
        for i in range(self.count):
            self.copy(i, 0).start()
        for i in range(self.count):
            self.copy(i, 1).start()

    def forward(self):
        for i in range(self.count):
            self.copy(i, 0).wait_recv()
            mine = self.part(self.ways(i)[1], i)
            mine[...] = (mine[...].astype(F32) + self.diag(i)[...].astype(F32)).astype(BF16)
            self.copy(i, 2).start()

    def collect(self, i):
        self.copy(i, 1).wait_recv()
        self.copy(i, 2).wait_recv()
        return self.own(i)[...].astype(F32) + self.second(i)[...].astype(F32)

    def finish(self):
        for i in range(self.count):
            for kind in range(3):
                self.copy(i, kind).wait_send()


def shard_at(ref, kind, index, size):
    if kind == "row":
        return ref.at[pl.ds(pl.multiple_of(index * size, size), size)]
    return ref.at[:, pl.ds(pl.multiple_of(index * size, size), size)]


def turned(kind, size):
    return kind == "col" and size % 128 != 0


def row_exchange(rows, send, recv):
    t, x, y, d = tp_peers()
    return [
        remote(rows.at[t], rows.at[t], send.at[k], recv.at[k], spot(t=p))
        for k, p in enumerate((x, y, d))
    ]


class Named:
    def __init__(self, names, refs):
        for name, ref in zip(names, refs, strict=True):
            setattr(self, name, ref)


class Transfer:
    def __init__(self, copy):
        self.copy, self.waited = copy, False

    def start(self):
        self.copy.start()

    def wait(self):
        if not self.waited:
            self.waited = True
            self.copy.wait()


def need(*transfers):
    for transfer in transfers:
        transfer.wait()


def dot(left, right):
    return jnp.dot(left, right, preferred_element_type=F32)


def dot_t(left, right):
    return lax.dot_general(left, right, (((1,), (1,)), ((), ())), preferred_element_type=F32)


def t_dot(left, right):
    return lax.dot_general(left, right, (((0,), (0,)), ((), ())), preferred_element_type=F32)


def sigmoid(v):
    return 1.0 / (1.0 + jnp.exp(-v))


def d_silu(v, s):
    return s * (1.0 + v * (1.0 - s))


def as_rows(column):
    return jnp.broadcast_to(column, (column.shape[0], 128)).T[0:8]


def as_column(rows):
    return rows.T[:, 0:1]


def at_block(i, size):
    return pl.ds(i * size if isinstance(i, int) else pl.multiple_of(i * size, size), size)


def wide(row):
    return jnp.broadcast_to(row, (8, 128))


def tree_sum(terms):
    while len(terms) > 1:
        terms = [a + b for a, b in zip(terms[::2], terms[1::2])]
    return terms[0]


def power(base, exponent):
    result, square = None, base
    while exponent:
        if exponent & 1:
            result = square if result is None else result * square
        exponent >>= 1
        if exponent:
            square = square * square
    return result


def row_sums(values):
    return lax.dot_general(
        jnp.ones((8, values.shape[1]), F32), values, (((1,), (1,)), ((), ())),
        precision=HIGH, preferred_element_type=F32,
    )


class Line:
    def __init__(self, kinds, sizes, count, sources, places, sems):
        self.kinds, self.sizes, self.count = kinds, sizes, count
        self.sources, self.places = sources, places
        self.here, self.send_up, self.send_down, self.send_core, self.recv, self.recv_core = sems
        self.z, self.c = lax.axis_index("fsdp"), lax.axis_index("ctx")
        self.other = spot(c=1 - self.c)
        self.up = spot(f=(self.z + 1) % count)
        self.down = spot(f=(self.z + count - 1) % count)
        self.next = {}

    def slot(self, w, owner, core):
        return shard_at(self.places[w], self.kinds[w], owner * 2 + core, self.sizes[w])

    def to_core(self, w, owner, src):
        return remote(
            src, self.slot(w, owner, self.c), self.send_core.at[w, owner], self.recv_core.at[w, owner], self.other
        )

    def to_up(self, w, owner, src):
        return remote(src, self.slot(w, owner, self.c), self.send_up.at[w, owner], self.recv.at[w, owner], self.up)

    def to_down(self, w, owner, src):
        return remote(src, self.slot(w, owner, self.c), self.send_down.at[w, owner], self.recv.at[w, owner], self.down)

    def keep(self, w):
        return pltpu.make_async_copy(self.sources[w], self.slot(w, self.z, self.c), self.here.at[w])

    def own(self, group):
        for w in group:

            @pl.when(self.z + 1 < self.count)
            def _():
                self.to_up(w, self.z, self.sources[w]).start()

            @pl.when(self.z > 0)
            def _():
                self.to_down(w, self.z, self.sources[w]).start()

            self.to_core(w, self.z, self.sources[w]).start()
            self.keep(w).start()
            self.next[w] = 1

    def hand_on(self, w, step):
        low, high = self.z - step, self.z + step

        @pl.when(low >= 0)
        def _():
            got = self.slot(w, low, self.c)
            self.to_up(w, low, got).wait_recv()

            @pl.when(self.z + 1 < self.count)
            def _():
                self.to_up(w, low, got).start()

            self.to_core(w, low, got).start()

        @pl.when(high < self.count)
        def _():
            got = self.slot(w, high, self.c)
            self.to_down(w, high, got).wait_recv()

            @pl.when(self.z > 0)
            def _():
                self.to_down(w, high, got).start()

            self.to_core(w, high, got).start()

    def pump(self, group):
        for w in group:
            if self.next[w] < self.count:
                self.hand_on(w, self.next[w])
                self.next[w] += 1

    def done(self, group):
        for w in group:
            if self.next[w] < self.count:

                @pl.loop(self.next[w], self.count)
                def _(step):
                    self.hand_on(w, step)

            @pl.loop(0, self.count)
            def _(owner):
                got = self.slot(w, owner, self.c)
                self.to_core(w, owner, got).wait()

                @pl.when((owner <= self.z) & (self.z + 1 < self.count))
                def _():
                    self.to_up(w, owner, got).wait_send()

                @pl.when((owner >= self.z) & (self.z > 0))
                def _():
                    self.to_down(w, owner, got).wait_send()

            self.keep(w).wait()


WEIGHTS = named(lambda shared, value, gate, hidden, attended, update, up, down: None)
KINDS = ("row", "row", "row", "col", "col", "col", "row", "col")
FRONT_WEIGHTS = WEIGHTS
A_IN = named(lambda tok, keep, gain, damp, eta, q_gain, k_gain, ids_row, cot: None) + ["s_" + w for w in FRONT_WEIGHTS]
A_OUT = named(
    lambda rows_update, normed4, mixed4, mix_pre, xn, inv_rows, s_pre, v_pre, g_pre, keys, vals,
    queries, log_sum, attended, gated, hid_pre, upd_pre, cot4: None
) + ["w_" + w for w in FRONT_WEIGHTS if w != "update"]
A_HBM = named(
    lambda rows_update, normed4, mixed4, mix_pre, xn, v_pre, g_pre, keys, vals, attended, gated,
    hid_pre, upd_pre, cot4: None
) + [
    "w_" + w for w in FRONT_WEIGHTS if w != "update"
]
A_SCRATCH = named(
    lambda low_n, low_m, rows, ends, starts, end_out, end_in, part_h, got_h, w_update, send, recv,
    s_rows, r_rows, s_core, r_core, s_upd, r_upd, s_kv, r_kv, s_out, z_here, z_up, z_down, z_core,
    z_recv, z_recv_core: None
)


def front_kernel(kinds, sizes, turns, line_count, *refs):
    aside = [w for w, turn in zip(FRONT_WEIGHTS, turns) if turn and w != "down"]
    names = A_IN + A_OUT + A_SCRATCH + ["v_" + n for n in A_HBM] + ["t_" + w for w in aside]
    m = Named(names, refs)
    outs = {}
    for k, n in enumerate(A_HBM):
        outs[n] = pltpu.make_async_copy(getattr(m, "v_" + n), getattr(m, n), m.s_out.at[k])
        setattr(m, n, getattr(m, "v_" + n))
    out = types.SimpleNamespace(**outs)
    t, x, y, d = tp_peers()
    c = lax.axis_index("ctx")
    other = spot(c=1 - c)
    groups, count = m.xn.shape[0], m.xn.shape[1]
    step, nj, width = count // 8, m.damp.shape[0], m.damp.shape[1]
    B = 256
    half, nb, span = B // 2, count // B, count + B
    scale = 1.0 / math.sqrt(Z)

    def lanes(o):
        return pl.ds(pl.multiple_of(o * width, width), width)

    line = Line(
        kinds, sizes, line_count, [getattr(m, "s_" + w) for w in FRONT_WEIGHTS],
        [getattr(m, ("t_" if w in aside else "w_") + w) for w in FRONT_WEIGHTS],
        (m.z_here, m.z_up, m.z_down, m.z_core, m.z_recv, m.z_recv_core),
    )
    first_w, second_w, third_w, fourth_w = (0, 1, 2), (3, 4, 5), (6,), (7,)

    m.end_in[...] = jnp.zeros_like(m.end_in)
    value = m.tok[...].astype(F32)
    m.rows[t] = row_sums(value * value)
    greet([spot(t=x), spot(t=y), spot(t=d), other, line.up, line.down])
    sums = [
        remote(m.rows.at[t], m.rows.at[t], m.s_rows.at[k], m.r_rows.at[k], spot(t=p))
        for k, p in enumerate((x, y, d))
    ]
    for copy in sums:
        copy.start()
    line.own(first_w)
    line.own(second_w)
    for copy in sums:
        copy.wait()
    inv = lax.rsqrt((m.rows[0] + m.rows[1] + m.rows[2] + m.rows[3]) / D + EPSILON)
    m.inv_rows[...] = inv
    normed = m.tok[...].astype(F32) * inv.T[:, 0:1] * m.gain[...]
    m.low_n[...] = normed.astype(BF16)
    for g in range(groups):
        m.xn[g] = normed[:, g * 128 : (g + 1) * 128]
    out.xn.start()
    chunks = 8
    size = count // chunks

    def whole_run(low, place, base):
        return Gather(
            chunks,
            lambda i: low.at[pl.ds(i * size, size)],
            lambda o, i: place.at[pl.ds(i * size, size), lanes(o)],
            m.send, m.recv, base,
        )

    norm_run = whole_run(m.low_n, m.normed4, 0)
    cot_run = whole_run(m.cot, m.cot4, 24)
    mix_run = whole_run(m.low_m, m.mixed4, 48)
    norm_run.start()

    for g in range(groups):
        ln = pl.ds(g * 128, 128)
        decay = [wide(1.0 - m.damp[pl.ds(j, 1), ln]) for j in range(nj)]

        def scan(s, carry):
            states, chain = carry
            at = pl.ds(s, 8, stride=step)
            v, k = m.xn[g, at, :], m.keep[at, :]
            return tuple(v + (k * r) * a for r, a in zip(decay, states)), chain * k

        zero = jnp.zeros((8, 128), F32)
        states, chain = lax.fori_loop(0, step, scan, ((zero,) * nj, zero + 1.0), unroll=8)
        for j in range(nj):
            m.ends[0, j, :, ln] = states[j]
            m.ends[1, j, :, ln] = power(decay[j], step) * chain

    last = jnp.zeros((nj, width), F32)
    for q in range(8):
        last = m.ends[0, :, q, :] + m.ends[1, :, q, :] * last
    m.end_out[...] = last
    across = remote(m.end_out, m.end_in, m.s_core.at[0], m.r_core.at[0], other)
    across.start()
    line.pump(first_w)
    across.wait()
    last = jnp.where(c == 0, 0.0, m.end_in[...])
    for q in range(8):
        m.starts[:, q, :] = last
        last = m.ends[0, :, q, :] + m.ends[1, :, q, :] * last

    for g in range(groups):
        ln = pl.ds(g * 128, 128)
        decay = [wide(1.0 - m.damp[pl.ds(j, 1), ln]) for j in range(nj)]
        weight = [wide(m.damp[pl.ds(j, 1), ln] * m.eta[pl.ds(j, 1), ln]) for j in range(nj)]

        def scan(s, states):
            at = pl.ds(s, 8, stride=step)
            v, k = m.xn[g, at, :], m.keep[at, :]
            states = tuple(v + (k * r) * a for r, a in zip(decay, states))
            m.mix_pre[g, at, :] = v + tree_sum([w * a for w, a in zip(weight, states)])
            return states

        lax.fori_loop(0, step, scan, tuple(m.starts[j, :, ln] for j in range(nj)), unroll=8)
        pre = m.mix_pre[g]
        m.low_m[:, ln] = (pre * sigmoid(pre)).astype(BF16)
    norm_run.forward()
    mix_run.start()
    out.mix_pre.start()
    line.pump(first_w)
    line.pump(second_w)
    line.own(third_w)
    for o in range(4):

        @pl.when(t == o)
        def _():
            m.normed4[:, o * width : (o + 1) * width] = m.low_n[...]
            m.mixed4[:, o * width : (o + 1) * width] = m.low_m[...]
            m.cot4[:, o * width : (o + 1) * width] = m.cot[...]

    mix_run.forward()
    line.pump(first_w)
    line.pump(second_w)
    line.own(fourth_w)
    norm_run.finish()
    out.normed4.start()
    line.done(first_w)
    for copy in (out.w_shared, out.w_value, out.w_gate):
        copy.start()

    def rows(i):
        return at_block(i, B)

    def mine(i):
        return pl.ds(pl.multiple_of(count + i * B, B), B)

    def window(i):
        return pl.ds(pl.multiple_of(i * B, B), span)

    def kv_run(i):
        return [
            remote(m.keys.at[mine(i)], m.keys.at[rows(i)], m.s_kv.at[2 * i], m.r_kv.at[2 * i], other),
            remote(m.vals.at[mine(i)], m.vals.at[rows(i)], m.s_kv.at[2 * i + 1], m.r_kv.at[2 * i + 1], other),
        ]

    @pl.loop(0, nb)
    def _(i):
        value = dot(m.normed4[rows(i), :], m.w_value[...])
        m.v_pre[rows(i), :] = value.astype(BF16)
        m.vals[mine(i), :] = (value * sigmoid(value)).astype(BF16)
        kv_run(i)[1].start()

    out.v_pre.start()
    mix_run.finish()
    out.mixed4.start()
    cot_run.start()

    @pl.loop(0, nb)
    def _(i):
        pre = dot(m.mixed4[rows(i), :], m.w_shared[...])
        m.s_pre[rows(i), :] = pre
        shared = pre * sigmoid(pre)
        m.queries[rows(i), :] = (shared * m.q_gain[...]).astype(BF16)
        m.keys[mine(i), :] = (shared * m.k_gain[...]).astype(BF16)
        kv_run(i)[0].start()

    @pl.loop(0, nb)
    def _(i):
        m.g_pre[rows(i), :] = dot(m.mixed4[rows(i), :], m.w_gate[...])

    out.g_pre.start()
    line.pump(second_w)
    line.pump(third_w)
    line.pump(fourth_w)
    for i in range(nb):
        for copy in kv_run(i):
            copy.wait()
    out.keys.start()
    out.vals.start()
    line.done(second_w)
    for w in aside:
        if w != "up":
            getattr(m, "w_" + w)[...] = getattr(m, "t_" + w)[...].astype(F32).T.astype(BF16)
    for copy in (out.w_hidden, out.w_attended):
        copy.start()
    upd = [
        remote(m.w_update.at[:, lanes(p)], m.rows_update.at[pl.ds(pl.multiple_of(t * width, width), width)],
               m.s_upd.at[n], m.r_upd.at[n], spot(t=p))
        for n, p in enumerate((x, y, d))
    ]
    for copy in upd:
        copy.start()
    for o in range(4):

        @pl.when(t == o)
        def _():
            m.rows_update[o * width : (o + 1) * width, :] = m.w_update[:, o * width : (o + 1) * width]

    def run_h(i):
        return Scatter(
            2,
            lambda o, n: m.part_h.at[o, pl.ds(pl.multiple_of(i * B + n * half, half), half)],
            lambda n: m.got_h.at[0, i * 2 + n],
            lambda n: m.got_h.at[1, i * 2 + n],
            lambda n: m.got_h.at[2, i * 2 + n],
            m.send, m.recv, 72 + i * 6,
        )

    def attend(i):
        raw = dot_t(m.queries[rows(i), :], m.keys[window(i), :]) * scale
        same = as_column(m.ids_row[:, mine(i)]) == m.ids_row[0:1, window(i)]
        place = lax.broadcasted_iota(jnp.int32, raw.shape, 1) - lax.broadcasted_iota(jnp.int32, raw.shape, 0)
        s = jnp.where(same & (place <= count), raw, -1e30)
        peak = jnp.max(s, axis=1, keepdims=True)
        e = jnp.exp(s - peak)
        total = jnp.sum(e, axis=1, keepdims=True)
        m.log_sum[rows(i), :] = jnp.broadcast_to(peak + jnp.log(total), (B, 128))
        attended = dot((e * (1.0 / total)).astype(BF16), m.vals[window(i), :])
        m.attended[rows(i), :] = attended.astype(BF16)
        gate = m.g_pre[rows(i), :]
        gated = (gate * sigmoid(gate) * attended).astype(BF16)
        m.gated[rows(i), :] = gated
        part = dot(m.mixed4[rows(i), lanes(t)], m.w_hidden[...]) + dot(gated, m.w_attended[...])
        part = part.astype(BF16)
        for o in range(4):
            m.part_h[o, rows(i), :] = part[:, o * width : (o + 1) * width]
        run_h(i).start()

    def collect(i):
        run = run_h(i)
        for n in range(2):
            m.hid_pre[pl.ds(i * B + n * half, half), :] = run.collect(n) + run.part(t, n)[...].astype(F32)
        run.finish()

    def attend_some(start, stop):
        @pl.loop(start, stop)
        def _(i):
            attend(i)

            @pl.when(i > 0)
            def _():
                run_h(i - 1).forward()

    attend_some(0, nb // 2)
    line.pump(third_w)
    line.pump(fourth_w)
    cot_run.forward()
    attend_some(nb // 2, nb)
    line.pump(third_w)
    line.pump(fourth_w)
    out.attended.start()
    out.gated.start()
    for copy in upd:
        copy.wait()

    @pl.loop(0, nb)
    def _(i):
        m.upd_pre[rows(i), :] = dot(m.mixed4[rows(i), :], m.rows_update[...])

    run_h(nb - 1).forward()
    out.upd_pre.start()
    out.rows_update.start()
    line.done(third_w)
    out.w_up.start()
    line.done(fourth_w)
    out.w_down.start()
    for i in range(nb):
        collect(i)
    out.hid_pre.start()
    cot_run.finish()
    out.cot4.start()
    for copy in outs.values():
        copy.wait()


def front(ident, line_count, tok, keep, gain, damp, eta, q_gain, k_gain, ids_row, cot, shards):
    count, width = tok.shape
    groups, nj = width // 128, damp.shape[0]
    nb = count // 256
    turns = [turned(k, s.shape[1]) for k, s in zip(KINDS, shards)]
    shards = [s.T if turn else s for turn, s in zip(turns, shards)]
    kinds = ["row" if turn else k for turn, k in zip(turns, KINDS)]
    sizes = [s.shape[0] if k == "row" else s.shape[1] for k, s in zip(kinds, shards)]
    full = 4 * width
    values = shards[1].shape[1]
    s = jax.ShapeDtypeStruct
    outs = dict(
        rows_update=s((full, width), BF16),
        normed4=s((count, full), BF16),
        mixed4=s((count, full), BF16),
        mix_pre=s((groups, count, 128), F32),
        xn=s((groups, count, 128), F32),
        inv_rows=s((8, count), F32),
        s_pre=s((count, Z), F32),
        v_pre=s((count, values), BF16),
        g_pre=s((count, values), F32),
        keys=s((2 * count, Z), BF16),
        vals=s((2 * count, values), BF16),
        queries=s((count, Z), BF16),
        log_sum=s((count, 128), F32),
        attended=s((count, values), BF16),
        gated=s((count, values), BF16),
        hid_pre=s((count, width), F32),
        upd_pre=s((count, width), F32),
        cot4=s((count, full), BF16),
    )
    aside = []
    for name, kind, size, shard in zip(FRONT_WEIGHTS, kinds, sizes, shards):
        shape = (2 * line_count * size, shard.shape[1]) if kind == "row" else (shard.shape[0], 2 * line_count * size)
        if turns[FRONT_WEIGHTS.index(name)] and name != "down":
            aside.append(pltpu.VMEM(shape, shard.dtype))
            shape = shape[::-1]
        outs["w_" + name] = s(shape, shard.dtype)
    v, dma, k = pltpu.VMEM, pltpu.SemaphoreType.DMA, len(FRONT_WEIGHTS)
    n = 72 + 6 * nb
    scratch = dict(
        low_n=v((count, width), BF16),
        low_m=v((count, width), BF16),
        rows=v((4, 8, count), F32),
        ends=v((2, nj, 8, width), F32),
        starts=v((nj, 8, width), F32),
        end_out=v((nj, width), F32),
        end_in=v((nj, width), F32),
        part_h=v((4, count, width), BF16),
        got_h=v((3, 2 * nb, 128, width), BF16),
        w_update=v(outs["w_update"].shape, BF16),
        send=dma((n,)), recv=dma((n,)), s_rows=dma((3,)), r_rows=dma((3,)), s_core=dma((1,)), r_core=dma((1,)),
        s_upd=dma((3,)), r_upd=dma((3,)), s_kv=dma((2 * nb,)), r_kv=dma((2 * nb,)), s_out=dma((len(A_HBM),)),
        z_here=dma((k,)), z_up=dma((k, line_count)), z_down=dma((k, line_count)), z_core=dma((k, line_count)),
        z_recv=dma((k, line_count)), z_recv_core=dma((k, line_count)),
    )
    got = pl.pallas_call(
        functools.partial(front_kernel, kinds, sizes, turns, line_count),
        out_shape=[outs[n] for n in A_OUT],
        in_specs=[VMEM] * len(A_IN),
        out_specs=[ANY if n in A_HBM else VMEM for n in A_OUT],
        scratch_shapes=[scratch[n] for n in A_SCRATCH] + [v(outs[n].shape, outs[n].dtype) for n in A_HBM] + aside,
        compiler_params=pltpu.CompilerParams(collective_id=ident, has_side_effects=True, vmem_limit_bytes=60 * 2**20),
        name="front",
    )(tok, keep, gain[None], damp, eta, q_gain[None], k_gain[None], ids_row, cot, *shards)
    return Named(A_OUT, got)


class LineSum:
    def __init__(self, kinds, sizes, count, sources, pair, line, outs, sems):
        self.kinds, self.sizes, self.count = kinds, sizes, count
        self.sources, self.pair, self.line, self.outs = sources, pair, line, outs
        self.send_core, self.recv_core, self.send, self.recv = sems
        self.z, self.c = lax.axis_index("fsdp"), lax.axis_index("ctx")
        self.other = spot(c=1 - self.c)

    def block(self, w, owner, core):
        return shard_at(self.sources[w], self.kinds[w], owner * 2 + core, self.sizes[w])

    def across(self, w, owner):
        return remote(
            self.block(w, owner, 1 - self.c), self.pair[w].at[owner],
            self.send_core.at[w, owner], self.recv_core.at[w, owner], self.other,
        )

    def along(self, w, k):
        owner = (self.z + k) % self.count
        far = ((self.z == 0) & (owner == self.count - 1)) | ((self.z == self.count - 1) & (owner == 0))
        to = jnp.where(far, jnp.where(self.z == 0, 1, self.count - 2), owner)
        at = jnp.where(far, self.count, self.z)
        return remote(
            self.pair[w].at[owner], self.line[w].at[at], self.send.at[w, k], self.recv.at[w, at], spot(f=to)
        )

    def helps(self, owner):
        return ((self.z == 1) & (owner == self.count - 1)) | ((self.z == self.count - 2) & (owner == 0))

    def relay(self, w):
        @pl.loop(1, self.count)
        def _(k):
            owner = (self.z + k) % self.count

            @pl.when(self.helps(owner))
            def _():
                got = self.line[w].at[self.count]
                remote(got, got, self.send.at[w, k], self.recv.at[w, self.count], self.other).wait_recv()
                self.pair[w][owner] = (self.pair[w][owner].astype(F32) + got[...].astype(F32)).astype(BF16)
                self.along(w, k).start()

    def start(self, w):
        @pl.loop(1, self.count + 1)
        def _(k):
            self.across(w, (self.z + k) % self.count).start()

    def plus(self, w, owner):
        return self.pair[w][owner].astype(F32) + self.block(w, owner, self.c)[...].astype(F32)

    def send_on(self, w):
        @pl.loop(1, self.count)
        def _(i):
            k = jnp.where(self.z == 0, self.count - i, i)
            owner = (self.z + k) % self.count
            self.across(w, owner).wait_recv()
            self.pair[w][owner] = self.plus(w, owner).astype(BF16)

            @pl.when(jnp.logical_not(self.helps(owner)))
            def _():
                self.along(w, k).start()

    def end(self, w):
        self.across(w, self.z).wait_recv()
        self.outs[w][...] = self.plus(w, self.z)

        @pl.loop(1, self.count)
        def _(k):
            source = (self.z + k) % self.count
            got = self.line[w].at[source]
            merged = ((self.z == 0) & (source == self.count - 1)) | ((self.z == self.count - 1) & (source == 0))

            @pl.when(jnp.logical_not(merged))
            def _():
                remote(got, got, self.send.at[w, k], self.recv.at[w, source], self.other).wait_recv()
                self.outs[w][...] += got[...].astype(F32)

            self.along(w, k).wait_send()

        @pl.loop(0, self.count)
        def _(owner):
            self.across(w, owner).wait_send()


def line_plan(shapes, kinds, count):
    turns = [turned(k, s[1] // (2 * count)) for k, s in zip(kinds, shapes)]
    shapes = [s[::-1] if turn else s for turn, s in zip(turns, shapes)]
    kinds = ["row" if turn else k for turn, k in zip(turns, kinds)]
    sizes = [s[0 if k == "row" else 1] // (2 * count) for k, s in zip(kinds, shapes)]
    blocks = [(n, s[1]) if k == "row" else (s[0], n) for k, n, s in zip(kinds, sizes, shapes)]
    return turns, kinds, sizes, shapes, blocks


def line_peers(count):
    z = lax.axis_index("fsdp")
    return [spot(f=(z + k) % count) for k in range(1, count)]


MID_LOAD = named(
    lambda hid_pre, upd_pre, w_up, w_down, cot4, w_attended, g_pre, attended, w_gate, w_upd,
    w_hidden, queries, keys, vals, log_sum, v_pre: None
)
MID_IN = MID_LOAD + named(lambda tok, cot, f_gain, ids_row: None)
MID_STORE = named(lambda out, part_t, tok_grad, mix_grad, value_grad, hid4, upd_grad, gate_grad: None)
MID_OUT = MID_STORE + named(lambda f_gain_grad, q_grad, k_grad, d_up, d_down: None)
MID_SCRATCH = named(
    lambda block, part_f, up_rows, up_grads, ffn4, att_grad, k_all, v_all, part_g, got_g, low,
    rows_a, rows_b, k_send, v_send, k_got, v_got, p_up, p_down, l_up, l_down, send, recv, s_rows,
    r_rows, s_gr, r_gr, s_in, s_out, c_send, c_recv, l_send, l_recv: None
)


def mid_kernel(kinds, sizes, turn, line_count, *refs):
    m = Named(
        MID_IN + MID_OUT + MID_SCRATCH + ["i_" + n for n in MID_LOAD] + ["o_" + n for n in MID_STORE], refs
    )
    loads, stores = {}, {}
    for k, n in enumerate(MID_LOAD):
        loads[n] = Transfer(pltpu.make_async_copy(getattr(m, n), getattr(m, "i_" + n), m.s_in.at[k]))
        setattr(m, n, getattr(m, "i_" + n))
        loads[n].start()
    for k, n in enumerate(MID_STORE):
        stores[n] = pltpu.make_async_copy(getattr(m, "o_" + n), getattr(m, n), m.s_out.at[k])
        setattr(m, n, getattr(m, "o_" + n))
    load, store = types.SimpleNamespace(**loads), types.SimpleNamespace(**stores)
    t, x, y, d = tp_peers()
    other = spot(c=1 - lax.axis_index("ctx"))
    count, width = m.tok.shape
    hidden = m.w_up.shape[1]
    B = 256
    half, nb, span = B // 2, count // B, count + B
    scale = 1.0 / math.sqrt(Z)

    def rows(i):
        return at_block(i, B)

    def mine(i):
        return pl.ds(count + i * B, B)

    def window(i):
        return pl.ds(i * B, span)

    def lanes(o):
        return pl.ds(pl.multiple_of(o * width, width), width)

    greet([spot(t=x), spot(t=y), spot(t=d), other] + line_peers(line_count))
    m.f_gain_grad[...] = jnp.zeros_like(m.f_gain_grad)

    def gather_run(kind, i, low, place):
        return Gather(
            2,
            lambda n: low.at[pl.ds(i * B + n * half, half)],
            lambda o, n: place.at[pl.ds(i * B + n * half, half), lanes(o)],
            m.send, m.recv, (kind * nb + i) * 6,
        )

    def scatter_run(kind, i, part, got):
        return Scatter(
            2,
            lambda o, n: part.at[o, pl.ds(i * B + n * half, half)],
            lambda n: got.at[0, i * 2 + n],
            lambda n: got.at[1, i * 2 + n],
            lambda n: got.at[2, i * 2 + n],
            m.send, m.recv, (kind * nb + i) * 6,
        )

    run_p = [gather_run(0, i, m.low, m.ffn4) for i in range(nb)]
    run_gh = [gather_run(1, i, m.low, m.hid4) for i in range(nb)]
    run_g = [scatter_run(2, i, m.part_g, m.got_g) for i in range(nb)]
    run_f = [scatter_run(3, i, m.part_f, m.got_g) for i in range(nb)]
    line = LineSum(
        kinds, sizes, line_count, [m.w_up, m.w_down], [m.p_up, m.p_down], [m.l_up, m.l_down], [m.d_up, m.d_down],
        (m.c_send, m.c_recv, m.l_send, m.l_recv),
    )

    def row_run(kind, i, buf):
        return [
            remote(
                buf.at[t, :, rows(i)], buf.at[t, :, rows(i)],
                m.s_rows.at[(kind * nb + i) * 3 + n], m.r_rows.at[(kind * nb + i) * 3 + n], spot(t=p),
            )
            for n, p in enumerate((x, y, d))
        ]

    def row_total(buf, i):
        return buf[0, :, rows(i)] + buf[1, :, rows(i)] + buf[2, :, rows(i)] + buf[3, :, rows(i)]

    def split(part, i, value):
        low = value.astype(BF16)
        for o in range(4):
            part[o, rows(i), :] = low[:, o * width : (o + 1) * width]

    def place_own(full_ref, i):
        for o in range(4):

            @pl.when(t == o)
            def _():
                full_ref[rows(i), o * width : (o + 1) * width] = m.low[rows(i), :]

    def joined(run):
        pieces = [run.collect(n) + run.part(t, n)[...].astype(F32) for n in range(2)]
        return jnp.concatenate(pieces, axis=0)

    def inverse_mid(i):
        return lax.rsqrt(row_total(m.rows_a, i) / D + EPSILON)

    def block_stage(i):
        need(load.hid_pre, load.upd_pre)
        hidden_pre, update = m.hid_pre[rows(i), :], sigmoid(m.upd_pre[rows(i), :])
        block = update * (hidden_pre * sigmoid(hidden_pre)) + (1.0 - update) * m.tok[rows(i), :].astype(F32)
        m.block[rows(i), :] = block
        m.low[rows(i), :] = (block * m.f_gain[...]).astype(BF16)
        run_p[i].start()
        m.rows_a[t, :, rows(i)] = as_rows(jnp.sum(block * block, axis=1, keepdims=True))
        for copy in row_run(0, i, m.rows_a):
            copy.start()
        place_own(m.ffn4, i)

    def up_stage(i):
        need(load.w_up)
        run_p[i].finish()
        raw = dot(m.ffn4[rows(i), :], m.w_up[...])
        part = m.v_all.shape[1]
        parts = hidden // part
        for k in range(parts):
            m.v_all[pl.ds((parts * i + k) * B, B), :] = raw[:, k * part : (k + 1) * part]

    down, down_t = (dot_t, dot) if turn else (dot, dot_t)

    def ffn_stage(i):
        need(load.w_down, load.cot4)
        back = down_t(m.cot4[rows(i), :], m.w_down[...])
        for copy in row_run(0, i, m.rows_a):
            copy.wait()
        inv = as_column(inverse_mid(i))
        parts = hidden // m.v_all.shape[1]
        raw = jnp.concatenate([m.v_all[pl.ds((parts * i + k) * B, B), :] for k in range(parts)], axis=1)
        up_pre = raw * inv
        sig = sigmoid(up_pre)
        grad_up = (back * d_silu(up_pre, sig)).astype(BF16)
        split(m.part_g, i, dot_t(grad_up, m.w_up[...]))
        run_g[i].start()
        wide_grad = grad_up.astype(F32)
        m.up_grads[rows(i), :] = (wide_grad * inv).astype(BF16)
        m.rows_b[t, :, rows(i)] = as_rows(jnp.sum(wide_grad * raw, axis=1, keepdims=True))
        for copy in row_run(1, i, m.rows_b):
            copy.start()
        up_rows = (up_pre * sig).astype(BF16)
        m.up_rows[rows(i), :] = up_rows
        split(m.part_f, i, down(up_rows, m.w_down[...]))

    def grad_stage(i):
        grad_ffn = joined(run_g[i])
        for copy in row_run(1, i, m.rows_b):
            copy.wait()
        block = m.block[rows(i), :]
        inv_rows = inverse_mid(i)
        factor = inv_rows * inv_rows * inv_rows * row_total(m.rows_b, i) / D
        inv = as_column(inv_rows)
        grad_block = (
            m.cot[rows(i), :].astype(F32) + inv * (grad_ffn * m.f_gain[...]) - block * as_column(factor)
        )
        m.f_gain_grad[...] += jnp.sum(grad_ffn * block * inv, axis=0, keepdims=True)
        hidden_pre, update = m.hid_pre[rows(i), :], sigmoid(m.upd_pre[rows(i), :])
        sig = sigmoid(hidden_pre)
        m.low[rows(i), :] = (grad_block * update * d_silu(hidden_pre, sig)).astype(BF16)
        run_gh[i].start()
        keep = grad_block * (1.0 - update)
        m.tok_grad[rows(i), :] = keep
        tokens = m.tok[rows(i), :].astype(F32)
        m.upd_grad[rows(i), :] = (keep * (hidden_pre * sig - tokens) * update).astype(BF16)
        place_own(m.hid4, i)
        run_g[i].finish()

    def gate_stage(i):
        need(load.w_attended, load.g_pre, load.attended, load.w_gate, load.w_upd, load.w_hidden)
        run_gh[i].finish()
        grad_hidden = m.hid4[rows(i), :]
        grad_gated = dot_t(grad_hidden, m.w_attended[...])
        gate = m.g_pre[rows(i), :]
        sig = sigmoid(gate)
        grad_gate = (grad_gated * m.attended[rows(i), :].astype(F32) * d_silu(gate, sig)).astype(BF16)
        m.gate_grad[rows(i), :] = grad_gate
        split(m.part_t, i, dot_t(grad_gate, m.w_gate[...]) + dot_t(m.upd_grad[rows(i), :], m.w_upd[...]))
        m.att_grad[rows(i), :] = (grad_gated * (gate * sig)).astype(BF16)
        m.mix_grad[rows(i), :] = dot_t(grad_hidden, m.w_hidden[...])

    def grads_run(i):
        return [
            remote(m.k_send.at[rows(i)], m.k_got.at[rows(i)], m.s_gr.at[2 * i], m.r_gr.at[2 * i], other),
            remote(m.v_send.at[rows(i)], m.v_got.at[rows(i)], m.s_gr.at[2 * i + 1], m.r_gr.at[2 * i + 1], other),
        ]

    def attend_back(i):
        need(load.queries, load.keys, load.vals, load.log_sum)
        raw = dot_t(m.queries[rows(i), :], m.keys[window(i), :]) * scale
        same = as_column(m.ids_row[:, mine(i)]) == m.ids_row[0:1, window(i)]
        place = lax.broadcasted_iota(jnp.int32, raw.shape, 1) - lax.broadcasted_iota(jnp.int32, raw.shape, 0)
        exact = jnp.exp(jnp.where(same & (place <= count), raw, -1e30) - m.log_sum[rows(i), 0:1])
        grad_rows = m.att_grad[rows(i), :]
        value_part = t_dot(exact.astype(BF16), grad_rows)
        grad_probs = dot_t(grad_rows, m.vals[window(i), :])
        inner = jnp.sum(exact * grad_probs, axis=1, keepdims=True)
        grad_scores = exact * (grad_probs - inner) * scale
        high = grad_scores.astype(BF16)
        rest = (grad_scores - high.astype(F32)).astype(BF16)
        keys, queries = m.keys[window(i), :], m.queries[rows(i), :]
        m.q_grad[rows(i), :] = dot(high, keys) + dot(rest, keys)
        key_part = t_dot(high, queries) + t_dot(rest, queries)
        if i == 0:
            m.v_all[window(0), :] = value_part
            m.k_all[window(0), :] = key_part
        else:
            old, new = pl.ds(i * B, span - B), pl.ds(span + (i - 1) * B, B)
            m.v_all[old, :] += value_part[: span - B]
            m.v_all[new, :] = value_part[span - B :]
            m.k_all[old, :] += key_part[: span - B]
            m.k_all[new, :] = key_part[span - B :]
        m.k_send[rows(i), :] = m.k_all[rows(i), :].astype(BF16)
        m.v_send[rows(i), :] = m.v_all[rows(i), :].astype(BF16)
        for copy in grads_run(i):
            copy.start()

    def product(dst, left, right):
        for k in range(right.shape[1] // B):
            at = slice(k * B, (k + 1) * B)
            dst[:, at] = t_dot(left[...], right[:, at]).astype(BF16)

    def key_end(i):
        need(load.v_pre)
        for copy in grads_run(i):
            copy.wait()
        m.k_grad[rows(i), :] = m.k_all[mine(i), :] + m.k_got[rows(i), :].astype(F32)
        value = m.v_pre[rows(i), :].astype(F32)
        grad = m.v_all[mine(i), :] + m.v_got[rows(i), :].astype(F32)
        m.value_grad[rows(i), :] = (grad * d_silu(value, sigmoid(value))).astype(BF16)

    block_stage(0)
    block_stage(1)
    run_p[0].forward()
    block_stage(2)
    run_p[1].forward()
    block_stage(3)
    run_p[2].forward()
    up_stage(0)
    ffn_stage(0)
    run_p[3].forward()
    up_stage(1)
    ffn_stage(1)
    run_g[0].forward()
    up_stage(2)
    ffn_stage(2)
    up_stage(3)
    run_g[1].forward()
    grad_stage(0)
    ffn_stage(3)
    run_g[2].forward()
    grad_stage(1)
    run_gh[0].forward()
    if turn:
        product(m.w_down, m.cot4, m.up_rows)
    else:
        product(m.w_down, m.up_rows, m.cot4)
    line.start(1)
    run_g[3].forward()
    grad_stage(2)
    run_gh[1].forward()
    product(m.w_up, m.ffn4, m.up_grads)
    line.start(0)
    line.send_on(1)
    grad_stage(3)
    run_gh[2].forward()
    gate_stage(0)
    line.send_on(0)
    run_gh[3].forward()
    run_f[0].start()
    run_f[1].start()
    gate_stage(1)
    attend_back(0)
    gate_stage(2)
    run_f[0].forward()
    run_f[2].start()
    line.relay(1)
    gate_stage(3)
    store.hid4.start()
    store.upd_grad.start()
    store.gate_grad.start()
    store.tok_grad.start()
    store.part_t.start()
    store.mix_grad.start()
    run_f[1].forward()
    run_f[3].start()
    attend_back(1)
    run_f[2].forward()
    attend_back(2)
    run_f[3].forward()
    line.relay(0)
    attend_back(3)
    key_end(0)
    key_end(1)
    key_end(2)
    key_end(3)
    store.value_grad.start()
    for i in range(nb):
        m.out[rows(i), :] = (m.block[rows(i), :] + joined(run_f[i])).astype(BF16)
        run_f[i].finish()
    store.out.start()
    line.end(1)
    line.end(0)
    for copy in stores.values():
        copy.wait()


def middle(ident, line_count, ins):
    tok, f_gain = ins["tok"], ins["f_gain"]
    count, width = tok.shape
    full = 4 * width
    values, hidden = ins["w_gate"].shape[1], ins["w_up"].shape[1]
    nb = count // 256
    (_, turn), kinds, sizes, _, blocks = line_plan([(full, hidden), (hidden, full)], KINDS[-2:], line_count)
    dma, s, v = pltpu.SemaphoreType.DMA, jax.ShapeDtypeStruct, pltpu.VMEM
    outs = dict(
        out=s((count, width), BF16),
        part_t=s((4, count, width), BF16),
        tok_grad=s((count, width), F32),
        mix_grad=s((count, width), F32),
        value_grad=s((count, values), BF16),
        hid4=s((count, full), BF16),
        upd_grad=s((count, width), BF16),
        gate_grad=s((count, values), BF16),
        f_gain_grad=s((1, width), F32),
        q_grad=s((count, Z), F32),
        k_grad=s((count, Z), F32),
        d_up=s(blocks[0], F32),
        d_down=s(blocks[1], F32),
    )
    scratch = dict(
        block=v((count, width), F32),
        part_f=v((4, count, width), BF16),
        up_rows=v((count, hidden), BF16),
        up_grads=v((count, hidden), BF16),
        ffn4=v((count, full), BF16),
        att_grad=v((count, values), BF16),
        k_all=v((2 * count, Z), F32),
        v_all=v((2 * count, values), F32),
        part_g=v((4, count, width), BF16),
        got_g=v((3, 2 * nb, 128, width), BF16),
        low=v((count, width), BF16),
        rows_a=v((4, 8, count), F32),
        rows_b=v((4, 8, count), F32),
        k_send=v((count, Z), BF16),
        v_send=v((count, values), BF16),
        k_got=v((count, Z), BF16),
        v_got=v((count, values), BF16),
        p_up=v((line_count,) + blocks[0], BF16),
        p_down=v((line_count,) + blocks[1], BF16),
        l_up=v((line_count + 1,) + blocks[0], BF16),
        l_down=v((line_count + 1,) + blocks[1], BF16),
        c_send=dma((2, line_count)), c_recv=dma((2, line_count)),
        l_send=dma((2, line_count)), l_recv=dma((2, line_count + 1)),
        send=dma((24 * nb,)), recv=dma((24 * nb,)),
        s_rows=dma((6 * nb,)), r_rows=dma((6 * nb,)),
        s_gr=dma((2 * nb,)), r_gr=dma((2 * nb,)),
        s_in=dma((len(MID_LOAD),)), s_out=dma((len(MID_STORE),)),
    )
    got_all = pl.pallas_call(
        functools.partial(mid_kernel, kinds, sizes, turn, line_count),
        out_shape=[outs[n] for n in MID_OUT],
        in_specs=[ANY if n in MID_LOAD else VMEM for n in MID_IN],
        out_specs=[ANY if n in MID_STORE else VMEM for n in MID_OUT],
        scratch_shapes=[scratch[n] for n in MID_SCRATCH]
        + [v(ins[n].shape, ins[n].dtype) for n in MID_LOAD]
        + [v(outs[n].shape, outs[n].dtype) for n in MID_STORE],
        compiler_params=pltpu.CompilerParams(collective_id=ident, has_side_effects=True, vmem_limit_bytes=62 * 2**20),
        name="middle",
    )(*[ins[n] for n in MID_IN])
    got_all = Named(MID_OUT, got_all)
    if turn:
        got_all.d_down = got_all.d_down.T
    return got_all


REAR_LOAD = named(
    lambda part_t, value_grad, w_value, gated, hid4, mixed4, upd_grad, gate_grad, normed4, mix_grad,
    mix_pre, xn, tok_grad: None
)
REAR_IN = REAR_LOAD + named(
    lambda q_grad, k_grad, s_pre, w_shared, tok, inv_rows, keep_next, gain, damp, eta, q_gain,
    k_gain, f_gain_grad: None
)
REAR_WEIGHTS = WEIGHTS[:-2]
REAR_OUT = named(lambda grad_in, small: None) + ["d_" + w for w in REAR_WEIGHTS]
REAR_SCRATCH = named(
    lambda part_v, got_v, got_t, part_s, got_s, low_s, full_s, grad_mix, back, rows, ends, starts,
    end_out, end_in, small_core, small_all, own_q, all_q, upd_cols, send, recv, s_rows, r_rows,
    s_core, r_core, s_upd, r_upd, s_small, r_small, s_q, r_q, s_in, c_send, c_recv, l_send, l_recv:
    None
)


def rear_kernel(kinds, sizes, turns, line_count, *refs):
    groups_of = [p + w for p in ("p_", "l_", "g_") for w in REAR_WEIGHTS]
    m = Named(REAR_IN + REAR_OUT + REAR_SCRATCH + groups_of + ["i_" + n for n in REAR_LOAD], refs)
    loads = {}
    for k, n in enumerate(REAR_LOAD):
        loads[n] = Transfer(pltpu.make_async_copy(getattr(m, n), getattr(m, "i_" + n), m.s_in.at[k]))
        setattr(m, n, getattr(m, "i_" + n))
        loads[n].start()
    load = types.SimpleNamespace(**loads)
    t, x, y, d = tp_peers()
    z, c = lax.axis_index("fsdp"), lax.axis_index("ctx")
    other = spot(c=1 - c)
    groups, count = m.xn.shape[0], m.xn.shape[1]
    step, nj, width = count // 8, m.damp.shape[0], m.damp.shape[1]
    B = 256
    half, nb = B // 2, count // B
    part = min(16, nj)
    zero = jnp.zeros((8, 128), F32)

    def lanes(o):
        return pl.ds(pl.multiple_of(o * width, width), width)

    line = LineSum(
        kinds, sizes, line_count,
        [getattr(m, "g_" + w) for w in REAR_WEIGHTS], [getattr(m, "p_" + w) for w in REAR_WEIGHTS],
        [getattr(m, "l_" + w) for w in REAR_WEIGHTS], [getattr(m, "d_" + w) for w in REAR_WEIGHTS],
        (m.c_send, m.c_recv, m.l_send, m.l_recv),
    )
    m.end_in[...] = jnp.zeros_like(m.end_in)
    greet([spot(t=x), spot(t=y), spot(t=d), other] + line_peers(line_count))

    run_s = Scatter(
        2,
        lambda o, n: m.part_s.at[pl.ds(pl.multiple_of(o * B + n * half, half), half)],
        lambda n: m.got_s.at[0, n], lambda n: m.got_s.at[1, n], lambda n: m.got_s.at[2, n],
        m.send, m.recv, 0,
    )
    run_full = Gather(
        2,
        lambda n: m.low_s.at[pl.ds(n * half, half)],
        lambda o, n: m.full_s.at[pl.ds(pl.multiple_of(o * B + n * half, half), half)],
        m.send, m.recv, 6,
    )

    def scatter_runs(kind, parts, got):
        return [
            Scatter(
                2,
                lambda o, n, i=i: parts.at[o, pl.ds(i * B + n * half, half)],
                lambda n, i=i: got.at[0, i * 2 + n],
                lambda n, i=i: got.at[1, i * 2 + n],
                lambda n, i=i: got.at[2, i * 2 + n],
                m.send, m.recv, 12 + 6 * (kind * nb + i),
            )
            for i in range(nb)
        ]

    run_t, run_v = (
        scatter_runs(k, parts, got)
        for k, (parts, got) in enumerate(((m.part_t, m.got_t), (m.part_v, m.got_v)))
    )

    m.part_s[...] = (m.q_grad[...] * m.q_gain[...] + m.k_grad[...] * m.k_gain[...]).astype(BF16)
    run_s.start()
    shared = m.s_pre[...] * sigmoid(m.s_pre[...])
    m.own_q[...] = jnp.zeros_like(m.own_q)
    m.own_q[0:1, 0:Z] = jnp.sum(shared * m.q_grad[...], axis=0, keepdims=True)
    m.own_q[0:1, Z:] = jnp.sum(shared * m.k_grad[...], axis=0, keepdims=True)
    m.all_q[t] = m.own_q[...]
    gains = [
        remote(m.own_q, m.all_q.at[t], m.s_q.at[k], m.r_q.at[k], spot(t=p)) for k, p in enumerate((x, y, d))
    ]
    for copy in gains:
        copy.start()
    need(load.part_t)
    run_t[0].start()
    run_t[1].start()
    def value_part(i):
        rows = slice(i * B, (i + 1) * B)
        low = dot_t(m.value_grad[rows, :], m.w_value[...]).astype(BF16)
        for o in range(4):
            m.part_v[o, rows, :] = low[:, o * width : (o + 1) * width]

    def product(w, left, right):
        dst = getattr(m, "g_" + w)
        if turns[REAR_WEIGHTS.index(w)]:
            left, right = right, left
        size = min(256, right.shape[1])
        for k in range(right.shape[1] // size):
            at = slice(k * size, (k + 1) * size)
            dst[:, at] = t_dot(left, right[:, at]).astype(BF16)

    at_w = {w: k for k, w in enumerate(REAR_WEIGHTS)}

    need(load.value_grad, load.w_value)

    def value_part(i):
        rows = slice(i * B, (i + 1) * B)
        low = dot_t(m.value_grad[rows, :], m.w_value[...]).astype(BF16)
        for o in range(4):
            m.part_v[o, rows, :] = low[:, o * width : (o + 1) * width]

    need(load.gated, load.hid4)
    product("attended", m.gated[...], m.hid4[...])
    line.start(at_w["attended"])
    run_s.forward()
    run_t[0].forward()
    run_t[2].start()
    run_t[1].forward()
    run_t[3].start()
    need(load.mixed4, load.upd_grad)
    product("hidden", m.mixed4[:, lanes(t)], m.hid4[...])
    line.start(at_w["hidden"])
    quarter = pl.ds(pl.multiple_of(t * B, B), B)
    for n in range(2):
        total = run_s.collect(n) + run_s.part(t, n)[...].astype(F32)
        pre = m.s_pre[pl.ds(pl.multiple_of(t * B + n * half, half), half), :]
        m.low_s[n * half : (n + 1) * half, :] = (total * d_silu(pre, sigmoid(pre))).astype(BF16)
    run_full.start()
    m.full_s[quarter, :] = m.low_s[...]
    run_t[2].forward()
    line.send_on(at_w["attended"])
    turn_update = turns[at_w["update"]]
    if turn_update:
        m.upd_cols[...] = t_dot(m.upd_grad[...], m.mixed4[...]).astype(BF16)
    else:
        m.upd_cols[...] = t_dot(m.mixed4[...], m.upd_grad[...]).astype(BF16)

    def ends_of(p):
        if turn_update:
            return m.upd_cols.at[:, lanes(p)], m.g_update.at[lanes(t)]
        return m.upd_cols.at[lanes(p)], m.g_update.at[:, lanes(t)]

    turn_copies = [
        remote(*ends_of(p), m.s_upd.at[k], m.r_upd.at[k], spot(t=p)) for k, p in enumerate((x, y, d))
    ] + [pltpu.make_async_copy(*ends_of(t), m.s_upd.at[3])]
    for copy in turn_copies:
        copy.start()
    run_t[3].forward()
    run_full.forward()
    need(load.value_grad, load.w_value)
    value_part(0)
    run_v[0].start()
    value_part(1)
    run_v[1].start()
    line.send_on(at_w["hidden"])
    need(load.gate_grad, load.normed4)
    product("gate", m.mixed4[...], m.gate_grad[...])
    line.start(at_w["gate"])
    value_part(2)
    value_part(3)
    run_s.finish()
    run_full.finish()
    product("shared", m.mixed4[...], m.full_s[...])
    line.start(at_w["shared"])
    run_v[0].forward()
    run_v[2].start()
    for copy in turn_copies:
        copy.wait()
    line.start(at_w["update"])
    product("value", m.normed4[...], m.value_grad[...])
    line.start(at_w["value"])
    line.send_on(at_w["gate"])
    run_v[1].forward()
    run_v[3].start()
    line.send_on(at_w["update"])
    need(load.mix_grad, load.mix_pre, load.xn, load.tok_grad)
    own_shared = m.w_shared[lanes(t), :]
    for i in range(nb):
        for n in range(2):
            at = pl.ds(i * B + n * half, half)
            mix = m.mix_grad[at, :] + run_t[i].collect(n) + run_t[i].part(t, n)[...].astype(F32)
            mix = mix + dot_t(m.full_s[at, :], own_shared)
            for g in range(groups):
                pre = m.mix_pre[g, at, :]
                m.grad_mix[g, at, :] = mix[:, g * 128 : (g + 1) * 128] * d_silu(pre, sigmoid(pre))
        run_t[i].finish()
    line.send_on(at_w["shared"])
    line.send_on(at_w["value"])

    def later(*steps):
        return list(steps)

    def relay(*names):
        def run():
            for name in names:
                line.relay(at_w[name])

        return run

    waiting = later(
        run_v[2].forward, run_v[3].forward, relay("attended"), relay("hidden"), relay("gate"),
        relay("update"), relay("shared"), relay("value"),
    )

    def go(count):
        for _ in range(min(count, len(waiting))):
            waiting.pop(0)()

    for g in range(groups):
        ln = pl.ds(g * 128, 128)
        for j0 in range(0, nj, part):
            decay = [wide(1.0 - m.damp[pl.ds(j, 1), ln]) for j in range(j0, j0 + part)]

            def scan(i, carry):
                a, w, chain = carry
                at, after = pl.ds(step - 1 - i, 8, stride=step), pl.ds(step - i, 8, stride=step)
                v, k = m.grad_mix[g, at, :], m.keep_next[after, :]
                held = [k * r for r in decay]
                w = tuple(k * p + r * q for p, r, q in zip(a, held, w))
                a = tuple(v + r * p for r, p in zip(held, a))
                return a, w, chain * k

            a, w, chain = lax.fori_loop(0, step, scan, ((zero,) * part, (zero,) * part, zero + 1.0), unroll=8)
            for n in range(part):
                less = power(decay[n], step - 1)
                m.ends[0, j0 + n, :, ln] = a[n]
                m.ends[1, j0 + n, :, ln] = w[n]
                m.ends[2, j0 + n, :, ln] = less * decay[n] * chain
                m.ends[3, j0 + n, :, ln] = float(step) * less * chain
            go(2)

    def merge(q, a, w):
        return (
            m.ends[0, :, q, :] + m.ends[2, :, q, :] * a,
            m.ends[1, :, q, :] + m.ends[2, :, q, :] * w + m.ends[3, :, q, :] * a,
        )

    a = w = jnp.zeros((nj, width), F32)
    for q in range(7, -1, -1):
        a, w = merge(q, a, w)
    m.end_out[0] = a
    m.end_out[1] = w
    across = remote(m.end_out, m.end_in, m.s_core.at[0], m.r_core.at[0], other)
    across.start()
    across.wait()
    a, w = jnp.where(c == 0, m.end_in[0], 0.0), jnp.where(c == 0, m.end_in[1], 0.0)
    for q in range(7, -1, -1):
        m.starts[0, :, q, :] = a
        m.starts[1, :, q, :] = w
        a, w = merge(q, a, w)

    for g in range(groups):
        ln = pl.ds(g * 128, 128)
        for j0 in range(0, nj, part):
            span = range(j0, j0 + part)
            decay = [wide(1.0 - m.damp[pl.ds(j, 1), ln]) for j in span]
            weight = [wide(m.damp[pl.ds(j, 1), ln] * m.eta[pl.ds(j, 1), ln]) for j in span]

            def scan(i, carry):
                a, w, sum_a, sum_w = carry
                at, after = pl.ds(step - 1 - i, 8, stride=step), pl.ds(step - i, 8, stride=step)
                v, k, u = m.grad_mix[g, at, :], m.keep_next[after, :], m.xn[g, at, :]
                held = [k * r for r in decay]
                w = tuple(k * p + r * q for p, r, q in zip(a, held, w))
                a = tuple(v + r * p for r, p in zip(held, a))
                sum_a = tuple(s + u * p for s, p in zip(sum_a, a))
                sum_w = tuple(s + u * p for s, p in zip(sum_w, w))
                base = v if j0 == 0 else m.back[g, at, :]
                m.back[g, at, :] = base + tree_sum([r * p for r, p in zip(weight, a)])
                return a, w, sum_a, sum_w

            first = (tuple(m.starts[0, j, :, ln] for j in span), tuple(m.starts[1, j, :, ln] for j in span))
            _, _, sum_a, sum_w = lax.fori_loop(
                0, step, scan, first + ((zero,) * part, (zero,) * part), unroll=8
            )
            for n, j in enumerate(span):
                at = pl.ds(j, 1)
                all_a = jnp.sum(sum_a[n], axis=0, keepdims=True)
                all_w = jnp.sum(sum_w[n], axis=0, keepdims=True)
                rate = m.damp[at, ln]
                m.small[at, ln] = m.eta[at, ln] * (all_a - rate * all_w)
                m.small[pl.ds(nj + j, 1), ln] = rate * all_a
            go(2)

    go(len(waiting))
    inv = m.inv_rows[...].T[:, 0:1]
    value = m.tok[...].astype(F32)
    for i in range(nb):
        for n in range(2):
            at = pl.ds(i * B + n * half, half)
            got = run_v[i].collect(n) + run_v[i].part(t, n)[...].astype(F32)
            m.grad_in[at, :] = got + jnp.concatenate([m.back[g, at, :] for g in range(groups)], axis=1)
        run_v[i].finish()
    grad_normed = m.grad_in[...]
    m.small[2 * nj :, :] = jnp.zeros((m.small.shape[0] - 2 * nj, width), F32)
    m.small[2 * nj : 2 * nj + 1, :] = jnp.sum(grad_normed * value * inv, axis=0, keepdims=True)
    m.small[2 * nj + 1 : 2 * nj + 2, :] = m.f_gain_grad[...]
    for copy in gains:
        copy.wait()
    m.small[2 * nj + 2 : 2 * nj + 3, :] = (
        m.all_q[0, 0:1] + m.all_q[1, 0:1] + m.all_q[2, 0:1] + m.all_q[3, 0:1]
    )
    scaled = grad_normed * m.gain[...]
    m.rows[t] = row_sums(scaled * value)
    sums = row_exchange(m.rows, m.s_rows, m.r_rows)
    pair = remote(m.small, m.small_core, m.s_small.at[0], m.r_small.at[0], other)
    for copy in sums + [pair]:
        copy.start()
    m.grad_in[...] = m.tok_grad[...] + inv * scaled
    pair.wait()
    m.small_all[z] = m.small[...] + m.small_core[...]
    wide_sums = [
        remote(
            m.small_all.at[z], m.small_all.at[z], m.s_small.at[k], m.r_small.at[k], spot(f=(z + k) % line_count)
        )
        for k in range(1, line_count)
    ]
    for copy in wide_sums:
        copy.start()
    for copy in sums:
        copy.wait()
    factor = m.inv_rows[...]
    factor = factor * factor * factor * (m.rows[0] + m.rows[1] + m.rows[2] + m.rows[3]) / D
    m.grad_in[...] -= value * factor.T[:, 0:1]
    for copy in wide_sums:
        copy.wait()
    total = m.small_all[0]
    for k in range(1, line_count):
        total = total + m.small_all[k]
    m.small[...] = total
    for w in ("attended", "hidden", "gate", "update", "shared", "value"):
        line.end(at_w[w])


def rear(ident, line_count, ins):
    count, width = ins["tok"].shape
    groups, nj = width // 128, ins["damp"].shape[0]
    full = 4 * width
    nb = count // 256
    values = ins["value_grad"].shape[1]
    shapes = [(full, Z), (full, values), (full, values), (width, full), (values, full), (width, full)]
    turns, kinds, sizes, shapes, blocks = line_plan(shapes, KINDS[:-2], line_count)
    dma, s, v, k = pltpu.SemaphoreType.DMA, jax.ShapeDtypeStruct, pltpu.VMEM, len(REAR_WEIGHTS)
    tall = 2 * nj + 8
    n = 12 + 12 * nb
    lanes = v((groups, count, 128), F32)
    got = v((3, 2 * nb, 128, width), BF16)
    scratch = dict(
        part_v=v((4, count, width), BF16),
        got_v=got, got_t=got,
        part_s=v((count, Z), BF16),
        got_s=v((3, 2, 128, Z), BF16),
        low_s=v((256, Z), BF16),
        full_s=v((count, Z), BF16),
        grad_mix=lanes, back=lanes,
        rows=v((4, 8, count), F32),
        ends=v((4, nj, 8, width), F32),
        starts=v((2, nj, 8, width), F32),
        end_out=v((2, nj, width), F32),
        end_in=v((2, nj, width), F32),
        small_core=v((tall, width), F32),
        small_all=v((line_count, tall, width), F32),
        own_q=v((8, width), F32),
        all_q=v((4, 8, width), F32),
        upd_cols=v((width, full) if turns[REAR_WEIGHTS.index("update")] else (full, width), BF16),
        send=dma((n,)), recv=dma((n,)), s_rows=dma((3,)), r_rows=dma((3,)), s_core=dma((1,)), r_core=dma((1,)),
        s_upd=dma((4,)), r_upd=dma((3,)), s_small=dma((line_count,)), r_small=dma((line_count,)),
        s_q=dma((3,)), r_q=dma((3,)), s_in=dma((len(REAR_LOAD),)),
        c_send=dma((k, line_count)), c_recv=dma((k, line_count)),
        l_send=dma((k, line_count)), l_recv=dma((k, line_count + 1)),
    )
    got = pl.pallas_call(
        functools.partial(rear_kernel, kinds, sizes, turns, line_count),
        out_shape=[s((count, width), F32), s((tall, width), F32)] + [s(b, F32) for b in blocks],
        in_specs=[ANY if name in REAR_LOAD else VMEM for name in REAR_IN],
        out_specs=[VMEM] * len(REAR_OUT),
        scratch_shapes=[scratch[name] for name in REAR_SCRATCH]
        + [v((line_count,) + b, BF16) for b in blocks]
        + [v((line_count + 1,) + b, BF16) for b in blocks]
        + [v(shape, BF16) for shape in shapes]
        + [v(ins[name].shape, ins[name].dtype) for name in REAR_LOAD],
        compiler_params=pltpu.CompilerParams(collective_id=ident, has_side_effects=True, vmem_limit_bytes=62 * 2**20),
        name="rear",
    )(*[ins[name] for name in REAR_IN])
    grads = [g.T if turn else g for turn, g in zip(turns, got[2:])]
    return got[0], got[1], grads


def finish_kernel(count, nj, *refs):
    small, sources, (norm, damp, eta, query, key, ffn) = refs[0], refs[1 : 1 + count], refs[1 + count : 7 + count]
    places, held, sem = refs[7 + count : 7 + 2 * count], refs[7 + 2 * count : -1], refs[-1]
    copies = [pltpu.make_async_copy(src, dst, sem.at[0, k]) for k, (src, dst) in enumerate(zip(sources, held))]
    for copy in copies:
        copy.start()
    damp[...] = small[0:nj, :]
    eta[...] = small[nj : 2 * nj, :]
    norm[...] = small[2 * nj : 2 * nj + 1, :]
    ffn[...] = small[2 * nj + 1 : 2 * nj + 2, :]
    query[...] = small[2 * nj + 2 : 2 * nj + 3, 0:Z]
    key[...] = small[2 * nj + 2 : 2 * nj + 3, Z : 2 * Z]
    outs = [pltpu.make_async_copy(src, dst, sem.at[1, k]) for k, (src, dst) in enumerate(zip(held, places))]
    for copy, out in zip(copies, outs):
        copy.wait()
        out.start()
    for out in outs:
        out.wait()


def finish(small, nj, arrays):
    s, width, k = jax.ShapeDtypeStruct, small.shape[1], len(arrays)
    row, table, unit = s((1, width), F32), s((nj, width), F32), s((1, Z), F32)
    got = pl.pallas_call(
        functools.partial(finish_kernel, k, nj),
        out_shape=[row, table, table, unit, unit, row] + [s(a.shape, a.dtype) for a in arrays],
        in_specs=[VMEM] + [ANY] * k,
        out_specs=[VMEM] * 6 + [ANY] * k,
        scratch_shapes=[pltpu.VMEM(a.shape, a.dtype) for a in arrays] + [pltpu.SemaphoreType.DMA((2, k))],
        compiler_params=pltpu.CompilerParams(vmem_limit_bytes=60 * 2**20),
        name="finish",
    )(small, *arrays)
    return got[:6], got[6:]


def on_device(
    line_count,
    layer_input, segment_ids, cotangent, norm_gain, ema_damping, ema_eta, query_gain, key_gain,
    ffn_gain, *weights,
):
    tok, cot = layer_input[0], cotangent[0]
    segment = segment_ids[0]
    row_count = tok.shape[0]
    core = lax.axis_index("ctx")
    offset = core * row_count
    all_ids = lax.all_gather(segment, "ctx", axis=0, tiled=True)
    same = jnp.concatenate(
        [jnp.zeros((1,), F32), (all_ids[1:] == all_ids[:-1]).astype(F32), jnp.zeros((8,), F32)]
    )
    keep_wide = jnp.broadcast_to(lax.dynamic_slice_in_dim(same, offset, row_count + 8, 0)[:, None], (row_count + 8, 128))
    prev_ids = jnp.where(core > 0, all_ids[:row_count], -1)
    ids_row = jnp.broadcast_to(jnp.concatenate([prev_ids, segment]).astype(F32)[None], (8, 2 * row_count))
    a = front(
        1, line_count, tok, keep_wide, norm_gain, ema_damping, ema_eta, query_gain, key_gain, ids_row, cot, weights
    )
    ins = {n: getattr(a, n) for n in MID_LOAD if n != "w_upd"}
    ins.update(w_upd=a.rows_update, tok=tok, cot=cot, f_gain=ffn_gain[None], ids_row=ids_row)
    m = middle(2, line_count, ins)
    ins = {n: getattr(m if n in MID_OUT else a, n) for n in REAR_IN if n in MID_OUT or n in A_OUT}
    ins.update(
        tok=tok, keep_next=keep_wide, gain=norm_gain[None], damp=ema_damping, eta=ema_eta,
        q_gain=query_gain[None], k_gain=key_gain[None],
    )
    grad_in, small, grads = rear(3, line_count, ins)
    (norm, damp, eta, query, key, ffn), (out, grad_in, *grads) = finish(
        small, ema_damping.shape[0], [m.out, grad_in, *grads, m.d_up, m.d_down]
    )
    return (out[None], grad_in[None], norm[0], damp, eta, query[0], key[0], ffn[0], *grads)


def solution(mesh):
    token = P("fsdp", "ctx", "tp")
    row, col = P(("fsdp", "ctx"), "tp"), P("tp", ("fsdp", "ctx"))
    shared = P(("fsdp", "ctx"), None)
    weights = (shared, row, row, col, col, col, row, col)
    small = P(None, "tp")
    return jax.shard_map(
        functools.partial(on_device, mesh.shape["fsdp"]),
        mesh=mesh,
        in_specs=(token, P("fsdp", "ctx"), token, P("tp"), small, small, P(), P(), P("tp")) + weights,
        out_specs=(token, token, P("tp"), small, small, P(), P(), P("tp")) + weights,
        check_vma=False,
    )
```
